32 devices in a mesh: dp: 8 (over z, y), tensor: 4 (over x, core).
Axes of the slice: x: 2, y: 2, z: 4, core: 2. Of those that a mesh axis runs over, the one named last changes fastest.
Arguments:
- tokens: bfloat16 [2048, 2048], P('dp'), may hold values from -24 to 24
- segment_ids: int32 [2048], P('dp'), may hold values from 1 to 3, as said below
- routes: int32 [2048, 8], P('dp'), may hold values from 0 to 15, all different within a row; in each aligned block of 256 rows (0 to 255, 256 to 511, ...) at most 256 rows name the same one
- norm1_gain: float32 [2048], replicated, may hold values from 0.5 to 1.5
- w_query: bfloat16 [2048, 2048], P(None, 'tensor'), may hold values from -0.125 to 0.125
- w_key: bfloat16 [2048, 2048], P(None, 'tensor'), may hold values from -0.125 to 0.125
- w_value: bfloat16 [2048, 2048], P(None, 'tensor'), may hold values from -0.125 to 0.125
- query_gain: float32 [16, 128], P('tensor'), may hold values from 0.5 to 1.5
- key_gain: float32 [16, 128], P('tensor'), may hold values from 0.5 to 1.5
- w_out: bfloat16 [2048, 2048], P('tensor'), may hold values from -4 to 4
- norm2_gain: float32 [2048], replicated, may hold values from 0.5 to 1.5
- w_router: bfloat16 [2048, 16], replicated, may hold values from -0.0625 to 0.0625
- w_gate: bfloat16 [16, 2048, 1024], P('dp', None, 'tensor'), may hold values from -0.125 to 0.125
- w_up: bfloat16 [16, 2048, 1024], P('dp', None, 'tensor'), may hold values from -0.125 to 0.125
- w_down: bfloat16 [16, 1024, 2048], P('dp', 'tensor'), may hold values from -7.1875 to 7.1875
- cotangent: bfloat16 [2048, 2048], P('dp'), may hold values from -6 to 6
Outputs:
- block_output: bfloat16 [2048, 2048], P('dp')
- input_grad: float32 [2048, 2048], P('dp')
- d_norm1_gain: float32 [2048], P('dp')
- d_w_query: float32 [2048, 2048], P('dp', 'tensor')
- d_w_key: float32 [2048, 2048], P('dp', 'tensor')
- d_w_value: float32 [2048, 2048], P('dp', 'tensor')
- d_query_gain: float32 [16, 128], P('tensor', 'dp')
- d_key_gain: float32 [16, 128], P('tensor', 'dp')
- d_w_out: float32 [2048, 2048], P('tensor', 'dp')
- d_norm2_gain: float32 [2048], P('dp')
- d_w_router: float32 [2048, 16], P('dp')
- d_w_gate: float32 [16, 2048, 1024], P('dp', None, 'tensor')
- d_w_up: float32 [16, 2048, 1024], P('dp', None, 'tensor')
- d_w_down: float32 [16, 1024, 2048], P('dp', 'tensor')
The draws below stay inside these ranges and needn't reach their ends.
Inputs may be any that keep to these rules, and one draw needn't show every extreme that they name: `routes`: in each aligned block of 256 tokens every token names 8 different experts and no expert is named by more than 256 tokens of the block; some expert is named by exactly 256 tokens of some block in every draw. `segment_ids`: ids never fall along the tokens. The one packed sequence of 2048 tokens holds three documents with ids of their own, and one of them has exactly 1920 tokens.
All inputs are finite; a program needn't handle non-finite values.
Results may differ from the reference program's by a relative error of at most 0.025.
Values may be sent and summed in bfloat16 or wider, within the bound.
No kernel may reach another device: no remote copies, remote signals or barrier semaphores. Data moves between devices by JAX's collectives and lax.ppermute only.
A program may use at most 384 MiB of HBM per device.

```python
import functools
import math
import jax
import jax.numpy as jnp
import numpy as np
from jax import lax

D = 2048
HEADS = 16
HEAD = 128
FF = 1024
TOPK = 8
TOK_DEV = 256
EXPERTS = 16
TOKENS = 2048
SEQ = 2048
SEQS = 1
CAP = 256
N_DP = 8
N_TENSOR = 4


def draw_segment_ids(key, part):
    key = jax.random.fold_in(key, 11)
    starts = jax.random.randint(key, (SEQS, 1), 1, TOK_DEV // 2)
    places = jnp.arange(SEQ, dtype=jnp.int32)[None, :]
    long_end = starts + SEQ - TOK_DEV // 2
    local_doc = (places >= starts).astype(jnp.int32) + (places >= long_end).astype(jnp.int32)
    base_ids = 3 * jnp.arange(SEQS, dtype=jnp.int32)[:, None]
    return (base_ids + local_doc + 1).reshape(-1).astype(jnp.int32)


def draw_tokens(key, part):
    key = jax.random.fold_in(key, 7)
    key_base, key_rows, key_cols = jax.random.split(key, 3)
    row_scale = jnp.exp(jax.random.uniform(key_rows, (TOKENS, 1), jnp.float32, jnp.log(0.5), jnp.log(5.0)))
    col_scale = jnp.exp(jax.random.uniform(key_cols, (1, D), jnp.float32, jnp.log(0.5), jnp.log(2.0)))
    values = jax.random.normal(key_base, (TOKENS, D), jnp.float32) * row_scale * col_scale
    return jnp.clip(values, -24.0, 24.0).astype(jnp.bfloat16)


def level_of(stream_key, dims, cuts, smallest, largest):
    def one(position, blocks):
        steps = jax.random.uniform(jax.random.fold_in(jax.random.fold_in(stream_key, 6), position), (blocks,), jnp.float32, smallest / len(cuts), largest / len(cuts))
        return jnp.repeat(jnp.exp(steps), dims[position] // blocks).reshape((-1,) + (1,) * (len(dims) - position - 1))

    factor_of = one(*cuts[0])
    for cut in cuts[1:]:
        factor_of = factor_of * one(*cut)
    return factor_of


def deal_out(stream_key, own, number, rows, amount, top, most, lean):
    order = jax.random.permutation(stream_key, amount)
    packed, usual = load_shares(amount, rows * top, most, lean, True), load_shares(amount, rows * top, most, lean, False)
    places = jnp.arange(amount)

    def named(sizes, offset_by):
        used = int((sizes > 0).sum())
        fixed = max(1, used // 4)
        moved = fixed + (places - fixed + offset_by * (used - fixed)) % max(1, amount - fixed)
        return jnp.zeros((amount,), jnp.int32).at[order[jnp.where(places < fixed, places, moved)]].set(jnp.asarray(sizes, jnp.int32))

    sizes = jnp.where(number % 4 == 0, named(packed, number // 4), named(usual, number - number // 4 - 1))
    mixed = jax.random.permutation(jax.random.fold_in(own, 3), amount)
    giver, sink = mixed[0:amount // 2 * 2:2], mixed[1:amount // 2 * 2:2]
    slack = jnp.minimum(sizes[giver] - 1, most - sizes[sink]) // 2
    slack = jnp.where((giver == order[0]) | (sink == order[0]) | (sizes[sink] == 0), 0, jnp.maximum(slack, 0))
    moved = jax.random.randint(jax.random.fold_in(own, 4), (amount // 2,), 0, 1 << 20) % (slack + 1)
    sizes = sizes.at[giver].add(-moved).at[sink].add(moved)
    items = jnp.searchsorted(jnp.cumsum(sizes), jnp.arange(rows * top), side="right").astype(jnp.int32)
    grid = items.reshape(top, rows).T
    grid = grid[jax.random.permutation(jax.random.fold_in(own, 1), rows)]
    offset_by = jax.random.randint(jax.random.fold_in(own, 2), (rows, 1), 0, top)
    return jnp.take_along_axis(grid, (jnp.arange(top)[None, :] + offset_by) % top, axis=1)


def load_shares(amount, total, limit, lean, full):
    loads = [(1 << 20) // math.isqrt(standing ** lean) + 1 for standing in range(1, amount + 1)]
    largest = limit if full else min(limit, max(-(-total // amount), total * loads[0] // sum(loads)))
    least = 1 if total - largest >= amount - 1 else 0
    given, rest = [largest] + [least] * (amount - 1), total - largest - least * (amount - 1)
    while rest > 0:
        free = [i for i in range(1, amount) if given[i] < largest] or [i for i in range(1, amount) if given[i] < limit]
        pool, remaining = sum([loads[i] for i in free]), rest
        for i in free:
            extra = min(limit - given[i], max(1, remaining * loads[i] // pool), rest)
            given[i] = given[i] + extra
            rest = rest - extra
    return np.array(given)


def centred(key, shape, width, most, cuts=(), kind=jnp.bfloat16):
    array = width * jax.random.normal(key, shape, jnp.float32)
    if cuts:
        array = array * level_of(key, shape, cuts, -0.22, 0.18)
    return jnp.clip(array, -most, most).astype(kind)


def setup_inputs(seed: int = 0) -> dict:
    arg_keys = jax.random.split(jax.random.key(seed), 17)
    tokens = draw_tokens(jax.random.fold_in(arg_keys[16], 71), 0)
    segment_ids = draw_segment_ids(jax.random.fold_in(arg_keys[16], 71), 0)
    routes_keys = jax.random.split(jax.random.fold_in(arg_keys[2], 1), TOKENS // TOK_DEV)
    routes_turns = jax.random.permutation(jax.random.fold_in(arg_keys[2], 3), TOKENS // TOK_DEV)
    routes = jax.vmap(lambda own, number: deal_out(jax.random.fold_in(arg_keys[2], 2), own, number, TOK_DEV, EXPERTS, TOPK, CAP, 1))(routes_keys, routes_turns).reshape((TOKENS, TOPK))
    norm1_gain = jnp.clip(1.0 + 0.1 * jax.random.normal(arg_keys[3], (D,), jnp.float32), 0.5, 1.5)
    w_query = centred(arg_keys[4], (D, HEADS * HEAD), D ** -0.5, 0.125, ((1, 4),))
    w_key = centred(arg_keys[5], (D, HEADS * HEAD), D ** -0.5, 0.125, ((1, 4),))
    w_value = centred(arg_keys[6], (D, HEADS * HEAD), D ** -0.5, 0.125, ((1, 4),))
    query_gain = jnp.clip(1.0 + 0.1 * jax.random.normal(arg_keys[7], (HEADS, HEAD), jnp.float32), 0.5, 1.5)
    key_gain = jnp.clip(1.0 + 0.1 * jax.random.normal(arg_keys[8], (HEADS, HEAD), jnp.float32), 0.5, 1.5)
    w_out = centred(arg_keys[9], (HEADS * HEAD, D), (max(HEADS * HEAD * 2 // SEQ, 1)) ** -0.5, 4.0, ((0, 4),))
    norm2_gain = jnp.clip(1.0 + 0.1 * jax.random.normal(arg_keys[10], (D,), jnp.float32), 0.5, 1.5)
    w_router = centred(arg_keys[11], (D, EXPERTS), (4 * D) ** -0.5, 0.0625)
    w_gate = centred(arg_keys[12], (EXPERTS, D, FF), D ** -0.5, 0.125, ((0, 8), (2, 4)))
    w_up = centred(arg_keys[13], (EXPERTS, D, FF), D ** -0.5, 0.125, ((0, 8), (2, 4)))
    w_down = centred(arg_keys[14], (EXPERTS, FF, D), 1.2, 7.1875, ((0, 8), (1, 4)))
    cotangent = centred(arg_keys[15], (TOKENS, D), 1.0, 6.0, ((0, 8),))
    return {"tokens": tokens, "segment_ids": segment_ids, "routes": routes, "norm1_gain": norm1_gain, "w_query": w_query, "w_key": w_key, "w_value": w_value, "query_gain": query_gain, "key_gain": key_gain, "w_out": w_out, "norm2_gain": norm2_gain, "w_router": w_router, "w_gate": w_gate, "w_up": w_up, "w_down": w_down, "cotangent": cotangent}


EPSILON = 1e-05
ROPE_BASE = 10000.0
NEGATIVE = -1e+30
HIGHEST_PREC = lax.Precision.HIGHEST

@jax.custom_vjp
def low(v):
    return lax.optimization_barrier(v.astype(jnp.bfloat16)).astype(jnp.float32)

@jax.custom_vjp
def low_back(v):
    return v

def low_keep(v):
    return (low(v), None)

def low_pass(kept, grad):
    return (grad,)

def back_keep(v):
    return (v, None)

def back_low(kept, grad):
    return (low(grad),)
low.defvjp(low_keep, low_pass)
low_back.defvjp(back_keep, back_low)

def matmul(left_side, right_side):
    return jnp.dot(left_side, right_side, precision=HIGHEST_PREC, preferred_element_type=jnp.float32)

def rms_norm(vector, gain):
    return vector * lax.rsqrt(lax.optimization_barrier(jnp.mean(vector * vector, -1, keepdims=True)) + EPSILON) * gain

def rope_tables(positions, head_size):
    frequency = ROPE_BASE ** (-jnp.arange(0, head_size, 2, dtype=jnp.float32) / head_size)
    angles = positions[:, None] * frequency[None, :]
    cos_table = jnp.concatenate([jnp.cos(angles), jnp.cos(angles)], -1)[:, None, :]
    sin_table = jnp.concatenate([jnp.sin(angles), jnp.sin(angles)], -1)[:, None, :]
    return (cos_table, sin_table)

def rotate(vector, cos_table, sin_table):
    half_size = vector.shape[-1] // 2
    turned = jnp.concatenate([-vector[..., half_size:], vector[..., :half_size]], -1)
    return vector * cos_table + turned * sin_table

def place_rows(route_block, experts, capacity):
    tok_count, top_count = route_block.shape
    flat_ids = route_block.reshape(-1).astype(jnp.int32)
    onehot = (flat_ids[:, None] == jnp.arange(experts, dtype=jnp.int32)[None, :]).astype(jnp.int32)
    slot_rank = (lax.optimization_barrier(jnp.sum(jnp.cumsum(onehot, 0) * onehot, 1)) - 1).astype(jnp.int32)
    dest_slot = (flat_ids * capacity + slot_rank).astype(jnp.int32)
    owner_tok = (jnp.arange(tok_count * top_count, dtype=jnp.int32) // top_count).astype(jnp.int32)
    slot_token = jnp.full((experts * capacity,), tok_count, jnp.int32).at[dest_slot].set(owner_tok)
    return (dest_slot, slot_token)

def attend(pieces):
    query_seq, key_seq, value_seq, segment_seq = pieces
    raw_scores = low_back(jnp.einsum('qhd,khd->hqk', query_seq, key_seq, precision=HIGHEST_PREC) / math.sqrt(HEAD))
    order_pos = jnp.arange(SEQ, dtype=jnp.int32)
    visible = (segment_seq[:, None] == segment_seq[None, :]) & (order_pos[None, :] <= order_pos[:, None])
    masked = jnp.where(visible[None], raw_scores, NEGATIVE)
    row_top = lax.optimization_barrier(jnp.max(masked, -1, keepdims=True))
    log_total = row_top + jnp.log(lax.optimization_barrier(jnp.sum(jnp.exp(masked - row_top), -1, keepdims=True)))
    attn_probs = jnp.where(visible[None], jnp.exp(masked - log_total), 0.0)
    return jnp.einsum('hqk,khd->qhd', low(attn_probs), value_seq, precision=HIGHEST_PREC)

def make_experts(w_gate, w_up, w_down):

    def run_block(pieces):
        rows_block, route_block, gate_block = pieces
        dest_slot, slot_token = place_rows(route_block, EXPERTS, CAP)
        padded = jnp.concatenate([rows_block, jnp.zeros((1, D), jnp.float32)], 0)
        rows_in = padded[slot_token].reshape(EXPERTS, CAP, D)
        gate_pre = low_back(jnp.einsum('ecd,edf->ecf', rows_in, w_gate, precision=HIGHEST_PREC))
        up_pre = low_back(jnp.einsum('ecd,edf->ecf', rows_in, w_up, precision=HIGHEST_PREC))
        hidden = low(gate_pre * jax.nn.sigmoid(gate_pre) * up_pre)
        quarter = FF // N_TENSOR
        partials = jnp.einsum('ectf,etfd->etcd', hidden.reshape(EXPERTS, CAP, N_TENSOR, quarter), w_down.reshape(EXPERTS, N_TENSOR, quarter, D), precision=HIGHEST_PREC)
        merged = lax.optimization_barrier(jnp.sum(low(low_back(partials)), 1)).reshape(EXPERTS * CAP, D)
        picked = merged[dest_slot].reshape(TOK_DEV, TOPK, D)
        return lax.optimization_barrier(jnp.sum(gate_block[:, :, None] * picked, 1))
    return run_block

def forward(segment_ids, routes, tokens, norm1_gain, w_query, w_key, w_value, query_gain, key_gain, w_out, norm2_gain, w_router, w_gate, w_up, w_down):
    normed_in = low(rms_norm(tokens, norm1_gain))
    query_raw = low_back(matmul(normed_in, w_query))
    key_raw = low_back(matmul(normed_in, w_key))
    value_att = low(low_back(matmul(normed_in, w_value)))
    query_unit = rms_norm(query_raw, query_gain.reshape(-1))
    key_unit = rms_norm(key_raw, key_gain.reshape(-1))
    positions = (jnp.arange(TOKENS, dtype=jnp.int32) % SEQ).astype(jnp.float32)
    cos_table, sin_table = rope_tables(positions, HEAD)
    query_att = low(low_back(rotate(query_unit.reshape(TOKENS, HEADS, HEAD), cos_table, sin_table)))
    key_att = low(low_back(rotate(key_unit.reshape(TOKENS, HEADS, HEAD), cos_table, sin_table)))
    mixed_heads = lax.map(jax.checkpoint(attend), (query_att.reshape(SEQS, SEQ, HEADS, HEAD), key_att.reshape(SEQS, SEQ, HEADS, HEAD), value_att.reshape(SEQS, SEQ, HEADS, HEAD), segment_ids.reshape(SEQS, SEQ)))
    attn_mix = low(low_back(mixed_heads.reshape(TOKENS, HEADS * HEAD)))
    resid_state = tokens + low_back(matmul(attn_mix, w_out))
    normed_mid = low(rms_norm(resid_state, norm2_gain))
    router_probs = jax.nn.softmax(low_back(matmul(normed_mid, w_router)), -1)
    chosen = (routes[:, :, None] == jnp.arange(EXPERTS, dtype=jnp.int32)[None, None, :]).astype(jnp.float32)
    gate_values = lax.optimization_barrier(jnp.sum(chosen * router_probs[:, None, :], -1))
    expert_out = lax.map(jax.checkpoint(make_experts(w_gate, w_up, w_down)), (normed_mid.reshape(N_DP, TOK_DEV, D), routes.reshape(N_DP, TOK_DEV, TOPK), gate_values.reshape(N_DP, TOK_DEV, TOPK)))
    return resid_state + expert_out.reshape(TOKENS, D)

def reference(tokens, segment_ids, routes, norm1_gain, w_query, w_key, w_value, query_gain, key_gain, w_out, norm2_gain, w_router, w_gate, w_up, w_down, cotangent):
    floats = (tokens.astype(jnp.float32), norm1_gain.astype(jnp.float32), w_query.astype(jnp.float32), w_key.astype(jnp.float32), w_value.astype(jnp.float32), query_gain.astype(jnp.float32), key_gain.astype(jnp.float32), w_out.astype(jnp.float32), norm2_gain.astype(jnp.float32), w_router.astype(jnp.float32), w_gate.astype(jnp.float32), w_up.astype(jnp.float32), w_down.astype(jnp.float32))
    output, pullback = jax.vjp(functools.partial(forward, segment_ids, routes), *floats)
    gradients = pullback(cotangent.astype(jnp.float32))
    return (output.astype(jnp.bfloat16), gradients[0], gradients[1], gradients[2], gradients[3], gradients[4], gradients[5], gradients[6], gradients[7], gradients[8], gradients[9], gradients[10], gradients[11], gradients[12])
```

```python
import functools
import math

import jax
import jax.numpy as jnp
from jax import lax
from jax.experimental import pallas as pl
from jax.experimental.pallas import tpu as pltpu
from jax.sharding import PartitionSpec as P

SPAN = 8


EPSILON = 1e-05
ROPE_BASE = 10000.0
NEGATIVE = -1e30
BF = jnp.bfloat16
F32 = jnp.float32
EVERY = ("dp", "tensor")
VMEM_LIMIT = 56 * 1024 * 1024
LANES = 128


def rope_tables(positions, head_size):
    frequency = ROPE_BASE ** (-jnp.arange(0, head_size, 2, dtype=jnp.float32) / head_size)
    angles = positions[:, None] * frequency[None, :]
    cos_table = jnp.concatenate([jnp.cos(angles), jnp.cos(angles)], -1)[:, None, :]
    sin_table = jnp.concatenate([jnp.sin(angles), jnp.sin(angles)], -1)[:, None, :]
    return (cos_table, sin_table)


def rotate(vector, cos_table, sin_table):
    half_size = vector.shape[-1] // 2
    turned = jnp.concatenate([-vector[..., half_size:], vector[..., :half_size]], -1)
    return vector * cos_table + turned * sin_table


def unrotate(gradient, cos_table, sin_table):
    half_size = gradient.shape[-1] // 2
    scaled = gradient * sin_table
    turned = jnp.concatenate([scaled[..., half_size:], -scaled[..., :half_size]], -1)
    return gradient * cos_table + turned


def dot(left_side, right_side, left_dim, right_dim):
    return lax.dot_general(
        left_side,
        right_side,
        (((left_dim,), (right_dim,)), ((), ())),
        preferred_element_type=jnp.float32,
    )


def span_groups(owners):
    return [list(range(g, g + SPAN)) for g in range(0, owners, SPAN)]


def swap(array, axis, bit):
    count = lax.axis_size(axis)
    return lax.ppermute(array, axis, [(i, i ^ bit) for i in range(count)])


def pick(array, index):
    return lax.dynamic_index_in_dim(array, index, 0, keepdims=False)


def sum_tensor(partial, place):
    rows = partial.shape[0] // 4
    blocks = partial.reshape(2, 2, rows, partial.shape[1])
    core, side = place % 2, place // 2
    given = lax.dynamic_index_in_dim(blocks, 1 - core, 1, keepdims=False).astype(BF)
    kept = lax.dynamic_index_in_dim(blocks, core, 1, keepdims=False)
    kept = kept + swap(given, "tensor", 1).astype(F32)
    return pick(kept, side) + swap(pick(kept, 1 - side).astype(BF), "tensor", 2).astype(F32)


def spread_tensor(block, place):
    core, side = place % 2, place // 2
    other = swap(block, "tensor", 2)
    both = jnp.where(side == 0, jnp.stack([block, other]), jnp.stack([other, block]))
    across = swap(both, "tensor", 1)
    full = jnp.where(core == 0, jnp.stack([both, across], 1), jnp.stack([across, both], 1))
    return full.reshape((4 * block.shape[0],) + block.shape[1:])


def resident(shape):
    return pl.BlockSpec(shape, lambda *_: (0,) * len(shape), pipeline_mode=pl.Buffered(1))


def cost(macs, size, transcendentals=0):
    return pl.CostEstimate(flops=2 * macs, bytes_accessed=size, transcendentals=transcendentals)


PARAMS = pltpu.CompilerParams(vmem_limit_bytes=VMEM_LIMIT)


def turn_kernel(gate_ref, up_ref, down_ref, both_ref, down_out_ref):
    count, _, hidden = gate_ref.shape
    for e in range(count):
        both_ref[pl.ds(e * hidden, hidden), :] = gate_ref[e].T
        both_ref[pl.ds((count + e) * hidden, hidden), :] = up_ref[e].T
        down_out_ref[:, pl.ds(e * hidden, hidden)] = down_ref[e].T


def turn_weights(w_gate, w_up, w_down, block=256):
    count, width, hidden = w_gate.shape
    mid = count * hidden
    rows = pl.BlockSpec((count, block, hidden), lambda d: (0, d, 0))
    return pl.pallas_call(
        turn_kernel,
        grid=(width // block,),
        in_specs=[rows, rows, pl.BlockSpec((count, hidden, block), lambda d: (0, 0, d))],
        out_specs=[
            pl.BlockSpec((2 * mid, block), lambda d: (0, d)),
            pl.BlockSpec((block, mid), lambda d: (d, 0)),
        ],
        out_shape=[
            jax.ShapeDtypeStruct((2 * mid, width), BF),
            jax.ShapeDtypeStruct((width, mid), BF),
        ],
        compiler_params=PARAMS,
        cost_estimate=cost(0, 12 * mid * width),
    )(w_gate, w_up, w_down)


def expert_kernel(
    experts, first_ref, rows_ref, grad_ref, gate_ref, up_ref, down_ref, *outs
):
    low_ref, dots_ref, hid_ref, hid_turned_ref, glow_ref, ulow_ref = outs
    count, width, hidden_size = gate_ref.shape
    mid = count * hidden_size
    rows = rows_ref[:, :width]
    side = rows_ref[:, width:].astype(F32)
    lane = lax.broadcasted_iota(jnp.int32, side.shape, 1)
    dots = jnp.zeros(side.shape, F32)
    back_all = dot(grad_ref[...], down_ref[...], 1, 0)
    for e in range(count):
        column = first_ref[0] + e
        gate = jnp.sum(
            jnp.where((lane == column) | (lane == experts + column), side, 0.0), -1, keepdims=True
        )
        gate_pre = dot(rows, gate_ref[e], 1, 0)
        up_pre = dot(rows, up_ref[e], 1, 0)
        out_back = back_all[:, e * hidden_size : (e + 1) * hidden_size]
        sigma = 1.0 / (1.0 + jnp.exp(-gate_pre))
        silu = gate_pre * sigma
        hidden = silu * up_pre
        inner = jnp.sum(hidden * out_back, -1, keepdims=True)
        high = inner.astype(BF).astype(F32)
        dots = jnp.where(lane == column, high, dots)
        dots = jnp.where(lane == experts + column, inner - high, dots)
        hidden_low = (gate * hidden).astype(BF)
        hidden_grad = gate * out_back
        glow = (hidden_grad * up_pre * sigma * (1.0 + gate_pre * (1.0 - sigma))).astype(BF)
        ulow = (hidden_grad * silu).astype(BF)
        span = pl.ds(e * hidden_size, hidden_size)
        hid_ref[:, span] = hidden_low
        hid_turned_ref[span, :] = hidden_low.T
        glow_ref[:, span] = glow
        ulow_ref[:, span] = ulow
        low_ref[:, pl.ds(e * hidden_size, hidden_size)] = glow
        low_ref[:, pl.ds(mid + e * hidden_size, hidden_size)] = ulow
    dots_ref[...] = dots.astype(BF)


def expert_rows(rows_all, grad_all, w_gate, w_up, down_turned, first, experts, block):
    count, width, hidden = w_gate.shape
    total, wide = rows_all.shape
    mid = count * hidden

    def rows(columns):
        return pl.BlockSpec((block, columns), lambda i, *_: (i, 0))

    def shape(columns):
        return jax.ShapeDtypeStruct((total, columns), BF)

    return pl.pallas_call(
        functools.partial(expert_kernel, experts),
        grid_spec=pltpu.PrefetchScalarGridSpec(
            num_scalar_prefetch=1,
            grid=(total // block,),
            in_specs=[
                rows(wide),
                rows(width),
                resident(w_gate.shape),
                resident(w_up.shape),
                resident(down_turned.shape),
            ],
            out_specs=[
                rows(2 * mid),
                rows(wide - width),
                rows(mid),
                pl.BlockSpec((mid, block), lambda i, *_: (0, i)),
                rows(mid),
                rows(mid),
            ],
        ),
        out_shape=[
            shape(2 * mid),
            shape(wide - width),
            shape(mid),
            jax.ShapeDtypeStruct((mid, total), BF),
            shape(mid),
            shape(mid),
        ],
        compiler_params=PARAMS,
        cost_estimate=cost(3 * total * width * mid, total * wide * 6, total * mid),
    )(first, rows_all, grad_all, w_gate, w_up, down_turned)


def back_kernel(with_dots, index_ref, low_ref, both_ref, dots_ref, kept_ref, sent_ref):
    own = kept_ref.shape[2]
    place = index_ref[1]
    starts = [pl.multiple_of((r ^ place) * own, own) for r in range(4)]
    low = jnp.concatenate([low_ref[pl.ds(start, own), :] for start in starts], 0)
    back = dot(low, both_ref[...], 1, 0).astype(BF)
    columns = back.shape[1]
    for r in range(4):
        ref = sent_ref if r % 2 else kept_ref
        ref[0, r // 2, :, :columns] = back[r * own : (r + 1) * own]
        if with_dots:
            ref[0, r // 2, :, columns:] = dots_ref[pl.ds(starts[r], own), :]


def row_back(low, dots, both_turned, index, begin, end, with_dots):
    total, mid2 = low.shape
    block = 4 * (total // (4 * lax.axis_size("dp")))
    side = dots.shape[1] if with_dots else 0
    columns = end - begin
    owners = total // block
    out = pl.BlockSpec(
        (1, 2, block // 4, columns + side), lambda i, index_ref: (i ^ index_ref[0], 0, 0, 0)
    )
    shape = jax.ShapeDtypeStruct((owners, 2, block // 4, columns + side), BF)
    return pl.pallas_call(
        functools.partial(back_kernel, with_dots),
        grid_spec=pltpu.PrefetchScalarGridSpec(
            num_scalar_prefetch=1,
            grid=(owners,),
            in_specs=[
                pl.BlockSpec((block, mid2), lambda i, *_: (i, 0)),
                pl.BlockSpec(
                    (mid2, pl.Element(columns)), lambda i, *_: (0, begin), pipeline_mode=pl.Buffered(1)
                )
                if begin % columns
                else pl.BlockSpec(
                    (mid2, columns),
                    lambda i, *_: (0, begin // columns),
                    pipeline_mode=pl.Buffered(1),
                ),
                pl.BlockSpec((block, dots.shape[1]), lambda i, *_: (i, 0)),
            ],
            out_specs=[out, out],
        ),
        out_shape=[shape, shape],
        compiler_params=PARAMS,
        cost_estimate=cost(total * mid2 * columns, total * (mid2 + columns) * 2),
    )(index, low, both_turned, dots)


def sum_every(kept, sent, order):
    bits = lax.axis_size("dp").bit_length() - 1
    own, columns = kept.shape[2:]
    total = (kept.astype(F32) + swap(sent, "tensor", 1).astype(F32)).astype(BF)
    total = total.reshape((2,) * (bits + 1) + (own, columns))
    names = [("dp", 1 << (bits - 1 - i)) for i in range(bits)] + [("tensor", 2)]
    for name in order:
        axis = names.index(name)
        names.pop(axis)
        given = lax.index_in_dim(total, 1, axis, keepdims=False)
        total = lax.index_in_dim(total, 0, axis, keepdims=False).astype(F32)
        total = total + swap(given, *name).astype(F32)
        if names:
            total = total.astype(BF)
    return total


def out_kernel(hid_ref, down_ref, out_ref):
    count, hidden, _ = down_ref.shape
    out = dot(hid_ref[...], down_ref[...].reshape(count * hidden, -1), 1, 0)
    out_ref[...] = out.astype(BF)


def expert_out(hid, w_down, block=256):
    count, hidden, width = w_down.shape
    total = hid.shape[0]
    return pl.pallas_call(
        out_kernel,
        grid=(total // block,),
        in_specs=[
            pl.BlockSpec((block, count * hidden), lambda i: (i, 0)),
            resident(w_down.shape),
        ],
        out_specs=pl.BlockSpec((block, width), lambda i: (i, 0)),
        out_shape=jax.ShapeDtypeStruct((total, width), BF),
        compiler_params=PARAMS,
        cost_estimate=cost(total * width * count * hidden, total * width * 3),
    )(hid, w_down)


def over_kernel(left_ref, right_ref, out_ref):
    count, _, hidden = out_ref.shape
    product = dot(left_ref[...], right_ref[...], 0, 0)

    @pl.when(pl.program_id(1) == 0)
    def _():
        for e in range(count):
            out_ref[e] = product[:, e * hidden : (e + 1) * hidden]

    @pl.when(pl.program_id(1) > 0)
    def _():
        for e in range(count):
            out_ref[e] += product[:, e * hidden : (e + 1) * hidden]


def over_rows(rows, low, shape, block=256, chunk=2048):
    count, width, hidden = shape
    total = rows.shape[0]
    chunk = min(chunk, total)
    return pl.pallas_call(
        over_kernel,
        grid=(width // block, total // chunk),
        in_specs=[
            pl.BlockSpec((chunk, block), lambda d, k: (k, d)),
            pl.BlockSpec((chunk, count * hidden), lambda d, k: (k, 0)),
        ],
        out_specs=pl.BlockSpec((count, block, hidden), lambda d, k: (0, d, 0)),
        out_shape=jax.ShapeDtypeStruct(shape, F32),
        compiler_params=PARAMS,
        cost_estimate=cost(total * width * count * hidden, total * width * 4),
    )(rows, low)


def turned_kernel(left_ref, right_ref, out_ref):
    product = dot(left_ref[...], right_ref[...], 1, 0)

    @pl.when(pl.program_id(1) == 0)
    def _():
        out_ref[...] = product

    @pl.when(pl.program_id(1) > 0)
    def _():
        out_ref[...] += product


def turned_rows(left, right, block=256, chunk=2048):
    mid, total = left.shape
    width = right.shape[1]
    chunk = min(chunk, total)
    return pl.pallas_call(
        turned_kernel,
        grid=(width // block, total // chunk),
        in_specs=[
            pl.BlockSpec((mid, chunk), lambda d, k: (0, k)),
            pl.BlockSpec((chunk, block), lambda d, k: (k, d)),
        ],
        out_specs=pl.BlockSpec((mid, block), lambda d, k: (0, d)),
        out_shape=jax.ShapeDtypeStruct((mid, width), F32),
        compiler_params=PARAMS,
        cost_estimate=cost(total * width * mid, total * width * 4),
    )(left, right)


def per_device(
    tokens,
    segment_ids,
    routes,
    norm1_gain,
    w_query,
    w_key,
    w_value,
    query_gain,
    key_gain,
    w_out,
    norm2_gain,
    w_router,
    w_gate,
    w_up,
    w_down,
    cotangent,
):
    tok_count, model_width = tokens.shape
    heads_here, head_size = query_gain.shape
    local_width = heads_here * head_size
    tensor_count = lax.axis_size("tensor")
    full_width = local_width * tensor_count
    experts = w_router.shape[1]
    owners = lax.axis_size("dp")
    local_experts, _, local_hidden = w_gate.shape
    dp_place = lax.axis_index("dp")
    place = lax.axis_index("tensor")
    score_root = math.sqrt(head_size)
    own = tok_count // tensor_count
    parts = SPAN // heads_here
    part = tok_count // parts
    groups = span_groups(owners)

    def mine(array):
        return lax.dynamic_slice_in_dim(array, place * own, own, 0)

    def trade(array):
        return lax.all_to_all(
            array, "dp", split_axis=0, concat_axis=0, tiled=True, axis_index_groups=groups
        )

    out_grad_all = lax.all_gather(mine(cotangent), EVERY, axis=0, tiled=True)
    both_turned, down_turned = turn_weights(w_gate, w_up, w_down)

    state_in = tokens.astype(F32)
    scale_in = lax.rsqrt(jnp.mean(state_in * state_in, -1, keepdims=True) + EPSILON)
    unit_in = state_in * scale_in
    normed_in = (unit_in * norm1_gain).astype(BF)
    normed_in_all = lax.all_gather(mine(normed_in), EVERY, axis=0, tiled=True)
    query_raw = jnp.dot(normed_in, w_query, preferred_element_type=F32)
    key_raw = jnp.dot(normed_in, w_key, preferred_element_type=F32)
    value_att = jnp.dot(normed_in, w_value, preferred_element_type=F32).astype(BF)
    squares = lax.psum(
        jnp.stack([jnp.sum(query_raw * query_raw, -1), jnp.sum(key_raw * key_raw, -1)]), "tensor"
    )
    query_scale = lax.rsqrt(squares[0] / full_width + EPSILON)[:, None]
    key_scale = lax.rsqrt(squares[1] / full_width + EPSILON)[:, None]
    query_unit = query_raw * query_scale
    key_unit = key_raw * key_scale
    local_pos = jnp.arange(tok_count, dtype=jnp.int32)
    positions = (dp_place % SPAN * tok_count + local_pos).astype(F32)
    cos_table, sin_table = rope_tables(positions, head_size)
    query_att = rotate(
        (query_unit * query_gain.reshape(-1)).reshape(tok_count, heads_here, head_size),
        cos_table,
        sin_table,
    ).astype(BF)
    key_att = rotate(
        (key_unit * key_gain.reshape(-1)).reshape(tok_count, heads_here, head_size),
        cos_table,
        sin_table,
    ).astype(BF)

    def head_parts(array):
        split = array.reshape(parts, part, heads_here, head_size)
        return split.transpose(2, 0, 1, 3)

    def head_blocks(array):
        split = array.reshape(tok_count, heads_here, head_size).transpose(1, 0, 2)
        return jnp.broadcast_to(
            split[:, None], (heads_here, parts, tok_count, head_size)
        )

    segment_rows = jnp.zeros((16, head_size), BF).at[: tok_count // head_size].set(
        segment_ids.astype(BF).reshape(-1, head_size)
    )
    segment_rows = jnp.broadcast_to(segment_rows, (heads_here, parts) + segment_rows.shape)
    sent = jnp.concatenate(
        [head_parts(query_att), head_blocks(key_att), head_blocks(value_att), segment_rows], 2
    ).reshape(SPAN, part + 2 * tok_count + 16, head_size)
    got = trade(sent)
    seq = SPAN * tok_count
    query_h = got[:, :part].reshape(SPAN * part, head_size)
    key_h = got[:, part : part + tok_count].reshape(seq, head_size)
    value_h = got[:, part + tok_count : part + 2 * tok_count].reshape(seq, head_size)
    segment_h = got[:, part + 2 * tok_count :].reshape(SPAN, -1)[:, :tok_count]
    half = dp_place % SPAN % parts
    key_pos = jnp.arange(seq, dtype=jnp.int32)
    query_pos = (
        jnp.arange(SPAN, dtype=jnp.int32)[:, None] * tok_count
        + half * part
        + jnp.arange(part, dtype=jnp.int32)[None]
    ).reshape(-1)
    segment_q = lax.dynamic_slice_in_dim(segment_h, half * part, part, 1).reshape(-1)
    visible = (segment_h.reshape(-1)[None, :] == segment_q[:, None]) & (
        key_pos[None, :] <= query_pos[:, None]
    )
    raw_scores = dot(query_h, key_h, 1, 1) / score_root
    masked = jnp.where(visible, raw_scores, NEGATIVE)
    row_top = jnp.max(masked, -1, keepdims=True)
    log_total = row_top + jnp.log(jnp.sum(jnp.exp(masked - row_top), -1, keepdims=True))
    attn_probs = jnp.where(visible, jnp.exp(masked - log_total), 0.0)
    probs_low = attn_probs.astype(BF)
    mix_h = dot(probs_low, value_h, 1, 0).astype(BF)

    def to_tokens(array):
        back = trade(array).reshape(heads_here, parts, part, head_size)
        return back.transpose(1, 2, 0, 3).reshape(tok_count, local_width)

    attn_mix = to_tokens(mix_h.reshape(SPAN, part, head_size))
    attn_full = sum_tensor(jnp.dot(attn_mix, w_out, preferred_element_type=F32), place)
    resid_state = mine(state_in) + attn_full
    scale_mid = lax.rsqrt(jnp.mean(resid_state * resid_state, -1, keepdims=True) + EPSILON)
    unit_mid = resid_state * scale_mid
    normed_mid = (unit_mid * norm2_gain).astype(BF)
    logits = jnp.dot(normed_mid, w_router, preferred_element_type=F32)
    router_probs = jax.nn.softmax(logits, -1)
    chosen = jnp.sum(
        (mine(routes)[:, :, None] == jnp.arange(experts, dtype=jnp.int32)).astype(F32), 1
    )
    gates = router_probs * chosen
    gates_high = gates.astype(BF)
    gates_low = (gates - gates_high.astype(F32)).astype(BF)
    side_width = -(-2 * experts // 128) * 128
    side = jnp.concatenate(
        [gates_high, gates_low, jnp.zeros((own, side_width - 2 * experts), BF)], 1
    )
    rows_all = lax.all_gather(
        jnp.concatenate([normed_mid, side], 1), EVERY, axis=0, tiled=True
    )
    index = jnp.stack([dp_place, place]).astype(jnp.int32)
    first = (dp_place * local_experts).astype(jnp.int32).reshape(1)
    low, dots, hid, hid_turned, glow, ulow = expert_rows(
        rows_all, out_grad_all, w_gate, w_up, down_turned, first, experts, tok_count
    )
    bits = owners.bit_length() - 1
    first_three = [("tensor", 2), ("dp", 1), ("dp", 2)]
    rest = [("dp", 1 << b) for b in range(2, bits)]
    lanes = -(-(model_width + side_width) // (3 * LANES)) * LANES
    homes = []
    for g in range(3):
        begin, end = g * lanes, min((g + 1) * lanes, model_width)
        kept, sent = row_back(low, dots, both_turned, index, begin, end, g == 2)
        homes.append(sum_every(kept, sent, first_three[g:] + first_three[:g] + rest))
    home = jnp.concatenate(homes, 1)
    out_part = expert_out(hid, w_down)
    expert_full = lax.psum_scatter(out_part, EVERY, scatter_dimension=0, tiled=True).astype(F32)
    block_output = spread_tensor((resid_state + expert_full).astype(BF), place)
    d_w_down = turned_rows(hid_turned, out_grad_all).reshape(w_down.shape)
    d_w_gate = over_rows(rows_all, glow, w_gate.shape)
    d_w_up = over_rows(rows_all, ulow, w_up.shape)

    row_home = home[:, :model_width]
    side_home = home[:, model_width:]
    probs_grad = chosen * (side_home[:, :experts] + side_home[:, experts : 2 * experts])
    logit_low = (
        router_probs * (probs_grad - jnp.sum(router_probs * probs_grad, -1, keepdims=True))
    ).astype(BF)
    d_router = dot(logit_low, normed_mid, 0, 0)
    mid_grad = row_home + dot(logit_low, w_router, 1, 1)
    d_gain_mid = jnp.sum(mid_grad * unit_mid, 0)
    mid_scaled = mid_grad * norm2_gain
    resid_grad = mine(cotangent).astype(F32) + scale_mid * (
        mid_scaled - unit_mid * jnp.mean(mid_scaled * unit_mid, -1, keepdims=True)
    )
    resid_low = spread_tensor(resid_grad.astype(BF), place)
    d_out = dot(attn_mix, resid_low, 0, 0)
    d_out = lax.psum_scatter(d_out.astype(BF), "dp", scatter_dimension=1, tiled=True).astype(F32)
    mix_grad = head_parts(dot(resid_low, w_out, 1, 1).astype(BF)).reshape(SPAN, part, head_size)
    mix_grad_h = trade(mix_grad).reshape(SPAN * part, head_size)

    p_grad = dot(mix_grad_h, value_h, 1, 1)
    score_low = (attn_probs * (p_grad - jnp.sum(attn_probs * p_grad, -1, keepdims=True))).astype(BF)
    query_back = (dot(score_low, key_h, 1, 0) / score_root).astype(BF)
    key_back = (dot(score_low, query_h, 0, 0) / score_root).astype(BF)
    value_back = dot(probs_low, mix_grad_h, 0, 0).astype(BF)
    back = trade(
        jnp.concatenate(
            [
                query_back.reshape(SPAN, part, head_size),
                key_back.reshape(SPAN, tok_count, head_size),
                value_back.reshape(SPAN, tok_count, head_size),
            ],
            1,
        )
    ).reshape(heads_here, parts, part + 2 * tok_count, head_size)
    query_att_grad = (
        back[:, :, :part].transpose(1, 2, 0, 3).reshape(tok_count, heads_here, head_size)
    )
    key_att_grad = jnp.sum(back[:, :, part : part + tok_count].astype(F32), 1).astype(BF)
    key_att_grad = key_att_grad.transpose(1, 0, 2)
    value_low = jnp.sum(back[:, :, part + tok_count :].astype(F32), 1).astype(BF)
    value_low = value_low.transpose(1, 0, 2).reshape(tok_count, local_width)

    query_gain_in = unrotate(query_att_grad.astype(F32), cos_table, sin_table).reshape(
        tok_count, local_width
    )
    key_gain_in = unrotate(key_att_grad.astype(F32), cos_table, sin_table).reshape(
        tok_count, local_width
    )
    d_query_gain = jnp.sum(query_gain_in * query_unit, 0).reshape(heads_here, head_size)
    d_key_gain = jnp.sum(key_gain_in * key_unit, 0).reshape(heads_here, head_size)
    query_scaled = query_gain_in * query_gain.reshape(-1)
    key_scaled = key_gain_in * key_gain.reshape(-1)
    inner = lax.psum(
        jnp.stack([jnp.sum(query_scaled * query_unit, -1), jnp.sum(key_scaled * key_unit, -1)]),
        "tensor",
    )
    query_low = (
        query_scale * (query_scaled - query_unit * (inner[0] / full_width)[:, None])
    ).astype(BF)
    key_low = (key_scale * (key_scaled - key_unit * (inner[1] / full_width)[:, None])).astype(BF)

    slice_width = local_width // owners
    columns = jnp.stack([query_low.T, key_low.T, value_low.T])
    columns = columns.reshape(3, owners, slice_width, tok_count).transpose(1, 0, 2, 3)
    columns = columns.reshape(owners, 3 * slice_width, tok_count)
    columns = lax.all_to_all(columns, "dp", split_axis=0, concat_axis=0, tiled=True)
    columns = columns.transpose(1, 0, 2).reshape(3 * slice_width, owners * tok_count)
    d_columns = dot(columns, normed_in_all, 1, 0)

    in_part = (
        dot(query_low, w_query, 1, 1) + dot(key_low, w_key, 1, 1) + dot(value_low, w_value, 1, 1)
    )
    in_grad_norm = sum_tensor(in_part, place)
    unit_own = mine(unit_in)
    d_gain_in = jnp.sum(in_grad_norm * unit_own, 0)
    in_scaled = in_grad_norm * norm1_gain
    input_grad = resid_grad + mine(scale_in) * (
        in_scaled - unit_own * jnp.mean(in_scaled * unit_own, -1, keepdims=True)
    )
    input_grad = spread_tensor(input_grad.astype(BF), place).astype(F32)

    model_slice = model_width // owners
    head_slice = head_size // owners
    gains = jnp.stack([d_query_gain, d_key_gain]).reshape(2 * heads_here, owners, head_slice)
    gains = gains.transpose(1, 0, 2).reshape(owners, 1, 2 * heads_here * head_slice)
    gains = jnp.pad(gains, ((0, 0), (0, 0), (0, max(0, model_slice - gains.shape[2]))))
    gain_rows = gains.reshape(owners, -1, model_slice)
    by_owner = jnp.concatenate([d_router, d_gain_mid[None], d_gain_in[None]], 0)
    by_owner = by_owner.reshape(-1, owners, model_slice).transpose(1, 0, 2)
    small = jnp.concatenate([by_owner, gain_rows], 1).astype(BF)
    pad_rows = -small.shape[1] % 16
    small = jnp.pad(small, ((0, 0), (0, pad_rows), (0, 0)))
    big = d_columns.reshape(3 * slice_width, owners, model_slice).transpose(1, 0, 2).astype(BF)
    final = lax.all_to_all(
        jnp.concatenate([big, small], 1), "dp", split_axis=0, concat_axis=0, tiled=True
    ).astype(F32)
    weights = final[:, : 3 * slice_width].reshape(owners, 3, slice_width, model_slice)
    weights = weights.transpose(1, 3, 0, 2).reshape(3, model_slice, local_width)
    small = jnp.sum(final[:, 3 * slice_width :], 0)
    shared = lax.psum(small[: experts + 2], "tensor")
    gains = small[experts + 2 : experts + 2 + gain_rows.shape[1]].reshape(-1)
    gains = gains[: 2 * heads_here * head_slice].reshape(2, heads_here, head_slice)

    return (
        block_output,
        input_grad,
        shared[experts + 1],
        weights[0],
        weights[1],
        weights[2],
        gains[0],
        gains[1],
        d_out,
        shared[experts],
        shared[:experts].T,
        d_w_gate,
        d_w_up,
        d_w_down,
    )


def solution(mesh):
    in_specs = (
        P("dp", None),
        P("dp"),
        P("dp", None),
        P(),
        P(None, "tensor"),
        P(None, "tensor"),
        P(None, "tensor"),
        P("tensor", None),
        P("tensor", None),
        P("tensor", None),
        P(),
        P(),
        P("dp", None, "tensor"),
        P("dp", None, "tensor"),
        P("dp", "tensor", None),
        P("dp", None),
    )
    out_specs = (
        P("dp", None),
        P("dp", None),
        P("dp"),
        P("dp", "tensor"),
        P("dp", "tensor"),
        P("dp", "tensor"),
        P("tensor", "dp"),
        P("tensor", "dp"),
        P("tensor", "dp"),
        P("dp"),
        P("dp", None),
        P("dp", None, "tensor"),
        P("dp", None, "tensor"),
        P("dp", "tensor", None),
    )
    return jax.shard_map(
        per_device, mesh=mesh, in_specs=in_specs, out_specs=out_specs, check_vma=False
    )
```

```python
import functools
import math

import jax
import jax.numpy as jnp
from jax import lax
from jax.experimental import pallas as pl
from jax.experimental.pallas import tpu as pltpu
from jax.sharding import PartitionSpec as P

SPAN = 8


EPSILON = 1e-05
ROPE_BASE = 10000.0
NEGATIVE = -1e30
BF = jnp.bfloat16
F32 = jnp.float32
EVERY = ("dp", "tensor")
VMEM_LIMIT = 56 * 1024 * 1024
LANES = 128


def rope_tables(positions, head_size):
    frequency = ROPE_BASE ** (-jnp.arange(0, head_size, 2, dtype=jnp.float32) / head_size)
    angles = positions[:, None] * frequency[None, :]
    cosine, sine = jnp.cos(angles), jnp.sin(angles)
    return jnp.concatenate([cosine, cosine], -1), jnp.concatenate([-sine, sine], -1)


def dot(left_side, right_side, left_dim, right_dim):
    return lax.dot_general(
        left_side,
        right_side,
        (((left_dim,), (right_dim,)), ((), ())),
        preferred_element_type=jnp.float32,
    )


def swap(array, axis, bit):
    count = lax.axis_size(axis)
    return lax.ppermute(array, axis, [(i, i ^ bit) for i in range(count)])


def resident(shape):
    return pl.BlockSpec(shape, lambda *_: (0,) * len(shape), pipeline_mode=pl.Buffered(1))


def cost(macs, size, transcendentals=0):
    return pl.CostEstimate(flops=2 * macs, bytes_accessed=size, transcendentals=transcendentals)


PARAMS = pltpu.CompilerParams(vmem_limit_bytes=VMEM_LIMIT)


def turn_kernel(gate_ref, up_ref, down_ref, both_ref, down_out_ref):
    count, _, hidden = gate_ref.shape
    for e in range(count):
        both_ref[pl.ds(e * hidden, hidden), :] = gate_ref[e].T
        both_ref[pl.ds((count + e) * hidden, hidden), :] = up_ref[e].T
        down_out_ref[:, pl.ds(e * hidden, hidden)] = down_ref[e].T


def turn_weights(w_gate, w_up, w_down, block=256):
    count, width, hidden = w_gate.shape
    mid = count * hidden
    rows = pl.BlockSpec((count, block, hidden), lambda d: (0, d, 0))
    return pl.pallas_call(
        turn_kernel,
        grid=(width // block,),
        in_specs=[rows, rows, pl.BlockSpec((count, hidden, block), lambda d: (0, 0, d))],
        out_specs=[
            pl.BlockSpec((2 * mid, block), lambda d: (0, d)),
            pl.BlockSpec((block, mid), lambda d: (d, 0)),
        ],
        out_shape=[
            jax.ShapeDtypeStruct((2 * mid, width), BF),
            jax.ShapeDtypeStruct((width, mid), BF),
        ],
        compiler_params=PARAMS,
        cost_estimate=cost(0, 12 * mid * width),
    )(w_gate, w_up, w_down)


def hidden_back_kernel(grad_ref, down_ref, out_ref):
    out_ref[...] = dot(grad_ref[...], down_ref[...], 1, 0)


def hidden_back(grad_all, down_turned, block=256):
    width, mid = down_turned.shape
    total = grad_all.shape[0]
    return pl.pallas_call(
        hidden_back_kernel,
        grid=(total // block,),
        in_specs=[pl.BlockSpec((block, width), lambda i: (i, 0)), resident(down_turned.shape)],
        out_specs=pl.BlockSpec((block, mid), lambda i: (i, 0)),
        out_shape=jax.ShapeDtypeStruct((total, mid), F32),
        compiler_params=PARAMS,
        cost_estimate=cost(total * width * mid, total * width * 3),
    )(grad_all, down_turned)


def expert_kernel(experts, axes, index_ref, *refs):
    pieces, refs = (refs[:3], refs[3:6]), refs[6:]
    back_ref, gate_ref, up_ref, both_ref, rows_ref = refs[:5]
    hid_ref, hid_turned_ref, glow_ref, ulow_ref = refs[5:9]
    kept_refs, sent_refs, low_ref, side_ref = refs[9:12], refs[12:15], refs[15], refs[16]
    count, width, hidden_size = gate_ref.shape
    mid = count * hidden_size
    own = kept_refs[0].shape[2]
    starts = [pl.multiple_of((r ^ index_ref[1]) * own, own) for r in range(4)]
    for r in range(4):
        begin = 0
        for piece, axis in zip(pieces[r % 2], axes):
            place = [0] * (len(piece.shape) - 2)
            place[axis] = r // 2
            columns = piece.shape[-1]
            end = min(begin + columns, width)
            value = piece[tuple(place)]
            rows_ref[pl.ds(starts[r], own), begin:end] = value[:, : end - begin]
            if end - begin < columns:
                side_ref[pl.ds(starts[r], own), :] = value[:, end - begin :]
            begin = end
    rows = rows_ref[...]
    side = side_ref[...].astype(F32)
    lane = lax.broadcasted_iota(jnp.int32, side.shape, 1)
    dots = jnp.zeros(side.shape, F32)
    for e in range(count):
        column = index_ref[0] * count + e
        gate = jnp.sum(
            jnp.where((lane == column) | (lane == experts + column), side, 0.0), -1, keepdims=True
        )
        span = pl.ds(e * hidden_size, hidden_size)
        gate_pre = dot(rows, gate_ref[e], 1, 0)
        up_pre = dot(rows, up_ref[e], 1, 0)
        out_back = back_ref[:, span]
        sigma = 1.0 / (1.0 + jnp.exp(-gate_pre))
        silu = gate_pre * sigma
        hidden = silu * up_pre
        inner = jnp.sum(hidden * out_back, -1, keepdims=True)
        high = inner.astype(BF).astype(F32)
        dots = jnp.where(lane == column, high, dots)
        dots = jnp.where(lane == experts + column, inner - high, dots)
        hidden_low = (gate * hidden).astype(BF)
        hidden_grad = gate * out_back
        glow = (hidden_grad * up_pre * sigma * (1.0 + gate_pre * (1.0 - sigma))).astype(BF)
        ulow = (hidden_grad * silu).astype(BF)
        hid_ref[:, span] = hidden_low
        hid_turned_ref[span, :] = hidden_low.T
        glow_ref[:, span] = glow
        ulow_ref[:, span] = ulow
        low_ref[:, span] = glow
        low_ref[:, pl.ds(mid + e * hidden_size, hidden_size)] = ulow
    low_ref[:, 2 * mid :] = dots.astype(BF)
    low = jnp.concatenate([low_ref[pl.ds(start, own), :] for start in starts], 0)
    begin = 0
    for kept_ref, sent_ref in zip(kept_refs, sent_refs):
        columns = kept_ref.shape[3]
        end = min(begin + columns, width)
        back = dot(low[:, : 2 * mid], both_ref[:, begin:end], 1, 0).astype(BF)
        if end - begin < columns:
            back = jnp.concatenate([back, low[:, 2 * mid :]], 1)
        begin = end
        for r in range(4):
            ref = sent_ref if r % 2 else kept_ref
            ref[0, r // 2] = back[r * own : (r + 1) * own]


def expert_rows(pieces, names, back_all, w_gate, w_up, both_turned, index, experts, block):
    count, width, hidden = w_gate.shape
    total, mid = back_all.shape
    owners = total // block
    groups = [piece.shape[-1] for piece in pieces[0]]
    side = sum(groups) - width

    def rows(columns):
        return pl.BlockSpec((block, columns), lambda i, index_ref: (i ^ index_ref[0], 0))

    def shape(columns):
        return jax.ShapeDtypeStruct((total, columns), BF)

    def given(columns, order):
        sizes = tuple(1 if axis == "dp" else 2 for axis, _ in order)

        def place(i, *_):
            return tuple(i // bit % 2 if axis == "dp" else 0 for axis, bit in order) + (0, 0)

        return pl.BlockSpec(sizes + (block // 4, columns), place)

    def part(columns):
        return pl.BlockSpec((1, 2, block // 4, columns), lambda i, *_: (i, 0, 0, 0))

    def part_shape(columns):
        return jax.ShapeDtypeStruct((owners, 2, block // 4, columns), BF)

    given_specs = [given(columns, order) for columns, order in zip(groups, names)]
    axes = [[axis for axis, _ in order].index("tensor") for order in names]
    outs = pl.pallas_call(
        functools.partial(expert_kernel, experts, axes),
        grid_spec=pltpu.PrefetchScalarGridSpec(
            num_scalar_prefetch=1,
            grid=(owners,),
            in_specs=given_specs * 2
            + [
                rows(mid),
                resident(w_gate.shape),
                resident(w_up.shape),
                resident(both_turned.shape),
            ],
            out_specs=[
                rows(width),
                rows(mid),
                pl.BlockSpec((mid, block), lambda i, index_ref: (0, i ^ index_ref[0])),
                rows(mid),
                rows(mid),
            ]
            + [part(columns) for columns in groups] * 2,
            scratch_shapes=[pltpu.VMEM((block, 2 * mid + side), BF), pltpu.VMEM((block, side), BF)],
        ),
        out_shape=[
            shape(width),
            shape(mid),
            jax.ShapeDtypeStruct((mid, total), BF),
            shape(mid),
            shape(mid),
        ]
        + [part_shape(columns) for columns in groups] * 2,
        compiler_params=PARAMS,
        cost_estimate=cost(4 * total * width * mid, total * width * 8, total * mid),
    )(index, *pieces[0], *pieces[1], back_all, w_gate, w_up, both_turned)
    return outs[:5], outs[5:8], outs[8:]


def gather_every(groups, orders, beside, later):
    totals, names = list(groups), [[] for _ in groups]
    for step in range(len(orders[0])):
        if step == len(orders[0]) - 1:
            totals, later = lax.optimization_barrier((totals, later))
        others = [swap(total, *order[step]) for total, order in zip(totals, orders)]
        if step == len(orders[0]) - 1:
            others, beside = lax.optimization_barrier((others, beside))
        totals = [jnp.stack([total, other]) for total, other in zip(totals, others)]
        for name, order in zip(names, orders):
            name.insert(0, order[step])
    return (totals, [swap(total, "tensor", 1) for total in totals]), names, beside, later


def sum_every(kept, sent, orders, beside, finish):
    bits = lax.axis_size("dp").bit_length() - 1
    totals, names = [], []
    for kept_group, sent_group in zip(kept, sent):
        own, columns = kept_group.shape[2:]
        total = kept_group.astype(F32) + swap(sent_group, "tensor", 1).astype(F32)
        totals.append(total.astype(BF).reshape((2,) * (bits + 1) + (own, columns)))
        names.append([("dp", 1 << (bits - 1 - i)) for i in range(bits)] + [("tensor", 2)])
    for step in range(bits + 1):
        if step == bits:
            totals, beside = lax.optimization_barrier((totals, beside[:1] + finish(*beside[1:])))
        halves, others = [], []
        for total, left, order in zip(totals, names, orders):
            axis = left.index(order[step])
            left.pop(axis)
            given = lax.index_in_dim(total, 1, axis, keepdims=False)
            halves.append(lax.index_in_dim(total, 0, axis, keepdims=False))
            others.append(swap(given, *order[step]))
        if step == 0:
            others, beside = lax.optimization_barrier((others, beside))
        totals = [(a.astype(F32) + b.astype(F32)).astype(BF) for a, b in zip(halves, others)]
    return list(zip(halves, others)), *beside


def out_kernel(core_ref, hid_ref, down_ref, kept_ref, sent_ref):
    count, hidden, _ = down_ref.shape
    own = kept_ref.shape[1]
    rows = []
    for r in range(4):
        start = pl.multiple_of((r // 2 * 2 + ((r % 2) ^ core_ref[0])) * own, own)
        rows.append(hid_ref[pl.ds(start, own), :])
    weight = down_ref[...].reshape(count * hidden, -1)
    out = dot(jnp.concatenate(rows, 0), weight, 1, 0).astype(BF)
    for r in range(4):
        ref = sent_ref if r % 2 else kept_ref
        ref[r // 2] = out[r * own : (r + 1) * own]


def expert_out(hid, w_down, core, block):
    count, hidden, width = w_down.shape
    total = hid.shape[0]
    out = pl.BlockSpec((2, block // 4, width), lambda i, *_: (i, 0, 0))
    shape = jax.ShapeDtypeStruct((total // block * 2, block // 4, width), BF)
    return pl.pallas_call(
        out_kernel,
        grid_spec=pltpu.PrefetchScalarGridSpec(
            num_scalar_prefetch=1,
            grid=(total // block,),
            in_specs=[
                pl.BlockSpec((block, count * hidden), lambda i, *_: (i, 0)),
                resident(w_down.shape),
            ],
            out_specs=[out, out],
        ),
        out_shape=[shape, shape],
        compiler_params=PARAMS,
        cost_estimate=cost(total * width * count * hidden, total * width * 3),
    )(core, hid, w_down)


def over_kernel(left_ref, right_ref, out_ref):
    count, _, hidden = out_ref.shape
    product = dot(left_ref[...], right_ref[...], 0, 0)

    @pl.when(pl.program_id(1) == 0)
    def _():
        for e in range(count):
            out_ref[e] = product[:, e * hidden : (e + 1) * hidden]

    @pl.when(pl.program_id(1) > 0)
    def _():
        for e in range(count):
            out_ref[e] += product[:, e * hidden : (e + 1) * hidden]


def over_rows(rows, low, shape, block=256, chunk=2048):
    count, width, hidden = shape
    total = rows.shape[0]
    chunk = min(chunk, total)
    return pl.pallas_call(
        over_kernel,
        grid=(width // block, total // chunk),
        in_specs=[
            pl.BlockSpec((chunk, block), lambda d, k: (k, d)),
            pl.BlockSpec((chunk, count * hidden), lambda d, k: (k, 0)),
        ],
        out_specs=pl.BlockSpec((count, block, hidden), lambda d, k: (0, d, 0)),
        out_shape=jax.ShapeDtypeStruct(shape, F32),
        compiler_params=PARAMS,
        cost_estimate=cost(total * width * count * hidden, total * width * 4),
    )(rows, low)


def turned_kernel(left_ref, right_ref, out_ref):
    product = dot(left_ref[...], right_ref[...], 1, 0)

    @pl.when(pl.program_id(1) == 0)
    def _():
        out_ref[...] = product

    @pl.when(pl.program_id(1) > 0)
    def _():
        out_ref[...] += product


def turned_rows(left, right, block=256, chunk=2048):
    mid, total = left.shape
    width = right.shape[1]
    chunk = min(chunk, total)
    return pl.pallas_call(
        turned_kernel,
        grid=(width // block, total // chunk),
        in_specs=[
            pl.BlockSpec((mid, chunk), lambda d, k: (0, k)),
            pl.BlockSpec((chunk, block), lambda d, k: (k, d)),
        ],
        out_specs=pl.BlockSpec((mid, block), lambda d, k: (0, d)),
        out_shape=jax.ShapeDtypeStruct((mid, width), F32),
        compiler_params=PARAMS,
        cost_estimate=cost(total * width * mid, total * width * 4),
    )(left, right)


def front_kernel(tokens_ref, gain_ref, query_ref, key_ref, value_ref, *outs):
    normed_ref, query_out_ref, key_out_ref, value_out_ref, squares_ref = outs

    @pl.when(pl.program_id(0) == 0)
    def _():
        state = tokens_ref[...].astype(F32)
        scale = lax.rsqrt(jnp.mean(state * state, -1, keepdims=True) + EPSILON)
        normed_ref[...] = (state * scale * gain_ref[...]).astype(BF)
        squares_ref[...] = jnp.zeros_like(squares_ref)

    normed = normed_ref[...]
    query = dot(normed, query_ref[...], 1, 0)
    key = dot(normed, key_ref[...], 1, 0)
    query_out_ref[...] = query
    key_out_ref[...] = key
    value_out_ref[...] = dot(normed, value_ref[...], 1, 0).astype(BF)
    squares_ref[...] += two_rows(query * query, key * key)


def row_sums(array):
    ones = jnp.ones((8, array.shape[1]), F32)
    return lax.dot_general(
        ones,
        array,
        (((1,), (1,)), ((), ())),
        precision=lax.Precision.HIGHEST,
        preferred_element_type=F32,
    )


def two_rows(first, second):
    row = lax.broadcasted_iota(jnp.int32, (8, first.shape[0]), 0)
    return jnp.where(row == 0, row_sums(first), jnp.where(row == 1, row_sums(second), 0.0))


def norm_kernel(tokens_ref, gain_ref, out_ref):
    state = tokens_ref[...].astype(F32)
    scale = lax.rsqrt(jnp.mean(state * state, -1, keepdims=True) + EPSILON)
    out_ref[...] = (state * scale * gain_ref[...]).astype(BF)


def norm_all(tokens, gain, block):
    total, width = tokens.shape
    return pl.pallas_call(
        norm_kernel,
        grid=(total // block,),
        in_specs=[pl.BlockSpec((block, width), lambda i: (i, 0)), resident((1, width))],
        out_specs=pl.BlockSpec((block, width), lambda i: (i, 0)),
        out_shape=jax.ShapeDtypeStruct((total, width), BF),
        compiler_params=PARAMS,
        cost_estimate=cost(0, total * width * 4),
    )(tokens, gain[None])


def project(tokens, gain, w_query, w_key, w_value, block=256):
    count, width = tokens.shape
    local = w_query.shape[1]
    weight = pl.BlockSpec((width, block), lambda i: (0, i))
    out = pl.BlockSpec((count, block), lambda i: (0, i))
    return pl.pallas_call(
        front_kernel,
        grid=(local // block,),
        in_specs=[resident(tokens.shape), resident((1, width)), weight, weight, weight],
        out_specs=[resident((count, width)), out, out, out, resident((8, count))],
        out_shape=[
            jax.ShapeDtypeStruct((count, width), BF),
            jax.ShapeDtypeStruct((count, local), F32),
            jax.ShapeDtypeStruct((count, local), F32),
            jax.ShapeDtypeStruct((count, local), BF),
            jax.ShapeDtypeStruct((8, count), F32),
        ],
        compiler_params=PARAMS,
        cost_estimate=cost(3 * count * width * local, 6 * width * local),
    )(tokens, gain[None], w_query, w_key, w_value)


def scales_of(sums, full_width):
    return lax.rsqrt(sums.T / full_width + EPSILON)


def pack_kernel(full_width, query_ref, key_ref, value_ref, sums_ref, *refs):
    query_gain_ref, key_gain_ref, cos_ref, sin_ref, segment_ref, out_ref = refs
    parts, heads = out_ref.shape[0] // query_gain_ref.shape[0], query_gain_ref.shape[0]
    size = cos_ref.shape[1]
    count = cos_ref.shape[0]
    part = count // parts
    scales = scales_of(sums_ref[...], full_width)
    for h in range(heads):
        span = slice(h * size, (h + 1) * size)

        def turned(ref, column, gain_ref):
            unit = ref[:, span] * scales[:, column : column + 1]
            vector = unit * gain_ref[pl.ds(h, 1), :]
            rolled = pltpu.roll(vector, size // 2, 1)
            return (vector * cos_ref[...] + rolled * sin_ref[...]).astype(BF)

        query = turned(query_ref, 0, query_gain_ref)
        key = turned(key_ref, 1, key_gain_ref)
        value = value_ref[:, span]
        for p in range(parts):
            place = h * parts + p
            out_ref[place, :part] = query[p * part : (p + 1) * part]
            out_ref[place, part : part + count] = key
            out_ref[place, part + count : part + 2 * count] = value
            out_ref[place, part + 2 * count :] = segment_ref[...]


def pack_heads(query, key, value, sums, query_gain, key_gain, cos, sin, segments, full_width):
    count = query.shape[0]
    size = cos.shape[1]
    parts = SPAN // query_gain.shape[0]
    return pl.pallas_call(
        functools.partial(pack_kernel, full_width),
        out_shape=jax.ShapeDtypeStruct(
            (SPAN, count // parts + 2 * count + segments.shape[0], size), BF
        ),
        compiler_params=PARAMS,
        cost_estimate=cost(0, 12 * query.size),
    )(query, key, value, sums, query_gain, key_gain, cos, sin, segments)


def head_views(got_ref, s, part, count):
    length = (s + 1) * count
    size = got_ref.shape[2]
    query = got_ref[s, :part]
    key = got_ref[: s + 1, part : part + count].reshape(length, size)
    value = got_ref[: s + 1, part + count : part + 2 * count].reshape(length, size)
    return query, key, value


def visible_pairs(got_ref, half, s, part, count):
    size = got_ref.shape[2]
    per_block = count // size
    first = part + 2 * count

    def rows(block):
        return got_ref[block, first : first + 16].astype(F32)

    row = lax.broadcasted_iota(jnp.int32, (16, size), 0)
    chosen = jnp.sum(jnp.where(row == half, rows(s), 0.0), 0, keepdims=True)
    own = jnp.broadcast_to(chosen, (size, size)).T
    pieces = []
    for block in range(s + 1):
        values = rows(block)
        for r in range(per_block):
            pieces.append(own == values[r : r + 1])
    pieces = [jnp.where(piece, 1.0, 0.0) for piece in pieces]
    same = jnp.concatenate(pieces, 1) > 0.5
    query_pos = s * count + half * part + lax.broadcasted_iota(jnp.int32, same.shape, 0)
    return same & (lax.broadcasted_iota(jnp.int32, same.shape, 1) <= query_pos)


def attend_kernel(part, count, half_ref, got_ref, mix_ref, log_ref):
    half = half_ref[0]
    size = got_ref.shape[2]
    for s in range(SPAN):
        query, key, value = head_views(got_ref, s, part, count)
        visible = visible_pairs(got_ref, half, s, part, count)
        scores = jnp.where(visible, dot(query, key, 1, 1) / math.sqrt(size), NEGATIVE)
        top = jnp.max(scores, -1, keepdims=True)
        weights = jnp.where(visible, jnp.exp(scores - top), 0.0)
        total = jnp.sum(weights, -1, keepdims=True)
        mix_ref[s] = dot((weights / total).astype(BF), value, 1, 0).astype(BF)
        log_ref[s] = jnp.broadcast_to(top + jnp.log(total), (part, size))


def attend(got, half, part, count):
    size = got.shape[2]
    return pl.pallas_call(
        functools.partial(attend_kernel, part, count),
        in_specs=[
            pl.BlockSpec(memory_space=pltpu.SMEM),
            pl.BlockSpec(memory_space=pltpu.VMEM),
        ],
        out_shape=[
            jax.ShapeDtypeStruct((SPAN, part, size), BF),
            jax.ShapeDtypeStruct((SPAN, part, size), F32),
        ],
        compiler_params=PARAMS,
        cost_estimate=cost(SPAN * SPAN * part * count * size, 4 * got.size, SPAN * SPAN * part * count),
    )(half, got)


def attend_back_kernel(part, count, half_ref, got_ref, log_ref, grad_ref, out_ref, key_sum, value_sum):
    half = half_ref[0]
    size = got_ref.shape[2]
    root = math.sqrt(size)
    for s in reversed(range(SPAN)):
        length = (s + 1) * count
        query, key, value = head_views(got_ref, s, part, count)
        visible = visible_pairs(got_ref, half, s, part, count)
        scores = dot(query, key, 1, 1) / root - log_ref[s, :, :1]
        probs = jnp.where(visible, jnp.exp(jnp.where(visible, scores, 0.0)), 0.0)
        grad = grad_ref[s]
        probs_grad = dot(grad, value, 1, 1)
        inner = jnp.sum(probs * probs_grad, -1, keepdims=True)
        low = (probs * (probs_grad - inner)).astype(BF)
        out_ref[s, :part] = (dot(low, key, 1, 0) / root).astype(BF)
        key_back = dot(low, query, 0, 0)
        value_back = dot(probs.astype(BF), grad, 0, 0)
        if s == SPAN - 1:
            key_sum[...] = key_back
            value_sum[...] = value_back
        else:
            key_sum[:length] += key_back
            value_sum[:length] += value_back
    for s in range(SPAN):
        span = slice(s * count, (s + 1) * count)
        out_ref[s, part : part + count] = (key_sum[span] / root).astype(BF)
        out_ref[s, part + count :] = value_sum[span].astype(BF)


def attend_back(got, half, log_total, mix_grad, part, count):
    size = got.shape[2]
    vmem = pl.BlockSpec(memory_space=pltpu.VMEM)
    return pl.pallas_call(
        functools.partial(attend_back_kernel, part, count),
        in_specs=[pl.BlockSpec(memory_space=pltpu.SMEM), vmem, vmem, vmem],
        out_shape=jax.ShapeDtypeStruct((SPAN, part + 2 * count, size), BF),
        scratch_shapes=[pltpu.VMEM((SPAN * count, size), F32)] * 2,
        compiler_params=PARAMS,
        cost_estimate=cost(
            3 * SPAN * SPAN * part * count * size, 6 * got.size, SPAN * SPAN * part * count
        ),
    )(half, got, log_total, mix_grad)


def block_rows(place, r, own, part):
    block = r ^ place
    per_part = part // own
    return block // per_part, pl.multiple_of(block % per_part * own, own)


def project_out_kernel(own, place_ref, mix_ref, weight_ref, kept_ref, sent_ref):
    parts = SPAN * LANES // weight_ref.shape[0]
    part = mix_ref.shape[1]
    rows = []
    for r in range(4):
        p, start = block_rows(place_ref[0], r, own, part)
        rows.append(
            jnp.concatenate(
                [mix_ref[h + p, pl.ds(start, own), :] for h in range(0, SPAN, parts)], 1
            )
        )
    product = dot(jnp.concatenate(rows, 0), weight_ref[...], 1, 0).astype(BF)
    for r in range(4):
        ref = sent_ref if r % 2 else kept_ref
        ref[r // 2] = product[r * own : (r + 1) * own]


def project_out(mix, w_out, place, own, block=512):
    local, width = w_out.shape
    out = pl.BlockSpec((2, own, block), lambda d, *_: (0, 0, d))
    shape = jax.ShapeDtypeStruct((2, own, width), BF)
    return pl.pallas_call(
        functools.partial(project_out_kernel, own),
        grid_spec=pltpu.PrefetchScalarGridSpec(
            num_scalar_prefetch=1,
            grid=(width // block,),
            in_specs=[resident(mix.shape), pl.BlockSpec((local, block), lambda d, *_: (0, d))],
            out_specs=[out, out],
        ),
        out_shape=[shape, shape],
        compiler_params=PARAMS,
        cost_estimate=cost(4 * own * local * width, local * width * 3),
    )(place, mix, w_out)


def middle_kernel(experts, place_ref, tokens_ref, kept_ref, core_ref, side_ref, *refs):
    gain_ref, router_ref, routes_ref, resid_ref, probs_ref, chosen_ref = refs[:6]
    row_refs = refs[6:]
    width = tokens_ref.shape[1]
    state = tokens_ref[...].astype(F32) + kept_ref[0].astype(F32)
    state = state + core_ref[0].astype(F32) + side_ref[...].astype(F32)
    resid_ref[...] = state
    scale = lax.rsqrt(jnp.mean(state * state, -1, keepdims=True) + EPSILON)
    normed = (state * scale * gain_ref[...]).astype(BF)
    logits = dot(normed, router_ref[...], 1, 0)
    lane = lax.broadcasted_iota(jnp.int32, logits.shape, 1)
    real = lane < experts
    top = jnp.max(jnp.where(real, logits, NEGATIVE), -1, keepdims=True)
    powers = jnp.exp(jnp.minimum(logits - top, 0.0))
    total = jnp.sum(jnp.where(real, powers, 0.0), -1, keepdims=True)
    probs = powers / total
    routes = routes_ref[...]
    chosen = jnp.zeros(logits.shape, F32)
    for k in range(routes.shape[1]):
        column = routes[:, k : k + 1]
        hit = (lane == column) | (lane == column + experts)
        chosen = jnp.where(hit, 1.0, chosen)
    probs_ref[...] = jnp.where(real, probs, 0.0)
    chosen_ref[...] = jnp.where(real, chosen, 0.0)
    gates = probs * chosen
    high = gates.astype(BF).astype(F32)
    side = jnp.where(real, high, jnp.where(lane < 2 * experts, gates - high, 0.0))
    rows = jnp.concatenate([normed, side.astype(BF)], 1)
    begin = 0
    for ref in row_refs:
        ref[...] = rows[:, begin : begin + ref.shape[1]]
        begin += ref.shape[1]


def middle(tokens, kept, core, side, gain, router_wide, routes, place, experts, groups):
    own, width = side.shape
    wide = router_wide.shape[1]
    shape = jax.ShapeDtypeStruct
    return pl.pallas_call(
        functools.partial(middle_kernel, experts),
        grid_spec=pltpu.PrefetchScalarGridSpec(
            num_scalar_prefetch=1,
            grid=(1,),
            in_specs=[
                pl.BlockSpec((own, width), lambda i, place_ref: (place_ref[0], 0)),
                resident(kept.shape),
                resident(core.shape),
                resident(side.shape),
                resident((1, width)),
                resident(router_wide.shape),
                pl.BlockSpec((own, routes.shape[1]), lambda i, place_ref: (place_ref[0], 0)),
            ],
            out_specs=[
                resident((own, width)),
                resident((own, wide)),
                resident((own, wide)),
            ]
            + [resident((own, columns)) for columns in groups],
        ),
        out_shape=[
            shape((own, width), F32),
            shape((own, wide), F32),
            shape((own, wide), F32),
        ]
        + [shape((own, columns), BF) for columns in groups],
        compiler_params=PARAMS,
        cost_estimate=cost(own * width * wide, own * width * 20),
    )(place, tokens, kept, core, side, gain[None], router_wide, routes)


def middle_back_kernel(experts, place_ref, *refs):
    homes = refs[:6]
    resid_ref, probs_ref, chosen_ref, gain_ref, router_ref, cotangent_ref = refs[6:12]
    grad_ref, low_ref, small_ref = refs[12:]
    width = resid_ref.shape[1]
    parts = [a[...].astype(F32) + b[...].astype(F32) for a, b in zip(homes[:3], homes[3:])]
    home = jnp.concatenate(parts, 1)
    side = home[:, width:]
    lanes = side.shape[1]
    gate_grad = (side + pltpu.roll(side, lanes - experts, 1)) * chosen_ref[...]
    probs = probs_ref[...]
    inner = jnp.sum(probs * gate_grad, -1, keepdims=True)
    logit_low = (probs * (gate_grad - inner)).astype(BF)
    state = resid_ref[...]
    scale = lax.rsqrt(jnp.mean(state * state, -1, keepdims=True) + EPSILON)
    unit = state * scale
    mid_grad = home[:, :width] + dot(logit_low, router_ref[...], 1, 1)
    scaled = mid_grad * gain_ref[...]
    grad = cotangent_ref[...].astype(F32) + scale * (
        scaled - unit * jnp.mean(scaled * unit, -1, keepdims=True)
    )
    grad_ref[...] = grad
    low_ref[...] = grad.astype(BF)
    normed = (unit * gain_ref[...]).astype(BF)
    small_ref[:experts] = dot(logit_low, normed, 0, 0)[:experts]
    d_gain = jnp.sum(mid_grad * unit, 0, keepdims=True)
    row = lax.broadcasted_iota(jnp.int32, (8, width), 0)
    small_ref[experts:] = jnp.where(row == 0, d_gain, 0.0)


def middle_back(homes, resid, probs, chosen, gain, router_wide, cotangent, place, experts):
    own, width = resid.shape
    shape = jax.ShapeDtypeStruct
    arrays = list(homes) + [resid, probs, chosen, gain[None], router_wide]
    return pl.pallas_call(
        functools.partial(middle_back_kernel, experts),
        grid_spec=pltpu.PrefetchScalarGridSpec(
            num_scalar_prefetch=1,
            grid=(1,),
            in_specs=[resident(a.shape) for a in arrays]
            + [pl.BlockSpec((own, width), lambda i, place_ref: (place_ref[0], 0))],
            out_specs=[
                resident((own, width)),
                resident((own, width)),
                resident((experts + 8, width)),
            ],
        ),
        out_shape=[
            shape((own, width), F32),
            shape((own, width), BF),
            shape((experts + 8, width), F32),
        ],
        compiler_params=PARAMS,
        cost_estimate=cost(2 * own * width * LANES, own * width * 30),
    )(place, *arrays, cotangent)


def spread(block):
    side = swap(block, "tensor", 2)
    core = swap(block, "tensor", 1)
    return block, core, side, swap(side, "tensor", 1)


def mix_back_kernel(place_ref, *refs):
    blocks, weight_ref, out_ref = refs[:4], refs[4], refs[5]
    own = blocks[0].shape[0]
    part, size = out_ref.shape[1:]
    parts = SPAN * size // weight_ref.shape[0]
    lows = jnp.concatenate([ref[...] for ref in blocks], 0)
    product = dot(lows, weight_ref[...], 1, 1).astype(BF)
    for r in range(4):
        p, start = block_rows(place_ref[0], r, own, part)
        for h in range(SPAN // parts):
            out_ref[h * parts + p, pl.ds(start, own), :] = product[
                r * own : (r + 1) * own, h * size : (h + 1) * size
            ]


def mix_back(blocks, w_out, place, part, size):
    vmem = pl.BlockSpec(memory_space=pltpu.VMEM)
    local, width = w_out.shape
    return pl.pallas_call(
        mix_back_kernel,
        in_specs=[pl.BlockSpec(memory_space=pltpu.SMEM)] + [vmem] * 5,
        out_shape=jax.ShapeDtypeStruct((SPAN, part, size), BF),
        compiler_params=PARAMS,
        cost_estimate=cost(4 * blocks[0].shape[0] * local * width, local * width * 4),
    )(place, *blocks, w_out)


def out_grad_kernel(place_ref, *refs):
    blocks, mix_ref, out_ref = refs[:4], refs[4], refs[5]
    own = blocks[0].shape[0]
    heads_parts, part, size = mix_ref.shape
    lows = jnp.concatenate([ref[...] for ref in blocks], 0)
    parts = 4 * own // part
    pieces = []
    for h in range(heads_parts // parts):
        rows = []
        for r in range(4):
            p, start = block_rows(place_ref[0], r, own, part)
            rows.append(mix_ref[h * parts + p, pl.ds(start, own), :])
        pieces.append(dot(jnp.concatenate(rows, 0), lows, 0, 0).astype(BF))
    if len(out_ref.shape) == 2:
        out_ref[...] = jnp.concatenate(pieces, 0)
        return
    rows, wide = out_ref.shape[1:]
    block = lows.shape[1]
    product = jnp.concatenate(pieces, 0)
    for q in range(wide // block):
        out_ref[0, :, q * block : (q + 1) * block] = product[q * rows : (q + 1) * rows]


def out_weight_grad(blocks, mix, place, local, owners):
    own, width = blocks[0].shape
    block = width // owners
    if block % LANES == 0:
        rows = local // owners
        out = pl.BlockSpec((1, rows, width), lambda d, *_: (d, 0, 0))
        shape = jax.ShapeDtypeStruct((owners, rows, width), BF)
    else:
        block = 4 * LANES
        out = pl.BlockSpec((local, block), lambda d, *_: (0, d))
        shape = jax.ShapeDtypeStruct((local, width), BF)
    column = pl.BlockSpec((own, block), lambda d, *_: (0, d))
    return pl.pallas_call(
        out_grad_kernel,
        grid_spec=pltpu.PrefetchScalarGridSpec(
            num_scalar_prefetch=1,
            grid=(width // block,),
            in_specs=[column] * 4 + [resident(mix.shape)],
            out_specs=out,
        ),
        out_shape=shape,
        compiler_params=PARAMS,
        cost_estimate=cost(4 * own * local * width, local * width * 3),
    )(place, *blocks, mix)


def unturn_kernel(full_width, back_ref, query_ref, key_ref, sums_ref, *refs):
    query_gain_ref, key_gain_ref, cos_ref, sin_ref = refs[:4]
    query_out_ref, key_out_ref, value_out_ref, inner_ref, gains_ref = refs[4:]
    heads, size = query_gain_ref.shape
    parts = SPAN // heads
    count = cos_ref.shape[0]
    part = count // parts
    scales = scales_of(sums_ref[...], full_width)
    inner = [0.0, 0.0]
    for h in range(heads):
        span = slice(h * size, (h + 1) * size)
        first = h * parts
        query = jnp.concatenate([back_ref[first + p, :part] for p in range(parts)], 0)
        key = sum(back_ref[first + p, part : part + count].astype(F32) for p in range(parts))
        value = sum(back_ref[first + p, part + count :].astype(F32) for p in range(parts))
        value_out_ref[:, span] = value.astype(BF)
        key = key.astype(BF)
        items = ((query, query_ref, query_gain_ref, query_out_ref), (key, key_ref, key_gain_ref, key_out_ref))
        for n, (grad, raw_ref, gain_ref, out_ref) in enumerate(items):
            grad = grad.astype(F32)
            gain_in = grad * cos_ref[...] - pltpu.roll(grad, size // 2, 1) * sin_ref[...]
            unit = raw_ref[:, span] * scales[:, n : n + 1]
            gains_ref[n * heads + h] = jnp.broadcast_to(
                jnp.sum(gain_in * unit, 0, keepdims=True), (8, size)
            )
            scaled = gain_in * gain_ref[pl.ds(h, 1), :]
            out_ref[:, span] = scaled
            inner[n] = inner[n] + scaled * unit
    inner_ref[...] = two_rows(inner[0], inner[1])


def unturn(back, query, key, sums, query_gain, key_gain, cos, sin, full_width):
    count, local = query.shape
    heads, size = query_gain.shape
    shape = jax.ShapeDtypeStruct
    return pl.pallas_call(
        functools.partial(unturn_kernel, full_width),
        out_shape=[
            shape((count, local), F32),
            shape((count, local), F32),
            shape((count, local), BF),
            shape((8, count), F32),
            shape((2 * heads, 8, size), F32),
        ],
        compiler_params=PARAMS,
        cost_estimate=cost(0, 24 * query.size),
    )(back, query, key, sums, query_gain, key_gain, cos, sin)


def columns_kernel(full_width, *refs):
    query_scaled_ref, key_scaled_ref, value_ref, query_ref, key_ref, sums_ref, inner_ref = refs[:7]
    query_low_ref, key_low_ref, out_ref = refs[7:]
    owners, rows, _ = out_ref.shape
    rows = rows // 3
    scales = scales_of(sums_ref[...], full_width)
    means = inner_ref[...].T / full_width
    items = ((query_scaled_ref, query_ref, query_low_ref), (key_scaled_ref, key_ref, key_low_ref))
    lows = []
    for n, (scaled_ref, raw_ref, low_ref) in enumerate(items):
        scale = scales[:, n : n + 1]
        unit = raw_ref[...] * scale
        low = (scale * (scaled_ref[...] - unit * means[:, n : n + 1])).astype(BF)
        low_ref[...] = low
        lows.append(low)
    for n, low in enumerate(lows + [value_ref[...]]):
        turned = low.T
        for d in range(owners):
            out_ref[d, n * rows : (n + 1) * rows] = turned[d * rows : (d + 1) * rows]


def columns_of(query_scaled, key_scaled, value, query, key, sums, inner, full_width, owners):
    count, local = query.shape
    low = jax.ShapeDtypeStruct((count, local), BF)
    return pl.pallas_call(
        functools.partial(columns_kernel, full_width),
        out_shape=[low, low, jax.ShapeDtypeStruct((owners, 3 * local // owners, count), BF)],
        compiler_params=PARAMS,
        cost_estimate=cost(0, 24 * query.size),
    )(query_scaled, key_scaled, value, query, key, sums, inner)


def input_kernel(own, place_ref, *refs):
    lows, weights, kept_ref, sent_ref = refs[:3], refs[3:6], refs[6], refs[7]
    place = place_ref[0]
    total = None
    for low_ref, weight_ref in zip(lows, weights):
        rows = [
            low_ref[pl.ds(pl.multiple_of((r ^ place) * own, own), own), :] for r in range(4)
        ]
        product = dot(jnp.concatenate(rows, 0), weight_ref[...], 1, 1)
        total = product if total is None else total + product
    total = total.astype(BF)
    for r in range(4):
        ref = sent_ref if r % 2 else kept_ref
        ref[r // 2] = total[r * own : (r + 1) * own]


def input_back(lows, weights, place, own, block=512):
    width, local = weights[0].shape
    out = pl.BlockSpec((2, own, block), lambda d, *_: (0, 0, d))
    shape = jax.ShapeDtypeStruct((2, own, width), BF)
    return pl.pallas_call(
        functools.partial(input_kernel, own),
        grid_spec=pltpu.PrefetchScalarGridSpec(
            num_scalar_prefetch=1,
            grid=(width // block,),
            in_specs=[resident(lows[0].shape)] * 3
            + [pl.BlockSpec((block, local), lambda d, *_: (d, 0))] * 3,
            out_specs=[out, out],
        ),
        out_shape=[shape, shape],
        compiler_params=PARAMS,
        cost_estimate=cost(12 * own * local * width, local * width * 7),
    )(place, *lows, *weights)


def last_kernel(place_ref, tokens_ref, *refs):
    kept_ref, core_ref, side_ref, grad_ref, gain_ref, small_ref, out_ref = refs
    own = grad_ref.shape[0]
    extra = out_ref.shape[0] - own
    used = small_ref.shape[0]
    state = tokens_ref[...].astype(F32)
    scale = lax.rsqrt(jnp.mean(state * state, -1, keepdims=True) + EPSILON)
    unit = state * scale
    grad = kept_ref[0].astype(F32) + core_ref[0].astype(F32) + side_ref[...].astype(F32)
    scaled = grad * gain_ref[...]
    out = grad_ref[...] + scale * (scaled - unit * jnp.mean(scaled * unit, -1, keepdims=True))
    out_ref[:own] = out.astype(BF)
    d_gain = jnp.sum(grad * unit, 0, keepdims=True)
    row = lax.broadcasted_iota(jnp.int32, (8, state.shape[1]), 0)
    gains = small_ref[used - 8 :] + jnp.where(row == 1, d_gain, 0.0)
    rows = [small_ref[: used - 8], gains]
    if extra > used:
        rows.append(jnp.zeros((extra - used, state.shape[1]), F32))
    out_ref[own:] = jnp.concatenate(rows, 0).astype(BF)


def last(tokens, kept, core, side, grad, gain, small, place):
    own, width = side.shape
    arrays = [kept, core, side, grad, gain[None], small]
    rows = own + -(-small.shape[0] // 16) * 16
    return pl.pallas_call(
        last_kernel,
        grid_spec=pltpu.PrefetchScalarGridSpec(
            num_scalar_prefetch=1,
            grid=(1,),
            in_specs=[pl.BlockSpec((own, width), lambda i, place_ref: (place_ref[0], 0))]
            + [resident(a.shape) for a in arrays],
            out_specs=resident((rows, width)),
        ),
        out_shape=jax.ShapeDtypeStruct((rows, width), BF),
        compiler_params=PARAMS,
        cost_estimate=cost(0, own),
    )(place, tokens, *arrays)


def join_kernel(own, place_ref, *refs):
    out_ref = refs[4]
    for r in range(4):
        start = pl.multiple_of((r ^ place_ref[0]) * own, own)
        out_ref[pl.ds(start, own), :] = refs[r][:own].astype(out_ref.dtype)


def join_blocks(blocks, place, own, kind):
    width = blocks[0].shape[1]
    vmem = pl.BlockSpec(memory_space=pltpu.VMEM)
    return pl.pallas_call(
        functools.partial(join_kernel, own),
        in_specs=[pl.BlockSpec(memory_space=pltpu.SMEM)] + [vmem] * 4,
        out_shape=jax.ShapeDtypeStruct((4 * own, width), kind),
        compiler_params=PARAMS,
        cost_estimate=cost(0, own),
    )(place, *blocks)


def weights_kernel(columns_ref, rows_ref, small_ref, out_ref):
    owners, columns, count = columns_ref.shape
    total = None
    for s in range(owners):
        product = dot(columns_ref[s], rows_ref[pl.ds(s * count, count), :], 1, 0)
        total = product if total is None else total + product
    out_ref[0, :columns] = total.astype(BF)
    out_ref[0, columns:] = small_ref[0]


def weight_columns(columns, rows, small):
    owners, count3, count = columns.shape
    width = rows.shape[1]
    slab = width // owners
    extra = small.shape[1]
    return pl.pallas_call(
        weights_kernel,
        grid=(owners,),
        in_specs=[
            resident(columns.shape),
            pl.BlockSpec((rows.shape[0], slab), lambda d: (0, d)),
            pl.BlockSpec((1, extra, slab), lambda d: (d, 0, 0)),
        ],
        out_specs=pl.BlockSpec((1, count3 + extra, slab), lambda d: (d, 0, 0)),
        out_shape=jax.ShapeDtypeStruct((owners, count3 + extra, slab), BF),
        compiler_params=PARAMS,
        cost_estimate=cost(rows.shape[0] * width * count3, rows.size * 2),
    )(columns, rows, small)


def per_device(
    tokens,
    segment_ids,
    routes,
    norm1_gain,
    w_query,
    w_key,
    w_value,
    query_gain,
    key_gain,
    w_out,
    norm2_gain,
    w_router,
    w_gate,
    w_up,
    w_down,
    cotangent,
):
    tok_count, model_width = tokens.shape
    heads_here, head_size = query_gain.shape
    local_width = heads_here * head_size
    tensor_count = lax.axis_size("tensor")
    full_width = local_width * tensor_count
    experts = w_router.shape[1]
    owners = lax.axis_size("dp")
    dp_place = lax.axis_index("dp")
    tensor_place = lax.axis_index("tensor")
    own = tok_count // tensor_count
    parts = SPAN // heads_here
    part = tok_count // parts
    groups = [list(range(g, g + SPAN)) for g in range(0, owners, SPAN)]
    place = tensor_place.astype(jnp.int32).reshape(1)
    index = jnp.stack([dp_place, tensor_place]).astype(jnp.int32)
    half = (dp_place % SPAN % parts).astype(jnp.int32).reshape(1)

    def mine(array):
        return lax.dynamic_slice_in_dim(array, tensor_place * own, own, 0)

    def trade(array):
        return lax.all_to_all(
            array, "dp", split_axis=0, concat_axis=0, tiled=True, axis_index_groups=groups
        )

    def sum_tensor(kept, sent):
        core = swap(sent, "tensor", 1)
        given = (kept[1].astype(F32) + core[1].astype(F32)).astype(BF)
        return kept, core, swap(given, "tensor", 2)

    out_grad_all = lax.all_gather(mine(cotangent), EVERY, axis=0, tiled=True)
    both_turned, down_turned = turn_weights(w_gate, w_up, w_down)
    side_width = -(-2 * experts // LANES) * LANES
    router_wide = jnp.pad(
        jnp.concatenate([w_router, w_router], 1), ((0, 0), (0, side_width - 2 * experts))
    )
    local_pos = jnp.arange(tok_count, dtype=jnp.int32)
    positions = (dp_place % SPAN * tok_count + local_pos).astype(F32)
    cos_table, sin_table = rope_tables(positions, head_size)
    segment_rows = jnp.pad(
        segment_ids.astype(BF).reshape(-1, head_size), ((0, 16 - tok_count // head_size), (0, 0))
    )

    normed_in, query_raw, key_raw, value_att, squares = project(
        tokens, norm1_gain, w_query, w_key, w_value
    )
    squares = lax.psum(squares, "tensor")
    packed = pack_heads(
        query_raw,
        key_raw,
        value_att,
        squares,
        query_gain,
        key_gain,
        cos_table,
        sin_table,
        segment_rows,
        full_width,
    )
    got, both_turned, down_turned = lax.optimization_barrier(
        (trade(packed), both_turned, down_turned)
    )
    mix_heads, log_total = attend(got, half, part, tok_count)
    mix = trade(mix_heads)
    kept, core, side = sum_tensor(*project_out(mix, w_out, place, own))
    lanes = -(-(model_width + side_width) // (3 * LANES)) * LANES
    resid_state, router_probs, chosen, *rows_own = middle(
        tokens,
        kept,
        core,
        side,
        norm2_gain,
        router_wide,
        routes,
        place,
        experts,
        [lanes, lanes, model_width + side_width - 2 * lanes],
    )
    bits = owners.bit_length() - 1
    first_three = [("tensor", 2), ("dp", 1), ("dp", 2)]
    rest = [("dp", 1 << b) for b in range(2, bits)]
    orders = [first_three[g:] + first_three[:g] + rest for g in range(3)]
    pieces, names, back_all, tokens_own = gather_every(
        rows_own,
        [order[::-1] for order in orders],
        hidden_back(out_grad_all, down_turned),
        mine(tokens),
    )
    tokens_all = lax.all_gather(tokens_own, EVERY, axis=0, tiled=True)
    (rows_all, hid, hid_turned, glow, ulow), kept_groups, sent_groups = expert_rows(
        pieces, names, back_all, w_gate, w_up, both_turned, index, experts, tok_count
    )
    d_w_gate = over_rows(rows_all, glow, w_gate.shape)
    out_kept, out_sent = expert_out(hid, w_down, place % 2, tok_count)

    def add_core(kept_rows, sent_rows):
        core_rows = swap(sent_rows, "tensor", 1)
        return ((kept_rows.astype(F32) + core_rows.astype(F32)).astype(BF),)

    homes, d_w_gate, out_part = sum_every(
        kept_groups, sent_groups, orders, (d_w_gate, out_kept, out_sent), add_core
    )
    core_groups = [
        [d * tensor_count + x * 2 + c for d in range(owners) for x in range(2)] for c in range(2)
    ]
    expert_full = lax.psum_scatter(
        out_part.reshape(-1, model_width),
        EVERY,
        scatter_dimension=0,
        tiled=True,
        axis_index_groups=core_groups,
    )
    d_w_down = turned_rows(hid_turned, out_grad_all).reshape(w_down.shape)
    d_w_up = over_rows(rows_all, ulow, w_up.shape)
    normed_in_all = norm_all(tokens_all, norm1_gain, tok_count)

    resid_grad, resid_low, small = middle_back(
        [home[0] for home in homes] + [home[1] for home in homes],
        resid_state,
        router_probs,
        chosen,
        norm2_gain,
        router_wide,
        cotangent,
        place,
        experts,
    )
    resid_blocks = spread(resid_low)
    mix_grad = trade(mix_back(resid_blocks, w_out, place, part, head_size))
    d_out = out_weight_grad(resid_blocks, mix, place, local_width, owners)
    mix_grad, d_out = lax.optimization_barrier((mix_grad, d_out))
    back, d_w_down, d_w_up, normed_in_all = lax.optimization_barrier(
        (
            trade(attend_back(got, half, log_total, mix_grad, part, tok_count)),
            d_w_down,
            d_w_up,
            normed_in_all,
        )
    )
    d_out, expert_full = lax.optimization_barrier((d_out, expert_full))
    model_slice = model_width // owners
    if model_slice % LANES == 0:
        d_out = lax.psum_scatter(d_out, "dp", scatter_dimension=0, tiled=True)[0]
        d_out = d_out.reshape(own, owners, model_slice).transpose(1, 0, 2)
        d_out = d_out.reshape(local_width, model_slice).astype(F32)
    else:
        d_out = lax.psum_scatter(d_out, "dp", scatter_dimension=1, tiled=True).astype(F32)
    block_own = (resid_state + expert_full.astype(F32)).astype(BF)
    block_output = join_blocks(spread(block_own), place, own, BF)

    query_scaled, key_scaled, value_low, inner, gains = unturn(
        back, query_raw, key_raw, squares, query_gain, key_gain, cos_table, sin_table, full_width
    )
    inner = lax.psum(inner, "tensor")
    query_low, key_low, columns = columns_of(
        query_scaled, key_scaled, value_low, query_raw, key_raw, squares, inner, full_width, owners
    )
    columns = lax.all_to_all(columns, "dp", split_axis=0, concat_axis=0, tiled=True)
    kept, core, side = sum_tensor(
        *input_back(
            (query_low, key_low, value_low), (w_query, w_key, w_value), place, own
        )
    )
    input_blocks = spread(
        last(tokens, kept, core, side, resid_grad, norm1_gain, small, place)
    )
    input_grad = join_blocks(input_blocks, place, own, F32)

    head_slice = head_size // owners
    slice_width = local_width // owners
    gain_count = 2 * heads_here * head_slice
    gain_rows = -(-gain_count // model_slice)
    gains = gains[:, 0].reshape(2 * heads_here, owners, head_slice).transpose(1, 0, 2)
    gains = jnp.pad(
        gains.reshape(owners, gain_count), ((0, 0), (0, gain_rows * model_slice - gain_count))
    ).reshape(owners, gain_rows, model_slice)
    shared = sum(block[own : own + experts + 2].astype(F32) for block in input_blocks)
    shared = shared.reshape(experts + 2, owners, model_slice).transpose(1, 0, 2)
    extra = jnp.concatenate([shared, gains], 1).astype(BF)
    extra = jnp.pad(extra, ((0, 0), (0, -extra.shape[1] % 16), (0, 0)))
    if model_slice % LANES == 0:
        final = weight_columns(columns, normed_in_all, extra)
    else:
        columns = columns.transpose(1, 0, 2).reshape(3 * slice_width, owners * tok_count)
        final = dot(columns, normed_in_all, 1, 0).reshape(3 * slice_width, owners, model_slice)
        final = jnp.concatenate([final.transpose(1, 0, 2).astype(BF), extra], 1)
    final = lax.all_to_all(final, "dp", split_axis=0, concat_axis=0, tiled=True)
    weights = final[:, : 3 * slice_width].reshape(owners, 3, slice_width, model_slice)
    weights = weights.transpose(1, 3, 0, 2).reshape(3, model_slice, local_width).astype(F32)
    extra = jnp.sum(final[:, 3 * slice_width :].astype(F32), 0)
    gains = extra[experts + 2 : experts + 2 + gain_rows].reshape(-1)[:gain_count]
    gains = gains.reshape(2, heads_here, head_slice)

    return (
        block_output,
        input_grad,
        extra[experts + 1],
        weights[0],
        weights[1],
        weights[2],
        gains[0],
        gains[1],
        d_out,
        extra[experts],
        extra[:experts].T,
        d_w_gate,
        d_w_up,
        d_w_down,
    )


def solution(mesh):
    in_specs = (
        P("dp", None),
        P("dp"),
        P("dp", None),
        P(),
        P(None, "tensor"),
        P(None, "tensor"),
        P(None, "tensor"),
        P("tensor", None),
        P("tensor", None),
        P("tensor", None),
        P(),
        P(),
        P("dp", None, "tensor"),
        P("dp", None, "tensor"),
        P("dp", "tensor", None),
        P("dp", None),
    )
    out_specs = (
        P("dp", None),
        P("dp", None),
        P("dp"),
        P("dp", "tensor"),
        P("dp", "tensor"),
        P("dp", "tensor"),
        P("tensor", "dp"),
        P("tensor", "dp"),
        P("tensor", "dp"),
        P("dp"),
        P("dp", None),
        P("dp", None, "tensor"),
        P("dp", None, "tensor"),
        P("dp", "tensor", None),
    )
    return jax.shard_map(
        per_device, mesh=mesh, in_specs=in_specs, out_specs=out_specs, check_vma=False
    )
```

```python
import functools
import math

import jax
import jax.numpy as jnp
from jax import lax
from jax.experimental import pallas as pl
from jax.experimental.pallas import tpu as pltpu
from jax.sharding import PartitionSpec as P

SPAN = 8


EPSILON = 1e-05
ROPE_BASE = 10000.0
NEGATIVE = -1e30
BF = jnp.bfloat16
F32 = jnp.float32
EVERY = ("dp", "tensor")
VMEM_LIMIT = 56 * 1024 * 1024
LANES = 128


def rope_tables(positions, head_size):
    frequency = ROPE_BASE ** (-jnp.arange(0, head_size, 2, dtype=jnp.float32) / head_size)
    angles = positions[:, None] * frequency[None, :]
    cosine, sine = jnp.cos(angles), jnp.sin(angles)
    return jnp.concatenate([cosine, cosine], -1), jnp.concatenate([-sine, sine], -1)


def dot(left_side, right_side, left_dim, right_dim):
    return lax.dot_general(
        left_side,
        right_side,
        (((left_dim,), (right_dim,)), ((), ())),
        preferred_element_type=jnp.float32,
    )


def swap(array, axis, bit):
    count = lax.axis_size(axis)
    return lax.ppermute(array, axis, [(i, i ^ bit) for i in range(count)])


def resident(shape):
    return pl.BlockSpec(shape, lambda *_: (0,) * len(shape), pipeline_mode=pl.Buffered(1))


def cost(macs, size, transcendentals=0):
    return pl.CostEstimate(flops=2 * macs, bytes_accessed=size, transcendentals=transcendentals)


PARAMS = pltpu.CompilerParams(vmem_limit_bytes=VMEM_LIMIT)


def turn_kernel(gate_ref, up_ref, down_ref, both_ref, down_out_ref):
    count, _, hidden = gate_ref.shape
    for e in range(count):
        both_ref[pl.ds(e * hidden, hidden), :] = gate_ref[e].T
        both_ref[pl.ds((count + e) * hidden, hidden), :] = up_ref[e].T
        down_out_ref[:, pl.ds(e * hidden, hidden)] = down_ref[e].T


def turn_weights(w_gate, w_up, w_down, block=256):
    count, width, hidden = w_gate.shape
    mid = count * hidden
    rows = pl.BlockSpec((count, block, hidden), lambda d: (0, d, 0))
    return pl.pallas_call(
        turn_kernel,
        grid=(width // block,),
        in_specs=[rows, rows, pl.BlockSpec((count, hidden, block), lambda d: (0, 0, d))],
        out_specs=[
            pl.BlockSpec((2 * mid, block), lambda d: (0, d)),
            pl.BlockSpec((block, mid), lambda d: (d, 0)),
        ],
        out_shape=[
            jax.ShapeDtypeStruct((2 * mid, width), BF),
            jax.ShapeDtypeStruct((width, mid), BF),
        ],
        compiler_params=PARAMS,
        cost_estimate=cost(0, 12 * mid * width),
    )(w_gate, w_up, w_down)


def hidden_back_kernel(grad_ref, down_ref, out_ref):
    out_ref[...] = dot(grad_ref[...], down_ref[...], 1, 0)


def hidden_back(grad_all, down_turned, block=256):
    width, mid = down_turned.shape
    total = grad_all.shape[0]
    return pl.pallas_call(
        hidden_back_kernel,
        grid=(total // block,),
        in_specs=[pl.BlockSpec((block, width), lambda i: (i, 0)), resident(down_turned.shape)],
        out_specs=pl.BlockSpec((block, mid), lambda i: (i, 0)),
        out_shape=jax.ShapeDtypeStruct((total, mid), F32),
        compiler_params=PARAMS,
        cost_estimate=cost(total * width * mid, total * width * 3),
    )(grad_all, down_turned)


def expert_kernel(experts, axes, index_ref, *refs):
    pieces, refs = (refs[:3], refs[3:6]), refs[6:]
    back_ref, gate_ref, up_ref, both_ref, rows_ref = refs[:5]
    hid_ref, hid_turned_ref, glow_ref, ulow_ref = refs[5:9]
    kept_refs, sent_refs, low_ref, side_ref = refs[9:12], refs[12:15], refs[15], refs[16]
    count, width, hidden_size = gate_ref.shape
    mid = count * hidden_size
    own = kept_refs[0].shape[2]
    starts = [pl.multiple_of((r ^ index_ref[1]) * own, own) for r in range(4)]
    for r in range(4):
        begin = 0
        for piece, axis in zip(pieces[r % 2], axes):
            place = [0] * (len(piece.shape) - 2)
            place[axis] = r // 2
            columns = piece.shape[-1]
            end = min(begin + columns, width)
            value = piece[tuple(place)]
            rows_ref[pl.ds(starts[r], own), begin:end] = value[:, : end - begin]
            if end - begin < columns:
                side_ref[pl.ds(starts[r], own), :] = value[:, end - begin :]
            begin = end
    rows = rows_ref[...]
    side = side_ref[...].astype(F32)
    lane = lax.broadcasted_iota(jnp.int32, side.shape, 1)
    dots = jnp.zeros(side.shape, F32)
    for e in range(count):
        column = index_ref[0] * count + e
        gate = jnp.sum(
            jnp.where((lane == column) | (lane == experts + column), side, 0.0), -1, keepdims=True
        )
        span = pl.ds(e * hidden_size, hidden_size)
        gate_pre = dot(rows, gate_ref[e], 1, 0)
        up_pre = dot(rows, up_ref[e], 1, 0)
        out_back = back_ref[:, span]
        sigma = 1.0 / (1.0 + jnp.exp(-gate_pre))
        silu = gate_pre * sigma
        hidden = silu * up_pre
        inner = jnp.sum(hidden * out_back, -1, keepdims=True)
        high = inner.astype(BF).astype(F32)
        dots = jnp.where(lane == column, high, dots)
        dots = jnp.where(lane == experts + column, inner - high, dots)
        hidden_low = (gate * hidden).astype(BF)
        hidden_grad = gate * out_back
        glow = (hidden_grad * up_pre * sigma * (1.0 + gate_pre * (1.0 - sigma))).astype(BF)
        ulow = (hidden_grad * silu).astype(BF)
        hid_ref[:, span] = hidden_low
        hid_turned_ref[span, :] = hidden_low.T
        glow_ref[:, span] = glow
        ulow_ref[:, span] = ulow
        low_ref[:, span] = glow
        low_ref[:, pl.ds(mid + e * hidden_size, hidden_size)] = ulow
    low_ref[:, 2 * mid :] = dots.astype(BF)
    low = jnp.concatenate([low_ref[pl.ds(start, own), :] for start in starts], 0)
    begin = 0
    for kept_ref, sent_ref in zip(kept_refs, sent_refs):
        columns = kept_ref.shape[3]
        end = min(begin + columns, width)
        back = dot(low[:, : 2 * mid], both_ref[:, begin:end], 1, 0).astype(BF)
        if end - begin < columns:
            back = jnp.concatenate([back, low[:, 2 * mid :]], 1)
        begin = end
        for r in range(4):
            ref = sent_ref if r % 2 else kept_ref
            ref[0, r // 2] = back[r * own : (r + 1) * own]


def expert_rows(pieces, names, back_all, w_gate, w_up, both_turned, index, experts, block):
    count, width, hidden = w_gate.shape
    total, mid = back_all.shape
    owners = total // block
    groups = [piece.shape[-1] for piece in pieces[0]]
    side = sum(groups) - width

    def rows(columns):
        return pl.BlockSpec((block, columns), lambda i, index_ref: (i ^ index_ref[0], 0))

    def shape(columns):
        return jax.ShapeDtypeStruct((total, columns), BF)

    def given(columns, order):
        sizes = tuple(1 if axis == "dp" else 2 for axis, _ in order)

        def place(i, *_):
            return tuple(i // bit % 2 if axis == "dp" else 0 for axis, bit in order) + (0, 0)

        return pl.BlockSpec(sizes + (block // 4, columns), place)

    def part(columns):
        return pl.BlockSpec((1, 2, block // 4, columns), lambda i, *_: (i, 0, 0, 0))

    def part_shape(columns):
        return jax.ShapeDtypeStruct((owners, 2, block // 4, columns), BF)

    given_specs = [given(columns, order) for columns, order in zip(groups, names)]
    axes = [[axis for axis, _ in order].index("tensor") for order in names]
    outs = pl.pallas_call(
        functools.partial(expert_kernel, experts, axes),
        grid_spec=pltpu.PrefetchScalarGridSpec(
            num_scalar_prefetch=1,
            grid=(owners,),
            in_specs=given_specs * 2
            + [
                rows(mid),
                resident(w_gate.shape),
                resident(w_up.shape),
                resident(both_turned.shape),
            ],
            out_specs=[
                rows(width),
                rows(mid),
                pl.BlockSpec((mid, block), lambda i, index_ref: (0, i ^ index_ref[0])),
                rows(mid),
                rows(mid),
            ]
            + [part(columns) for columns in groups] * 2,
            scratch_shapes=[pltpu.VMEM((block, 2 * mid + side), BF), pltpu.VMEM((block, side), BF)],
        ),
        out_shape=[
            shape(width),
            shape(mid),
            jax.ShapeDtypeStruct((mid, total), BF),
            shape(mid),
            shape(mid),
        ]
        + [part_shape(columns) for columns in groups] * 2,
        compiler_params=PARAMS,
        cost_estimate=cost(4 * total * width * mid, total * width * 8, total * mid),
    )(index, *pieces[0], *pieces[1], back_all, w_gate, w_up, both_turned)
    return outs[:5], outs[5:8], outs[8:]


def gather_every(groups, orders, beside, later):
    totals, names = list(groups), [[] for _ in groups]
    for step in range(len(orders[0])):
        if step == len(orders[0]) - 1:
            totals, later = lax.optimization_barrier((totals, later))
        others = [swap(total, *order[step]) for total, order in zip(totals, orders)]
        if step == len(orders[0]) - 1:
            others, beside = lax.optimization_barrier((others, beside))
        totals = [jnp.stack([total, other]) for total, other in zip(totals, others)]
        for name, order in zip(names, orders):
            name.insert(0, order[step])
    return (totals, [swap(total, "tensor", 1) for total in totals]), names, beside, later


def sum_every(kept, sent, orders, beside, finish):
    bits = lax.axis_size("dp").bit_length() - 1
    totals, names = [], []
    for kept_group, sent_group in zip(kept, sent):
        own, columns = kept_group.shape[2:]
        total = kept_group.astype(F32) + swap(sent_group, "tensor", 1).astype(F32)
        totals.append(total.astype(BF).reshape((2,) * (bits + 1) + (own, columns)))
        names.append([("dp", 1 << (bits - 1 - i)) for i in range(bits)] + [("tensor", 2)])
    for step in range(bits + 1):
        if step == 2:
            totals, beside = lax.optimization_barrier((totals, finish(*beside)))
        halves, others = [], []
        for total, left, order in zip(totals, names, orders):
            axis = left.index(order[step])
            left.pop(axis)
            given = lax.index_in_dim(total, 1, axis, keepdims=False)
            halves.append(lax.index_in_dim(total, 0, axis, keepdims=False))
            others.append(swap(given, *order[step]))
        if step == 0:
            others, beside = lax.optimization_barrier((others, beside))
        totals = [(a.astype(F32) + b.astype(F32)).astype(BF) for a, b in zip(halves, others)]
    return list(zip(halves, others)), *beside


def out_kernel(core_ref, hid_ref, down_ref, kept_ref, sent_ref):
    count, hidden, _ = down_ref.shape
    own = kept_ref.shape[1]
    rows = []
    for r in range(4):
        start = pl.multiple_of((r // 2 * 2 + ((r % 2) ^ core_ref[0])) * own, own)
        rows.append(hid_ref[pl.ds(start, own), :])
    weight = down_ref[...].reshape(count * hidden, -1)
    out = dot(jnp.concatenate(rows, 0), weight, 1, 0).astype(BF)
    for r in range(4):
        ref = sent_ref if r % 2 else kept_ref
        ref[r // 2] = out[r * own : (r + 1) * own]


def expert_out(hid, w_down, core, block):
    count, hidden, width = w_down.shape
    total = hid.shape[0]
    out = pl.BlockSpec((2, block // 4, width), lambda i, *_: (i, 0, 0))
    shape = jax.ShapeDtypeStruct((total // block * 2, block // 4, width), BF)
    return pl.pallas_call(
        out_kernel,
        grid_spec=pltpu.PrefetchScalarGridSpec(
            num_scalar_prefetch=1,
            grid=(total // block,),
            in_specs=[
                pl.BlockSpec((block, count * hidden), lambda i, *_: (i, 0)),
                resident(w_down.shape),
            ],
            out_specs=[out, out],
        ),
        out_shape=[shape, shape],
        compiler_params=PARAMS,
        cost_estimate=cost(total * width * count * hidden, total * width * 3),
    )(core, hid, w_down)


def over_kernel(left_ref, right_ref, out_ref):
    count, _, hidden = out_ref.shape
    product = dot(left_ref[...], right_ref[...], 0, 0)

    @pl.when(pl.program_id(1) == 0)
    def _():
        for e in range(count):
            out_ref[e] = product[:, e * hidden : (e + 1) * hidden]

    @pl.when(pl.program_id(1) > 0)
    def _():
        for e in range(count):
            out_ref[e] += product[:, e * hidden : (e + 1) * hidden]


def over_rows(rows, low, shape, block=256, chunk=2048):
    count, width, hidden = shape
    total = rows.shape[0]
    chunk = min(chunk, total)
    return pl.pallas_call(
        over_kernel,
        grid=(width // block, total // chunk),
        in_specs=[
            pl.BlockSpec((chunk, block), lambda d, k: (k, d)),
            pl.BlockSpec((chunk, count * hidden), lambda d, k: (k, 0)),
        ],
        out_specs=pl.BlockSpec((count, block, hidden), lambda d, k: (0, d, 0)),
        out_shape=jax.ShapeDtypeStruct(shape, F32),
        compiler_params=PARAMS,
        cost_estimate=cost(total * width * count * hidden, total * width * 4),
    )(rows, low)


def turned_kernel(left_ref, right_ref, out_ref):
    product = dot(left_ref[...], right_ref[...], 1, 0)

    @pl.when(pl.program_id(1) == 0)
    def _():
        out_ref[...] = product

    @pl.when(pl.program_id(1) > 0)
    def _():
        out_ref[...] += product


def turned_rows(left, right, block=256, chunk=2048):
    mid, total = left.shape
    width = right.shape[1]
    chunk = min(chunk, total)
    return pl.pallas_call(
        turned_kernel,
        grid=(width // block, total // chunk),
        in_specs=[
            pl.BlockSpec((mid, chunk), lambda d, k: (0, k)),
            pl.BlockSpec((chunk, block), lambda d, k: (k, d)),
        ],
        out_specs=pl.BlockSpec((mid, block), lambda d, k: (0, d)),
        out_shape=jax.ShapeDtypeStruct((mid, width), F32),
        compiler_params=PARAMS,
        cost_estimate=cost(total * width * mid, total * width * 4),
    )(left, right)


def front_kernel(tokens_ref, gain_ref, query_ref, key_ref, value_ref, *outs):
    normed_ref, query_out_ref, key_out_ref, value_out_ref, squares_ref = outs

    @pl.when(pl.program_id(0) == 0)
    def _():
        state = tokens_ref[...].astype(F32)
        scale = lax.rsqrt(jnp.mean(state * state, -1, keepdims=True) + EPSILON)
        normed_ref[...] = (state * scale * gain_ref[...]).astype(BF)
        squares_ref[...] = jnp.zeros_like(squares_ref)

    normed = normed_ref[...]
    query = dot(normed, query_ref[...], 1, 0)
    key = dot(normed, key_ref[...], 1, 0)
    query_out_ref[...] = query
    key_out_ref[...] = key
    value_out_ref[...] = dot(normed, value_ref[...], 1, 0).astype(BF)
    squares_ref[...] += two_rows(query * query, key * key)


def row_sums(array):
    ones = jnp.ones((8, array.shape[1]), F32)
    return lax.dot_general(
        ones,
        array,
        (((1,), (1,)), ((), ())),
        precision=lax.Precision.HIGHEST,
        preferred_element_type=F32,
    )


def two_rows(first, second):
    row = lax.broadcasted_iota(jnp.int32, (8, first.shape[0]), 0)
    return jnp.where(row == 0, row_sums(first), jnp.where(row == 1, row_sums(second), 0.0))


def norm_kernel(tokens_ref, gain_ref, out_ref):
    state = tokens_ref[...].astype(F32)
    scale = lax.rsqrt(jnp.mean(state * state, -1, keepdims=True) + EPSILON)
    out_ref[...] = (state * scale * gain_ref[...]).astype(BF)


def norm_all(tokens, gain, block):
    total, width = tokens.shape
    return pl.pallas_call(
        norm_kernel,
        grid=(total // block,),
        in_specs=[pl.BlockSpec((block, width), lambda i: (i, 0)), resident((1, width))],
        out_specs=pl.BlockSpec((block, width), lambda i: (i, 0)),
        out_shape=jax.ShapeDtypeStruct((total, width), BF),
        compiler_params=PARAMS,
        cost_estimate=cost(0, total * width * 4),
    )(tokens, gain[None])


def project(tokens, gain, w_query, w_key, w_value, block=256):
    count, width = tokens.shape
    local = w_query.shape[1]
    weight = pl.BlockSpec((width, block), lambda i: (0, i))
    out = pl.BlockSpec((count, block), lambda i: (0, i))
    return pl.pallas_call(
        front_kernel,
        grid=(local // block,),
        in_specs=[resident(tokens.shape), resident((1, width)), weight, weight, weight],
        out_specs=[resident((count, width)), out, out, out, resident((8, count))],
        out_shape=[
            jax.ShapeDtypeStruct((count, width), BF),
            jax.ShapeDtypeStruct((count, local), F32),
            jax.ShapeDtypeStruct((count, local), F32),
            jax.ShapeDtypeStruct((count, local), BF),
            jax.ShapeDtypeStruct((8, count), F32),
        ],
        compiler_params=PARAMS,
        cost_estimate=cost(3 * count * width * local, 6 * width * local),
    )(tokens, gain[None], w_query, w_key, w_value)


def scales_of(sums, full_width):
    return lax.rsqrt(sums.T / full_width + EPSILON)


def pack_kernel(full_width, query_ref, key_ref, value_ref, sums_ref, *refs):
    query_gain_ref, key_gain_ref, cos_ref, sin_ref, segment_ref, out_ref = refs
    parts, heads = out_ref.shape[0] // query_gain_ref.shape[0], query_gain_ref.shape[0]
    size = cos_ref.shape[1]
    count = cos_ref.shape[0]
    part = count // parts
    piece = part // 4
    scales = scales_of(sums_ref[...], full_width)
    for h in range(heads):
        span = slice(h * size, (h + 1) * size)

        def turned(ref, column, gain_ref):
            unit = ref[:, span] * scales[:, column : column + 1]
            vector = unit * gain_ref[pl.ds(h, 1), :]
            rolled = pltpu.roll(vector, size // 2, 1)
            return (vector * cos_ref[...] + rolled * sin_ref[...]).astype(BF)

        query = turned(query_ref, 0, query_gain_ref)
        key = turned(key_ref, 1, key_gain_ref)
        value = value_ref[:, span]
        for p in range(parts):
            place = h * parts + p
            for t in range(4):
                start = (t * parts + p) * piece
                out_ref[place, t * piece : (t + 1) * piece] = query[start : start + piece]
            out_ref[place, part : part + count] = key
            out_ref[place, part + count : part + 2 * count] = value
            out_ref[place, part + 2 * count :] = segment_ref[p]


def pack_heads(query, key, value, sums, query_gain, key_gain, cos, sin, segments, full_width):
    count = query.shape[0]
    size = cos.shape[1]
    parts = SPAN // query_gain.shape[0]
    return pl.pallas_call(
        functools.partial(pack_kernel, full_width),
        out_shape=jax.ShapeDtypeStruct(
            (SPAN, count // parts + 2 * count + segments.shape[1], size), BF
        ),
        compiler_params=PARAMS,
        cost_estimate=cost(0, 12 * query.size),
    )(query, key, value, sums, query_gain, key_gain, cos, sin, segments)


def head_views(got_ref, s, part, count):
    length = (s + 1) * count
    size = got_ref.shape[2]
    query = got_ref[s, :part]
    key = got_ref[: s + 1, part : part + count].reshape(length, size)
    value = got_ref[: s + 1, part + count : part + 2 * count].reshape(length, size)
    return query, key, value


def visible_pairs(got_ref, half, s, part, count):
    size = got_ref.shape[2]
    per_block = count // size
    first = part + 2 * count

    def rows(block):
        return got_ref[block, first : first + 16].astype(F32)

    own = jnp.broadcast_to(rows(s)[per_block : per_block + 1], (size, size)).T
    pieces = []
    for block in range(s + 1):
        values = rows(block)
        for r in range(per_block):
            pieces.append(own == values[r : r + 1])
    pieces = [jnp.where(piece, 1.0, 0.0) for piece in pieces]
    same = jnp.concatenate(pieces, 1) > 0.5
    query = lax.broadcasted_iota(jnp.int32, same.shape, 0)
    piece = part // 4
    query_pos = s * count + query // piece * (count // 4) + half * piece + query % piece
    return same & (lax.broadcasted_iota(jnp.int32, same.shape, 1) <= query_pos)


def attend_kernel(part, count, half_ref, got_ref, mix_ref, log_ref):
    half = half_ref[0]
    size = got_ref.shape[2]
    for s in range(SPAN):
        query, key, value = head_views(got_ref, s, part, count)
        visible = visible_pairs(got_ref, half, s, part, count)
        scores = jnp.where(visible, dot(query, key, 1, 1) / math.sqrt(size), NEGATIVE)
        top = jnp.max(scores, -1, keepdims=True)
        weights = jnp.where(visible, jnp.exp(scores - top), 0.0)
        total = jnp.sum(weights, -1, keepdims=True)
        mix_ref[s] = dot((weights / total).astype(BF), value, 1, 0).astype(BF)
        log_ref[s] = jnp.broadcast_to(top + jnp.log(total), (part, size))


def attend(got, half, part, count):
    size = got.shape[2]
    return pl.pallas_call(
        functools.partial(attend_kernel, part, count),
        in_specs=[
            pl.BlockSpec(memory_space=pltpu.SMEM),
            pl.BlockSpec(memory_space=pltpu.VMEM),
        ],
        out_shape=[
            jax.ShapeDtypeStruct((SPAN, part, size), BF),
            jax.ShapeDtypeStruct((SPAN, part, size), F32),
        ],
        compiler_params=PARAMS,
        cost_estimate=cost(SPAN * SPAN * part * count * size, 4 * got.size, SPAN * SPAN * part * count),
    )(half, got)


def attend_back_kernel(part, count, half_ref, got_ref, log_ref, grad_ref, out_ref, key_sum, value_sum):
    half = half_ref[0]
    size = got_ref.shape[2]
    root = math.sqrt(size)
    for s in reversed(range(SPAN)):
        length = (s + 1) * count
        query, key, value = head_views(got_ref, s, part, count)
        visible = visible_pairs(got_ref, half, s, part, count)
        scores = dot(query, key, 1, 1) / root - log_ref[s, :, :1]
        probs = jnp.where(visible, jnp.exp(jnp.where(visible, scores, 0.0)), 0.0)
        grad = grad_ref[s]
        probs_grad = dot(grad, value, 1, 1)
        inner = jnp.sum(probs * probs_grad, -1, keepdims=True)
        low = (probs * (probs_grad - inner)).astype(BF)
        out_ref[s, :part] = (dot(low, key, 1, 0) / root).astype(BF)
        key_back = dot(low, query, 0, 0)
        value_back = dot(probs.astype(BF), grad, 0, 0)
        if s == SPAN - 1:
            key_sum[...] = key_back
            value_sum[...] = value_back
        else:
            key_sum[:length] += key_back
            value_sum[:length] += value_back
    for s in range(SPAN):
        span = slice(s * count, (s + 1) * count)
        out_ref[s, part : part + count] = (key_sum[span] / root).astype(BF)
        out_ref[s, part + count :] = value_sum[span].astype(BF)


def attend_back(got, half, log_total, mix_grad, part, count):
    size = got.shape[2]
    vmem = pl.BlockSpec(memory_space=pltpu.VMEM)
    return pl.pallas_call(
        functools.partial(attend_back_kernel, part, count),
        in_specs=[pl.BlockSpec(memory_space=pltpu.SMEM), vmem, vmem, vmem],
        out_shape=jax.ShapeDtypeStruct((SPAN, part + 2 * count, size), BF),
        scratch_shapes=[pltpu.VMEM((SPAN * count, size), F32)] * 2,
        compiler_params=PARAMS,
        cost_estimate=cost(
            3 * SPAN * SPAN * part * count * size, 6 * got.size, SPAN * SPAN * part * count
        ),
    )(half, got, log_total, mix_grad)


def middle_kernel(experts, place_ref, tokens_ref, mix_ref, *refs):
    weights, refs = refs[:4], refs[4:]
    gain_ref, router_ref, routes_ref, resid_ref, probs_ref, chosen_ref = refs[:6]
    row_refs = refs[6:]
    step = pl.program_id(0)
    parts = mix_ref.shape[0] // 4

    @pl.when(step == 0)
    def _():
        resid_ref[...] = tokens_ref[...].astype(F32)

    total = resid_ref[...]
    for r in range(4):
        rows = [mix_ref[p * 4 + (r ^ place_ref[0])] for p in range(parts)]
        total = total + dot(jnp.concatenate(rows, 0), weights[r][...], 1, 0)
    resid_ref[...] = total

    @pl.when(step == pl.num_programs(0) - 1)
    def _():
        state = total
        scale = lax.rsqrt(jnp.mean(state * state, -1, keepdims=True) + EPSILON)
        normed = (state * scale * gain_ref[...]).astype(BF)
        logits = dot(normed, router_ref[...], 1, 0)
        lane = lax.broadcasted_iota(jnp.int32, logits.shape, 1)
        real = lane < experts
        top = jnp.max(jnp.where(real, logits, NEGATIVE), -1, keepdims=True)
        powers = jnp.exp(jnp.minimum(logits - top, 0.0))
        probs = powers / jnp.sum(jnp.where(real, powers, 0.0), -1, keepdims=True)
        routes = routes_ref[...]
        chosen = jnp.zeros(logits.shape, F32)
        for k in range(routes.shape[1]):
            column = routes[:, k : k + 1]
            hit = (lane == column) | (lane == column + experts)
            chosen = jnp.where(hit, 1.0, chosen)
        probs_ref[...] = jnp.where(real, probs, 0.0)
        chosen_ref[...] = jnp.where(real, chosen, 0.0)
        gates = probs * chosen
        high = gates.astype(BF).astype(F32)
        side = jnp.where(real, high, jnp.where(lane < 2 * experts, gates - high, 0.0))
        rows = jnp.concatenate([normed, side.astype(BF)], 1)
        begin = 0
        for ref in row_refs:
            ref[...] = rows[:, begin : begin + ref.shape[1]]
            begin += ref.shape[1]


def middle(tokens, mix, weights, gain, router_wide, routes, place, experts, groups):
    local, width = weights[0].shape
    size = mix.shape[2]
    heads = local // size
    own = tokens.shape[0] // 4
    wide = router_wide.shape[1]
    shape = jax.ShapeDtypeStruct
    return pl.pallas_call(
        functools.partial(middle_kernel, experts),
        grid_spec=pltpu.PrefetchScalarGridSpec(
            num_scalar_prefetch=1,
            grid=(heads,),
            in_specs=[
                pl.BlockSpec((own, width), lambda i, place_ref: (place_ref[0], 0)),
                pl.BlockSpec((mix.shape[0] // heads,) + mix.shape[1:], lambda i, *_: (i, 0, 0)),
            ]
            + [pl.BlockSpec((size, width), lambda i, *_: (i, 0))] * 4
            + [
                resident((1, width)),
                resident(router_wide.shape),
                pl.BlockSpec((own, routes.shape[1]), lambda i, place_ref: (place_ref[0], 0)),
            ],
            out_specs=[
                resident((own, width)),
                resident((own, wide)),
                resident((own, wide)),
            ]
            + [resident((own, columns)) for columns in groups],
        ),
        out_shape=[
            shape((own, width), F32),
            shape((own, wide), F32),
            shape((own, wide), F32),
        ]
        + [shape((own, columns), BF) for columns in groups],
        compiler_params=PARAMS,
        cost_estimate=cost(4 * own * width * local, 8 * width * local),
    )(place, tokens, mix, *weights, gain[None], router_wide, routes)


def middle_back_kernel(experts, place_ref, *refs):
    homes, weights, refs = refs[:6], refs[6:10], refs[10:]
    resid_ref, probs_ref, chosen_ref, gain_ref, router_ref, cotangent_ref = refs[:6]
    grad_ref, low_ref, small_ref, mix_ref = refs[6:]
    width = resid_ref.shape[1]

    @pl.when(pl.program_id(0) == 0)
    def _():
        parts = [a[...].astype(F32) + b[...].astype(F32) for a, b in zip(homes[:3], homes[3:])]
        home = jnp.concatenate(parts, 1)
        side = home[:, width:]
        lanes = side.shape[1]
        gate_grad = (side + pltpu.roll(side, lanes - experts, 1)) * chosen_ref[...]
        probs = probs_ref[...]
        inner = jnp.sum(probs * gate_grad, -1, keepdims=True)
        logit_low = (probs * (gate_grad - inner)).astype(BF)
        state = resid_ref[...]
        scale = lax.rsqrt(jnp.mean(state * state, -1, keepdims=True) + EPSILON)
        unit = state * scale
        mid_grad = home[:, :width] + dot(logit_low, router_ref[...], 1, 1)
        scaled = mid_grad * gain_ref[...]
        grad = cotangent_ref[...].astype(F32) + scale * (
            scaled - unit * jnp.mean(scaled * unit, -1, keepdims=True)
        )
        grad_ref[...] = grad
        low_ref[...] = grad.astype(BF)
        normed = (unit * gain_ref[...]).astype(BF)
        small_ref[:experts] = dot(logit_low, normed, 0, 0)[:experts]
        d_gain = jnp.sum(mid_grad * unit, 0, keepdims=True)
        row = lax.broadcasted_iota(jnp.int32, (8, width), 0)
        small_ref[experts:] = jnp.where(row == 0, d_gain, 0.0)

    low = low_ref[...]
    parts, piece = mix_ref.shape[0] // 4, mix_ref.shape[1]
    for r in range(4):
        product = dot(low, weights[r][...], 1, 1).astype(BF)
        for p in range(parts):
            mix_ref[p * 4 + (r ^ place_ref[0])] = product[p * piece : (p + 1) * piece]


def middle_back(homes, weights, resid, probs, chosen, gain, router_wide, cotangent, place, experts, size):
    own, width = resid.shape
    heads = weights[0].shape[0] // size
    parts = SPAN // heads
    shape = jax.ShapeDtypeStruct
    arrays = [resid, probs, chosen, gain[None], router_wide]
    return pl.pallas_call(
        functools.partial(middle_back_kernel, experts),
        grid_spec=pltpu.PrefetchScalarGridSpec(
            num_scalar_prefetch=1,
            grid=(heads,),
            in_specs=[resident(a.shape) for a in homes]
            + [pl.BlockSpec((size, width), lambda i, *_: (i, 0))] * 4
            + [resident(a.shape) for a in arrays]
            + [pl.BlockSpec((own, width), lambda i, place_ref: (place_ref[0], 0))],
            out_specs=[
                resident((own, width)),
                resident((own, width)),
                resident((experts + 8, width)),
                pl.BlockSpec((parts * 4, own // parts, size), lambda i, *_: (i, 0, 0)),
            ],
        ),
        out_shape=[
            shape((own, width), F32),
            shape((own, width), BF),
            shape((experts + 8, width), F32),
            shape((heads * parts * 4, own // parts, size), BF),
        ],
        compiler_params=PARAMS,
        cost_estimate=cost(4 * own * width * heads * size, 8 * heads * size * width),
    )(place, *homes, *weights, *arrays, cotangent)


def spread(block):
    side = swap(block, "tensor", 2)
    core = swap(block, "tensor", 1)
    return block, core, side, swap(side, "tensor", 1)


def out_grad_kernel(*refs):
    blocks, mixes, out_ref = refs[:4], refs[4:8], refs[8]
    lows = jnp.concatenate([ref[...] for ref in blocks], 0)
    own = blocks[0].shape[0]
    parts = own // mixes[0].shape[1]
    pieces = []
    for h in range(mixes[0].shape[0] // parts):
        rows = [ref[h * parts + p] for ref in mixes for p in range(parts)]
        pieces.append(dot(jnp.concatenate(rows, 0), lows, 0, 0).astype(BF))
    product = jnp.concatenate(pieces, 0)
    if len(out_ref.shape) == 2:
        out_ref[...] = product
        return
    rows, wide = out_ref.shape[1:]
    block = lows.shape[1]
    for q in range(wide // block):
        out_ref[0, :, q * block : (q + 1) * block] = product[q * rows : (q + 1) * rows]


def out_weight_grad(blocks, mixes, local, owners):
    own, width = blocks[0].shape
    block = width // owners
    if block % LANES == 0:
        rows = local // owners
        out = pl.BlockSpec((1, rows, width), lambda d: (d, 0, 0))
        shape = jax.ShapeDtypeStruct((owners, rows, width), BF)
    else:
        block = 4 * LANES
        out = pl.BlockSpec((local, block), lambda d: (0, d))
        shape = jax.ShapeDtypeStruct((local, width), BF)
    return pl.pallas_call(
        out_grad_kernel,
        grid=(width // block,),
        in_specs=[pl.BlockSpec((own, block), lambda d: (0, d))] * 4
        + [resident(mix.shape) for mix in mixes],
        out_specs=out,
        out_shape=shape,
        compiler_params=PARAMS,
        cost_estimate=cost(4 * own * local * width, local * width * 3),
    )(*blocks, *mixes)


def unturn_kernel(full_width, back_ref, query_ref, key_ref, sums_ref, *refs):
    query_gain_ref, key_gain_ref, cos_ref, sin_ref = refs[:4]
    query_out_ref, key_out_ref, value_out_ref, inner_ref, gains_ref = refs[4:]
    heads, size = query_gain_ref.shape
    parts = SPAN // heads
    count = cos_ref.shape[0]
    part = count // parts
    piece = part // 4
    scales = scales_of(sums_ref[...], full_width)
    inner = [0.0, 0.0]
    for h in range(heads):
        span = slice(h * size, (h + 1) * size)
        first = h * parts
        query = jnp.concatenate(
            [
                back_ref[first + p, t * piece : (t + 1) * piece]
                for t in range(4)
                for p in range(parts)
            ],
            0,
        )
        key = sum(back_ref[first + p, part : part + count].astype(F32) for p in range(parts))
        value = sum(back_ref[first + p, part + count :].astype(F32) for p in range(parts))
        value_out_ref[:, span] = value.astype(BF)
        key = key.astype(BF)
        items = ((query, query_ref, query_gain_ref, query_out_ref), (key, key_ref, key_gain_ref, key_out_ref))
        for n, (grad, raw_ref, gain_ref, out_ref) in enumerate(items):
            grad = grad.astype(F32)
            gain_in = grad * cos_ref[...] - pltpu.roll(grad, size // 2, 1) * sin_ref[...]
            unit = raw_ref[:, span] * scales[:, n : n + 1]
            gains_ref[n * heads + h] = jnp.broadcast_to(
                jnp.sum(gain_in * unit, 0, keepdims=True), (8, size)
            )
            scaled = gain_in * gain_ref[pl.ds(h, 1), :]
            out_ref[:, span] = scaled
            inner[n] = inner[n] + scaled * unit
    inner_ref[...] = two_rows(inner[0], inner[1])


def unturn(back, query, key, sums, query_gain, key_gain, cos, sin, full_width):
    count, local = query.shape
    heads, size = query_gain.shape
    shape = jax.ShapeDtypeStruct
    return pl.pallas_call(
        functools.partial(unturn_kernel, full_width),
        out_shape=[
            shape((count, local), F32),
            shape((count, local), F32),
            shape((count, local), BF),
            shape((8, count), F32),
            shape((2 * heads, 8, size), F32),
        ],
        compiler_params=PARAMS,
        cost_estimate=cost(0, 24 * query.size),
    )(back, query, key, sums, query_gain, key_gain, cos, sin)


def columns_kernel(full_width, *refs):
    query_scaled_ref, key_scaled_ref, value_ref, query_ref, key_ref, sums_ref, inner_ref = refs[:7]
    query_low_ref, key_low_ref, out_ref = refs[7:]
    owners, rows, _ = out_ref.shape
    rows = rows // 3
    scales = scales_of(sums_ref[...], full_width)
    means = inner_ref[...].T / full_width
    items = ((query_scaled_ref, query_ref, query_low_ref), (key_scaled_ref, key_ref, key_low_ref))
    lows = []
    for n, (scaled_ref, raw_ref, low_ref) in enumerate(items):
        scale = scales[:, n : n + 1]
        unit = raw_ref[...] * scale
        low = (scale * (scaled_ref[...] - unit * means[:, n : n + 1])).astype(BF)
        low_ref[...] = low
        lows.append(low)
    for n, low in enumerate(lows + [value_ref[...]]):
        turned = low.T
        for d in range(owners):
            out_ref[d, n * rows : (n + 1) * rows] = turned[d * rows : (d + 1) * rows]


def columns_of(query_scaled, key_scaled, value, query, key, sums, inner, full_width, owners):
    count, local = query.shape
    low = jax.ShapeDtypeStruct((count, local), BF)
    return pl.pallas_call(
        functools.partial(columns_kernel, full_width),
        out_shape=[low, low, jax.ShapeDtypeStruct((owners, 3 * local // owners, count), BF)],
        compiler_params=PARAMS,
        cost_estimate=cost(0, 24 * query.size),
    )(query_scaled, key_scaled, value, query, key, sums, inner)


def input_kernel(own, place_ref, *refs):
    lows, weights, kept_ref, sent_ref = refs[:3], refs[3:6], refs[6], refs[7]
    place = place_ref[0]
    total = None
    for low_ref, weight_ref in zip(lows, weights):
        rows = [
            low_ref[pl.ds(pl.multiple_of((r ^ place) * own, own), own), :] for r in range(4)
        ]
        product = dot(jnp.concatenate(rows, 0), weight_ref[...], 1, 1)
        total = product if total is None else total + product
    total = total.astype(BF)
    for r in range(4):
        ref = sent_ref if r % 2 else kept_ref
        ref[r // 2] = total[r * own : (r + 1) * own]


def input_back(lows, weights, place, own, block=512):
    width, local = weights[0].shape
    out = pl.BlockSpec((2, own, block), lambda d, *_: (0, 0, d))
    shape = jax.ShapeDtypeStruct((2, own, width), BF)
    return pl.pallas_call(
        functools.partial(input_kernel, own),
        grid_spec=pltpu.PrefetchScalarGridSpec(
            num_scalar_prefetch=1,
            grid=(width // block,),
            in_specs=[resident(lows[0].shape)] * 3
            + [pl.BlockSpec((block, local), lambda d, *_: (d, 0))] * 3,
            out_specs=[out, out],
        ),
        out_shape=[shape, shape],
        compiler_params=PARAMS,
        cost_estimate=cost(12 * own * local * width, local * width * 7),
    )(place, *lows, *weights)


def last_kernel(place_ref, tokens_ref, *refs):
    kept_ref, core_ref, side_ref, grad_ref, gain_ref, small_ref, out_ref = refs
    own = grad_ref.shape[0]
    extra = out_ref.shape[0] - own
    used = small_ref.shape[0]
    state = tokens_ref[...].astype(F32)
    scale = lax.rsqrt(jnp.mean(state * state, -1, keepdims=True) + EPSILON)
    unit = state * scale
    grad = kept_ref[0].astype(F32) + core_ref[0].astype(F32) + side_ref[...].astype(F32)
    scaled = grad * gain_ref[...]
    out = grad_ref[...] + scale * (scaled - unit * jnp.mean(scaled * unit, -1, keepdims=True))
    out_ref[:own] = out.astype(BF)
    d_gain = jnp.sum(grad * unit, 0, keepdims=True)
    row = lax.broadcasted_iota(jnp.int32, (8, state.shape[1]), 0)
    gains = small_ref[used - 8 :] + jnp.where(row == 1, d_gain, 0.0)
    rows = [small_ref[: used - 8], gains]
    if extra > used:
        rows.append(jnp.zeros((extra - used, state.shape[1]), F32))
    out_ref[own:] = jnp.concatenate(rows, 0).astype(BF)


def last(tokens, kept, core, side, grad, gain, small, place):
    own, width = side.shape
    arrays = [kept, core, side, grad, gain[None], small]
    rows = own + -(-small.shape[0] // 16) * 16
    return pl.pallas_call(
        last_kernel,
        grid_spec=pltpu.PrefetchScalarGridSpec(
            num_scalar_prefetch=1,
            grid=(1,),
            in_specs=[pl.BlockSpec((own, width), lambda i, place_ref: (place_ref[0], 0))]
            + [resident(a.shape) for a in arrays],
            out_specs=resident((rows, width)),
        ),
        out_shape=jax.ShapeDtypeStruct((rows, width), BF),
        compiler_params=PARAMS,
        cost_estimate=cost(0, own),
    )(place, tokens, *arrays)


def tile_kernel(rows_ref, out_ref):
    rows, wide = rows_ref.shape
    block = out_ref.shape[1]
    for q in range(wide // block):
        out_ref[q * rows : (q + 1) * rows] = rows_ref[:, q * block : (q + 1) * block].astype(F32)


def tile_rows(rows, local):
    return pl.pallas_call(
        tile_kernel,
        out_shape=jax.ShapeDtypeStruct((local, rows.size // local), F32),
        compiler_params=PARAMS,
        cost_estimate=cost(0, rows.size * 6),
    )(rows)


def join_kernel(own, place_ref, *refs):
    out_ref = refs[4]
    for r in range(4):
        start = pl.multiple_of((r ^ place_ref[0]) * own, own)
        out_ref[pl.ds(start, own), :] = refs[r][:own].astype(out_ref.dtype)


def join_blocks(blocks, place, own, kind):
    width = blocks[0].shape[1]
    vmem = pl.BlockSpec(memory_space=pltpu.VMEM)
    return pl.pallas_call(
        functools.partial(join_kernel, own),
        in_specs=[pl.BlockSpec(memory_space=pltpu.SMEM)] + [vmem] * 4,
        out_shape=jax.ShapeDtypeStruct((4 * own, width), kind),
        compiler_params=PARAMS,
        cost_estimate=cost(0, own),
    )(place, *blocks)


def weights_kernel(columns_ref, rows_ref, small_ref, out_ref):
    owners, columns, count = columns_ref.shape
    total = None
    for s in range(owners):
        product = dot(columns_ref[s], rows_ref[pl.ds(s * count, count), :], 1, 0)
        total = product if total is None else total + product
    out_ref[0, :columns] = total.astype(BF)
    out_ref[0, columns:] = small_ref[0]


def weight_columns(columns, rows, small):
    owners, count3, count = columns.shape
    width = rows.shape[1]
    slab = width // owners
    extra = small.shape[1]
    return pl.pallas_call(
        weights_kernel,
        grid=(owners,),
        in_specs=[
            resident(columns.shape),
            pl.BlockSpec((rows.shape[0], slab), lambda d: (0, d)),
            pl.BlockSpec((1, extra, slab), lambda d: (d, 0, 0)),
        ],
        out_specs=pl.BlockSpec((1, count3 + extra, slab), lambda d: (d, 0, 0)),
        out_shape=jax.ShapeDtypeStruct((owners, count3 + extra, slab), BF),
        compiler_params=PARAMS,
        cost_estimate=cost(rows.shape[0] * width * count3, rows.size * 2),
    )(columns, rows, small)


def unpack_kernel(given_ref, *outs):
    owners, _, slab = given_ref.shape
    local = outs[0].shape[1]
    rows = local // owners
    group = LANES // rows
    for n, out_ref in enumerate(outs[:3]):
        for s in range(0, owners, group):
            pieces = [given_ref[s + g, n * rows : (n + 1) * rows] for g in range(group)]
            turned = jnp.concatenate(pieces, 0).astype(F32).T
            out_ref[:, s * rows : (s + group) * rows] = turned
    total = given_ref[0, 3 * rows :].astype(F32)
    for s in range(1, owners):
        total = total + given_ref[s, 3 * rows :].astype(F32)
    outs[3][...] = total


def unpack(given, local):
    owners, rows, slab = given.shape
    extra = rows - 3 * local // owners
    weight = jax.ShapeDtypeStruct((slab, local), F32)
    return pl.pallas_call(
        unpack_kernel,
        out_shape=[weight, weight, weight, jax.ShapeDtypeStruct((extra, slab), F32)],
        compiler_params=PARAMS,
        cost_estimate=cost(0, given.size * 6),
    )(given)


def per_device(
    tokens,
    segment_ids,
    routes,
    norm1_gain,
    w_query,
    w_key,
    w_value,
    query_gain,
    key_gain,
    w_out,
    norm2_gain,
    w_router,
    w_gate,
    w_up,
    w_down,
    cotangent,
):
    tok_count, model_width = tokens.shape
    heads_here, head_size = query_gain.shape
    local_width = heads_here * head_size
    tensor_count = lax.axis_size("tensor")
    full_width = local_width * tensor_count
    experts = w_router.shape[1]
    owners = lax.axis_size("dp")
    dp_place = lax.axis_index("dp")
    tensor_place = lax.axis_index("tensor")
    own = tok_count // tensor_count
    parts = SPAN // heads_here
    part = tok_count // parts
    groups = [list(range(g, g + SPAN)) for g in range(0, owners, SPAN)]
    place = tensor_place.astype(jnp.int32).reshape(1)
    index = jnp.stack([dp_place, tensor_place]).astype(jnp.int32)
    half = (dp_place % SPAN % parts).astype(jnp.int32).reshape(1)

    def mine(array):
        return lax.dynamic_slice_in_dim(array, tensor_place * own, own, 0)

    def trade(array):
        return lax.all_to_all(
            array, "dp", split_axis=0, concat_axis=0, tiled=True, axis_index_groups=groups
        )

    def trade_every(array):
        wide = None
        if owners > SPAN:
            count = SPAN * tensor_count
            wide = [list(range(g, g + count)) for g in range(0, owners * tensor_count, count)]
        return lax.all_to_all(
            array, EVERY, split_axis=0, concat_axis=0, tiled=True, axis_index_groups=wide
        )

    def sum_tensor(kept, sent):
        core = swap(sent, "tensor", 1)
        given = (kept[1].astype(F32) + core[1].astype(F32)).astype(BF)
        return kept, core, swap(given, "tensor", 2)

    out_grad_all = lax.all_gather(mine(cotangent), EVERY, axis=0, tiled=True)
    both_turned, down_turned = turn_weights(w_gate, w_up, w_down)
    side_width = -(-2 * experts // LANES) * LANES
    router_wide = jnp.pad(
        jnp.concatenate([w_router, w_router], 1), ((0, 0), (0, side_width - 2 * experts))
    )
    local_pos = jnp.arange(tok_count, dtype=jnp.int32)
    positions = (dp_place % SPAN * tok_count + local_pos).astype(F32)
    cos_table, sin_table = rope_tables(positions, head_size)
    segment_low = segment_ids.astype(BF)
    segment_parts = segment_low.reshape(tensor_count, parts, -1).transpose(1, 0, 2)
    segment_rows = jnp.concatenate(
        [
            jnp.broadcast_to(segment_low.reshape(1, -1, head_size), (parts, tok_count // head_size, head_size)),
            segment_parts.reshape(parts, 1, part),
        ],
        1,
    )
    segment_rows = jnp.pad(segment_rows, ((0, 0), (0, 16 - segment_rows.shape[1]), (0, 0)))

    normed_in, query_raw, key_raw, value_att, squares = project(
        tokens, norm1_gain, w_query, w_key, w_value
    )
    squares, w_out = lax.optimization_barrier((lax.psum(squares, "tensor"), w_out))
    out_weights = spread(w_out)
    packed = pack_heads(
        query_raw,
        key_raw,
        value_att,
        squares,
        query_gain,
        key_gain,
        cos_table,
        sin_table,
        segment_rows,
        full_width,
    )
    got = trade(packed)
    mix_heads, log_total = attend(got, half, part, tok_count)
    pieces_count, piece = SPAN * tensor_count, own // parts
    mix, both_turned, down_turned = lax.optimization_barrier(
        (
            trade_every(mix_heads.reshape(pieces_count, piece, head_size)),
            both_turned,
            down_turned,
        )
    )
    lanes = -(-(model_width + side_width) // (3 * LANES)) * LANES
    resid_state, router_probs, chosen, *rows_own = middle(
        tokens,
        mix,
        out_weights,
        norm2_gain,
        router_wide,
        routes,
        place,
        experts,
        [lanes, lanes, model_width + side_width - 2 * lanes],
    )
    bits = owners.bit_length() - 1
    first_three = [("tensor", 2), ("dp", 1), ("dp", 2)]
    rest = [("dp", 1 << b) for b in range(2, bits)]
    orders = [first_three[g:] + first_three[:g] + rest for g in range(3)]
    pieces, names, back_all, tokens_own = gather_every(
        rows_own,
        [order[::-1] for order in orders],
        hidden_back(out_grad_all, down_turned),
        mine(tokens),
    )
    tokens_all = lax.all_gather(tokens_own, EVERY, axis=0, tiled=True)
    (rows_all, hid, hid_turned, glow, ulow), kept_groups, sent_groups = expert_rows(
        pieces, names, back_all, w_gate, w_up, both_turned, index, experts, tok_count
    )
    out_kept, out_sent = expert_out(hid, w_down, place % 2, tok_count)
    d_w_gate = over_rows(rows_all, glow, w_gate.shape)

    def add_core(kept_rows, sent_rows):
        core_rows = swap(sent_rows, "tensor", 1)
        return ((kept_rows.astype(F32) + core_rows.astype(F32)).astype(BF),)

    homes, out_part = sum_every(kept_groups, sent_groups, orders, (out_kept, out_sent), add_core)
    core_groups = [
        [d * tensor_count + x * 2 + c for d in range(owners) for x in range(2)] for c in range(2)
    ]
    expert_full = lax.psum_scatter(
        out_part.reshape(-1, model_width),
        EVERY,
        scatter_dimension=0,
        tiled=True,
        axis_index_groups=core_groups,
    )
    d_w_down = turned_rows(hid_turned, out_grad_all).reshape(w_down.shape)
    d_w_up = over_rows(rows_all, ulow, w_up.shape)
    normed_in_all = norm_all(tokens_all, norm1_gain, tok_count)

    resid_grad, resid_low, small, mix_grad = middle_back(
        [home[0] for home in homes] + [home[1] for home in homes],
        out_weights,
        resid_state,
        router_probs,
        chosen,
        norm2_gain,
        router_wide,
        cotangent,
        place,
        experts,
        head_size,
    )
    mix_grad, d_w_up = lax.optimization_barrier((trade_every(mix_grad), d_w_up))
    mix_by_block = mix.reshape(SPAN, tensor_count, piece, head_size)
    mix_by_block, mix_grad = lax.optimization_barrier((mix_by_block, mix_grad))
    mixes = [
        lax.dynamic_index_in_dim(mix_by_block, tensor_place ^ r, 1, keepdims=False)
        for r in range(4)
    ]
    mixes = mixes[:1] + [swap(mixes[r], "tensor", r) for r in range(1, 4)]
    lows = [resid_low] + [swap(resid_low, "tensor", r) for r in range(1, 4)]
    d_out = out_weight_grad(lows, mixes, local_width, owners)
    back, d_w_down, normed_in_all, expert_full, d_out = lax.optimization_barrier(
        (
            trade(
                attend_back(
                    got,
                    half,
                    log_total,
                    mix_grad.reshape(SPAN, part, head_size),
                    part,
                    tok_count,
                )
            ),
            d_w_down,
            normed_in_all,
            expert_full,
            d_out,
        )
    )
    query_scaled, key_scaled, value_low, inner, gains = unturn(
        back, query_raw, key_raw, squares, query_gain, key_gain, cos_table, sin_table, full_width
    )
    inner = lax.psum(inner, "tensor")
    model_slice = model_width // owners
    if model_slice % LANES == 0:
        d_out = lax.psum_scatter(d_out, "dp", scatter_dimension=0, tiled=True)[0]
        d_out = tile_rows(d_out, local_width)
    else:
        d_out = lax.psum_scatter(d_out, "dp", scatter_dimension=1, tiled=True).astype(F32)
    block_own = (resid_state + expert_full.astype(F32)).astype(BF)
    out_blocks = spread(block_own)

    query_low, key_low, columns = columns_of(
        query_scaled, key_scaled, value_low, query_raw, key_raw, squares, inner, full_width, owners
    )
    columns = lax.all_to_all(columns, "dp", split_axis=0, concat_axis=0, tiled=True)
    block_output = join_blocks(out_blocks, place, own, BF)
    kept, core, side = sum_tensor(
        *input_back(
            (query_low, key_low, value_low), (w_query, w_key, w_value), place, own
        )
    )
    input_blocks = spread(
        last(tokens, kept, core, side, resid_grad, norm1_gain, small, place)
    )
    input_grad = join_blocks(input_blocks, place, own, F32)

    head_slice = head_size // owners
    slice_width = local_width // owners
    gain_count = 2 * heads_here * head_slice
    gain_rows = -(-gain_count // model_slice)
    gains = gains[:, 0].reshape(2 * heads_here, owners, head_slice).transpose(1, 0, 2)
    gains = jnp.pad(
        gains.reshape(owners, gain_count), ((0, 0), (0, gain_rows * model_slice - gain_count))
    ).reshape(owners, gain_rows, model_slice)
    shared = sum(block[own : own + experts + 2].astype(F32) for block in input_blocks)
    shared = shared.reshape(experts + 2, owners, model_slice).transpose(1, 0, 2)
    extra = jnp.concatenate([shared, gains], 1).astype(BF)
    extra = jnp.pad(extra, ((0, 0), (0, -extra.shape[1] % 16), (0, 0)))
    if model_slice % LANES == 0:
        final = weight_columns(columns, normed_in_all, extra)
    else:
        columns = columns.transpose(1, 0, 2).reshape(3 * slice_width, owners * tok_count)
        final = dot(columns, normed_in_all, 1, 0).reshape(3 * slice_width, owners, model_slice)
        final = jnp.concatenate([final.transpose(1, 0, 2).astype(BF), extra], 1)
    final, block_output, input_grad = lax.optimization_barrier(
        (
            lax.all_to_all(final, "dp", split_axis=0, concat_axis=0, tiled=True),
            block_output,
            input_grad,
        )
    )
    *weights, extra = unpack(final, local_width)
    gains = extra[experts + 2 : experts + 2 + gain_rows].reshape(-1)[:gain_count]
    gains = gains.reshape(2, heads_here, head_slice)

    return (
        block_output,
        input_grad,
        extra[experts + 1],
        weights[0],
        weights[1],
        weights[2],
        gains[0],
        gains[1],
        d_out,
        extra[experts],
        extra[:experts].T,
        d_w_gate,
        d_w_up,
        d_w_down,
    )


def solution(mesh):
    in_specs = (
        P("dp", None),
        P("dp"),
        P("dp", None),
        P(),
        P(None, "tensor"),
        P(None, "tensor"),
        P(None, "tensor"),
        P("tensor", None),
        P("tensor", None),
        P("tensor", None),
        P(),
        P(),
        P("dp", None, "tensor"),
        P("dp", None, "tensor"),
        P("dp", "tensor", None),
        P("dp", None),
    )
    out_specs = (
        P("dp", None),
        P("dp", None),
        P("dp"),
        P("dp", "tensor"),
        P("dp", "tensor"),
        P("dp", "tensor"),
        P("tensor", "dp"),
        P("tensor", "dp"),
        P("tensor", "dp"),
        P("dp"),
        P("dp", None),
        P("dp", None, "tensor"),
        P("dp", None, "tensor"),
        P("dp", "tensor", None),
    )
    return jax.shard_map(
        per_device, mesh=mesh, in_specs=in_specs, out_specs=out_specs, check_vma=False
    )
```

```python
import functools
import math

import jax
import jax.numpy as jnp
from jax import lax
from jax.experimental import pallas as pl
from jax.experimental.pallas import tpu as pltpu
from jax.sharding import PartitionSpec as P

SPAN = 8


EPSILON = 1e-05
ROPE_BASE = 10000.0
NEGATIVE = -1e30
BF = jnp.bfloat16
F32 = jnp.float32
EVERY = ("dp", "tensor")
VMEM_LIMIT = 56 * 1024 * 1024
LANES = 128


def rope_tables(positions, head_size):
    frequency = ROPE_BASE ** (-jnp.arange(0, head_size, 2, dtype=jnp.float32) / head_size)
    angles = positions[:, None] * frequency[None, :]
    cosine, sine = jnp.cos(angles), jnp.sin(angles)
    return jnp.concatenate([cosine, cosine], -1), jnp.concatenate([-sine, sine], -1)


def dot(left_side, right_side, left_dim, right_dim):
    return lax.dot_general(
        left_side,
        right_side,
        (((left_dim,), (right_dim,)), ((), ())),
        preferred_element_type=jnp.float32,
    )


def swap(array, axis, bit):
    count = lax.axis_size(axis)
    return lax.ppermute(array, axis, [(i, i ^ bit) for i in range(count)])


def total_tensor(array):
    others = [swap(array, "tensor", r) for r in range(1, 4)]
    return (array + others[0]) + (others[1] + others[2])


def resident(shape):
    return pl.BlockSpec(shape, lambda *_: (0,) * len(shape), pipeline_mode=pl.Buffered(1))


def cost(macs, size, transcendentals=0):
    return pl.CostEstimate(flops=2 * macs, bytes_accessed=size, transcendentals=transcendentals)


PARAMS = pltpu.CompilerParams(vmem_limit_bytes=VMEM_LIMIT)


def turn_kernel(gate_ref, up_ref, down_ref, both_ref, down_out_ref):
    count, _, hidden = gate_ref.shape
    for e in range(count):
        both_ref[pl.ds(e * hidden, hidden), :] = gate_ref[e].T
        both_ref[pl.ds((count + e) * hidden, hidden), :] = up_ref[e].T
        down_out_ref[:, pl.ds(e * hidden, hidden)] = down_ref[e].T


def turn_weights(w_gate, w_up, w_down, block=256):
    count, width, hidden = w_gate.shape
    mid = count * hidden
    rows = pl.BlockSpec((count, block, hidden), lambda d: (0, d, 0))
    return pl.pallas_call(
        turn_kernel,
        grid=(width // block,),
        in_specs=[rows, rows, pl.BlockSpec((count, hidden, block), lambda d: (0, 0, d))],
        out_specs=[
            pl.BlockSpec((2 * mid, block), lambda d: (0, d)),
            pl.BlockSpec((block, mid), lambda d: (d, 0)),
        ],
        out_shape=[
            jax.ShapeDtypeStruct((2 * mid, width), BF),
            jax.ShapeDtypeStruct((width, mid), BF),
        ],
        compiler_params=PARAMS,
        cost_estimate=cost(0, 12 * mid * width),
    )(w_gate, w_up, w_down)


def hidden_back_kernel(grad_ref, down_ref, out_ref):
    out_ref[...] = dot(grad_ref[...], down_ref[...], 1, 0)


def hidden_back(grad_all, down_turned, block=256):
    width, mid = down_turned.shape
    total = grad_all.shape[0]
    return pl.pallas_call(
        hidden_back_kernel,
        grid=(total // block,),
        in_specs=[pl.BlockSpec((block, width), lambda i: (i, 0)), resident(down_turned.shape)],
        out_specs=pl.BlockSpec((block, mid), lambda i: (i, 0)),
        out_shape=jax.ShapeDtypeStruct((total, mid), F32),
        compiler_params=PARAMS,
        cost_estimate=cost(total * width * mid, total * width * 3),
    )(grad_all, down_turned)


def expert_kernel(experts, axes, index_ref, *refs):
    pieces, refs = (refs[:3], refs[3:6]), refs[6:]
    back_ref, gate_ref, up_ref, both_ref, rows_ref = refs[:5]
    hid_ref, hid_turned_ref, glow_ref, ulow_ref = refs[5:9]
    kept_refs, sent_refs, low_ref, side_ref = refs[9:12], refs[12:15], refs[15], refs[16]
    count, width, hidden_size = gate_ref.shape
    mid = count * hidden_size
    own = kept_refs[0].shape[2]
    starts = [pl.multiple_of((r ^ index_ref[1]) * own, own) for r in range(4)]
    for r in range(4):
        begin = 0
        for piece, axis in zip(pieces[r % 2], axes):
            place = [0] * (len(piece.shape) - 2)
            place[axis] = r // 2
            columns = piece.shape[-1]
            end = min(begin + columns, width)
            value = piece[tuple(place)]
            rows_ref[pl.ds(starts[r], own), begin:end] = value[:, : end - begin]
            if end - begin < columns:
                side_ref[pl.ds(starts[r], own), :] = value[:, end - begin :]
            begin = end
    rows = rows_ref[...]
    side = side_ref[...].astype(F32)
    lane = lax.broadcasted_iota(jnp.int32, side.shape, 1)
    dots = jnp.zeros(side.shape, F32)
    for e in range(count):
        column = index_ref[0] * count + e
        gate = jnp.sum(
            jnp.where((lane == column) | (lane == experts + column), side, 0.0), -1, keepdims=True
        )
        span = pl.ds(e * hidden_size, hidden_size)
        gate_pre = dot(rows, gate_ref[e], 1, 0)
        up_pre = dot(rows, up_ref[e], 1, 0)
        out_back = back_ref[:, span]
        sigma = 1.0 / (1.0 + jnp.exp(-gate_pre))
        silu = gate_pre * sigma
        hidden = silu * up_pre
        inner = jnp.sum(hidden * out_back, -1, keepdims=True)
        high = inner.astype(BF).astype(F32)
        dots = jnp.where(lane == column, high, dots)
        dots = jnp.where(lane == experts + column, inner - high, dots)
        hidden_low = (gate * hidden).astype(BF)
        hidden_grad = gate * out_back
        glow = (hidden_grad * up_pre * sigma * (1.0 + gate_pre * (1.0 - sigma))).astype(BF)
        ulow = (hidden_grad * silu).astype(BF)
        hid_ref[:, span] = hidden_low
        hid_turned_ref[span, :] = hidden_low.T
        glow_ref[:, span] = glow
        ulow_ref[:, span] = ulow
        low_ref[:, span] = glow
        low_ref[:, pl.ds(mid + e * hidden_size, hidden_size)] = ulow
    low_ref[:, 2 * mid :] = dots.astype(BF)
    low = jnp.concatenate([low_ref[pl.ds(start, own), :] for start in starts], 0)
    begin = 0
    for kept_ref, sent_ref in zip(kept_refs, sent_refs):
        columns = kept_ref.shape[3]
        end = min(begin + columns, width)
        back = dot(low[:, : 2 * mid], both_ref[:, begin:end], 1, 0).astype(BF)
        if end - begin < columns:
            back = jnp.concatenate([back, low[:, 2 * mid :]], 1)
        begin = end
        for r in range(4):
            ref = sent_ref if r % 2 else kept_ref
            ref[0, r // 2] = back[r * own : (r + 1) * own]


def expert_rows(pieces, names, back_all, w_gate, w_up, both_turned, index, experts, block):
    count, width, hidden = w_gate.shape
    total, mid = back_all.shape
    owners = total // block
    groups = [piece.shape[-1] for piece in pieces[0]]
    side = sum(groups) - width

    def rows(columns):
        return pl.BlockSpec((block, columns), lambda i, index_ref: (i ^ index_ref[0], 0))

    def shape(columns):
        return jax.ShapeDtypeStruct((total, columns), BF)

    def given(columns, order):
        sizes = tuple(1 if axis == "dp" else 2 for axis, _ in order)

        def place(i, *_):
            return tuple(i // bit % 2 if axis == "dp" else 0 for axis, bit in order) + (0, 0)

        return pl.BlockSpec(sizes + (block // 4, columns), place)

    def part(columns):
        return pl.BlockSpec((1, 2, block // 4, columns), lambda i, *_: (i, 0, 0, 0))

    def part_shape(columns):
        return jax.ShapeDtypeStruct((owners, 2, block // 4, columns), BF)

    given_specs = [given(columns, order) for columns, order in zip(groups, names)]
    axes = [[axis for axis, _ in order].index("tensor") for order in names]
    outs = pl.pallas_call(
        functools.partial(expert_kernel, experts, axes),
        grid_spec=pltpu.PrefetchScalarGridSpec(
            num_scalar_prefetch=1,
            grid=(owners,),
            in_specs=given_specs * 2
            + [
                rows(mid),
                resident(w_gate.shape),
                resident(w_up.shape),
                resident(both_turned.shape),
            ],
            out_specs=[
                rows(width),
                rows(mid),
                pl.BlockSpec((mid, block), lambda i, index_ref: (0, i ^ index_ref[0])),
                rows(mid),
                rows(mid),
            ]
            + [part(columns) for columns in groups] * 2,
            scratch_shapes=[pltpu.VMEM((block, 2 * mid + side), BF), pltpu.VMEM((block, side), BF)],
        ),
        out_shape=[
            shape(width),
            shape(mid),
            jax.ShapeDtypeStruct((mid, total), BF),
            shape(mid),
            shape(mid),
        ]
        + [part_shape(columns) for columns in groups] * 2,
        compiler_params=PARAMS,
        cost_estimate=cost(4 * total * width * mid, total * width * 8, total * mid),
    )(index, *pieces[0], *pieces[1], back_all, w_gate, w_up, both_turned)
    return outs[:5], outs[5:8], outs[8:]


def gather_every(groups, orders, beside, later):
    totals, names = list(groups), [[] for _ in groups]
    for step in range(len(orders[0])):
        if step == len(orders[0]) - 1:
            totals, later = lax.optimization_barrier((totals, later))
        others = [swap(total, *order[step]) for total, order in zip(totals, orders)]
        if step == len(orders[0]) - 1:
            others, beside = lax.optimization_barrier((others, beside))
        totals = [jnp.stack([total, other]) for total, other in zip(totals, others)]
        for name, order in zip(names, orders):
            name.insert(0, order[step])
    return (totals, [swap(total, "tensor", 1) for total in totals]), names, beside, later


def sum_every(kept, sent, orders, beside, finish):
    bits = lax.axis_size("dp").bit_length() - 1
    totals, names = [], []
    for kept_group, sent_group in zip(kept, sent):
        own, columns = kept_group.shape[2:]
        total = kept_group.astype(F32) + swap(sent_group, "tensor", 1).astype(F32)
        totals.append(total.astype(BF).reshape((2,) * (bits + 1) + (own, columns)))
        names.append([("dp", 1 << (bits - 1 - i)) for i in range(bits)] + [("tensor", 2)])
    for step in range(bits + 1):
        halves, others = [], []
        for total, left, order in zip(totals, names, orders):
            axis = left.index(order[step])
            left.pop(axis)
            given = lax.index_in_dim(total, 1, axis, keepdims=False)
            halves.append(lax.index_in_dim(total, 0, axis, keepdims=False))
            others.append(swap(given, *order[step]))
        if step == 0:
            others, beside = lax.optimization_barrier((others, beside))
        if step == bits:
            others, beside = lax.optimization_barrier((others, finish(*beside)))
        totals = [(a.astype(F32) + b.astype(F32)).astype(BF) for a, b in zip(halves, others)]
    return list(zip(halves, others)), *beside


def out_kernel(core_ref, hid_ref, down_ref, kept_ref, sent_ref):
    count, hidden, _ = down_ref.shape
    own = kept_ref.shape[1]
    rows = []
    for r in range(4):
        start = pl.multiple_of((r // 2 * 2 + ((r % 2) ^ core_ref[0])) * own, own)
        rows.append(hid_ref[pl.ds(start, own), :])
    weight = down_ref[...].reshape(count * hidden, -1)
    out = dot(jnp.concatenate(rows, 0), weight, 1, 0).astype(BF)
    for r in range(4):
        ref = sent_ref if r % 2 else kept_ref
        ref[r // 2] = out[r * own : (r + 1) * own]


def expert_out(hid, w_down, core, block):
    count, hidden, width = w_down.shape
    total = hid.shape[0]
    out = pl.BlockSpec((2, block // 4, width), lambda i, *_: (i, 0, 0))
    shape = jax.ShapeDtypeStruct((total // block * 2, block // 4, width), BF)
    return pl.pallas_call(
        out_kernel,
        grid_spec=pltpu.PrefetchScalarGridSpec(
            num_scalar_prefetch=1,
            grid=(total // block,),
            in_specs=[
                pl.BlockSpec((block, count * hidden), lambda i, *_: (i, 0)),
                resident(w_down.shape),
            ],
            out_specs=[out, out],
        ),
        out_shape=[shape, shape],
        compiler_params=PARAMS,
        cost_estimate=cost(total * width * count * hidden, total * width * 3),
    )(core, hid, w_down)


def over_kernel(left_ref, right_ref, out_ref):
    count, _, hidden = out_ref.shape
    product = dot(left_ref[...], right_ref[...], 0, 0)

    @pl.when(pl.program_id(1) == 0)
    def _():
        for e in range(count):
            out_ref[e] = product[:, e * hidden : (e + 1) * hidden]

    @pl.when(pl.program_id(1) > 0)
    def _():
        for e in range(count):
            out_ref[e] += product[:, e * hidden : (e + 1) * hidden]


def over_rows(rows, low, shape, block=256, chunk=2048):
    count, width, hidden = shape
    total = rows.shape[0]
    chunk = min(chunk, total)
    return pl.pallas_call(
        over_kernel,
        grid=(width // block, total // chunk),
        in_specs=[
            pl.BlockSpec((chunk, block), lambda d, k: (k, d)),
            pl.BlockSpec((chunk, count * hidden), lambda d, k: (k, 0)),
        ],
        out_specs=pl.BlockSpec((count, block, hidden), lambda d, k: (0, d, 0)),
        out_shape=jax.ShapeDtypeStruct(shape, F32),
        compiler_params=PARAMS,
        cost_estimate=cost(total * width * count * hidden, total * width * 4),
    )(rows, low)


def turned_kernel(left_ref, right_ref, out_ref):
    product = dot(left_ref[...], right_ref[...], 1, 0)

    @pl.when(pl.program_id(1) == 0)
    def _():
        out_ref[...] = product

    @pl.when(pl.program_id(1) > 0)
    def _():
        out_ref[...] += product


def turned_rows(left, right, block=256, chunk=2048):
    mid, total = left.shape
    width = right.shape[1]
    chunk = min(chunk, total)
    return pl.pallas_call(
        turned_kernel,
        grid=(width // block, total // chunk),
        in_specs=[
            pl.BlockSpec((mid, chunk), lambda d, k: (0, k)),
            pl.BlockSpec((chunk, block), lambda d, k: (k, d)),
        ],
        out_specs=pl.BlockSpec((mid, block), lambda d, k: (0, d)),
        out_shape=jax.ShapeDtypeStruct((mid, width), F32),
        compiler_params=PARAMS,
        cost_estimate=cost(total * width * mid, total * width * 4),
    )(left, right)


def front_kernel(tokens_ref, gain_ref, query_ref, key_ref, value_ref, *outs):
    normed_ref, query_out_ref, key_out_ref, value_out_ref, squares_ref = outs

    @pl.when(pl.program_id(0) == 0)
    def _():
        state = tokens_ref[...].astype(F32)
        scale = lax.rsqrt(jnp.mean(state * state, -1, keepdims=True) + EPSILON)
        normed_ref[...] = (state * scale * gain_ref[...]).astype(BF)
        squares_ref[...] = jnp.zeros_like(squares_ref)

    normed = normed_ref[...]
    query = dot(normed, query_ref[...], 1, 0)
    key = dot(normed, key_ref[...], 1, 0)
    query_out_ref[...] = query
    key_out_ref[...] = key
    value_out_ref[...] = dot(normed, value_ref[...], 1, 0).astype(BF)
    squares_ref[...] += two_rows(query * query, key * key)


def row_sums(array):
    ones = jnp.ones((8, array.shape[1]), F32)
    return lax.dot_general(
        ones,
        array,
        (((1,), (1,)), ((), ())),
        precision=lax.Precision.HIGHEST,
        preferred_element_type=F32,
    )


def two_rows(first, second):
    row = lax.broadcasted_iota(jnp.int32, (8, first.shape[0]), 0)
    return jnp.where(row == 0, row_sums(first), jnp.where(row == 1, row_sums(second), 0.0))


def norm_kernel(tokens_ref, gain_ref, out_ref):
    state = tokens_ref[...].astype(F32)
    scale = lax.rsqrt(jnp.mean(state * state, -1, keepdims=True) + EPSILON)
    out_ref[...] = (state * scale * gain_ref[...]).astype(BF)


def norm_all(tokens, gain, block):
    total, width = tokens.shape
    return pl.pallas_call(
        norm_kernel,
        grid=(total // block,),
        in_specs=[pl.BlockSpec((block, width), lambda i: (i, 0)), resident((1, width))],
        out_specs=pl.BlockSpec((block, width), lambda i: (i, 0)),
        out_shape=jax.ShapeDtypeStruct((total, width), BF),
        compiler_params=PARAMS,
        cost_estimate=cost(0, total * width * 4),
    )(tokens, gain[None])


def project(tokens, gain, w_query, w_key, w_value, block=256):
    count, width = tokens.shape
    local = w_query.shape[1]
    weight = pl.BlockSpec((width, block), lambda i: (0, i))
    out = pl.BlockSpec((count, block), lambda i: (0, i))
    return pl.pallas_call(
        front_kernel,
        grid=(local // block,),
        in_specs=[resident(tokens.shape), resident((1, width)), weight, weight, weight],
        out_specs=[resident((count, width)), out, out, out, resident((8, count))],
        out_shape=[
            jax.ShapeDtypeStruct((count, width), BF),
            jax.ShapeDtypeStruct((count, local), F32),
            jax.ShapeDtypeStruct((count, local), F32),
            jax.ShapeDtypeStruct((count, local), BF),
            jax.ShapeDtypeStruct((8, count), F32),
        ],
        compiler_params=PARAMS,
        cost_estimate=cost(3 * count * width * local, 6 * width * local),
    )(tokens, gain[None], w_query, w_key, w_value)


def scales_of(sums, full_width):
    return lax.rsqrt(sums.T / full_width + EPSILON)


def pack_kernel(full_width, query_ref, key_ref, value_ref, sums_ref, *refs):
    query_gain_ref, key_gain_ref, cos_ref, sin_ref, segment_ref, out_ref = refs
    parts, heads = out_ref.shape[0] // query_gain_ref.shape[0], query_gain_ref.shape[0]
    size = cos_ref.shape[1]
    count = cos_ref.shape[0]
    part = count // parts
    piece = part // 4
    scales = scales_of(sums_ref[...], full_width)
    for h in range(heads):
        span = slice(h * size, (h + 1) * size)

        def turned(ref, column, gain_ref):
            unit = ref[:, span] * scales[:, column : column + 1]
            vector = unit * gain_ref[pl.ds(h, 1), :]
            rolled = pltpu.roll(vector, size // 2, 1)
            return (vector * cos_ref[...] + rolled * sin_ref[...]).astype(BF)

        query = turned(query_ref, 0, query_gain_ref)
        key = turned(key_ref, 1, key_gain_ref)
        value = value_ref[:, span]
        for p in range(parts):
            place = h * parts + p
            for t in range(4):
                start = (t * parts + p) * piece
                out_ref[place, t * piece : (t + 1) * piece] = query[start : start + piece]
            out_ref[place, part : part + count] = key
            out_ref[place, part + count : part + 2 * count] = value
            out_ref[place, part + 2 * count :] = segment_ref[p]


def pack_heads(query, key, value, sums, query_gain, key_gain, cos, sin, segments, full_width):
    count = query.shape[0]
    size = cos.shape[1]
    parts = SPAN // query_gain.shape[0]
    return pl.pallas_call(
        functools.partial(pack_kernel, full_width),
        out_shape=jax.ShapeDtypeStruct(
            (SPAN, count // parts + 2 * count + segments.shape[1], size), BF
        ),
        compiler_params=PARAMS,
        cost_estimate=cost(0, 12 * query.size),
    )(query, key, value, sums, query_gain, key_gain, cos, sin, segments)


def head_views(got_ref, s, part, count):
    length = (s + 1) * count
    size = got_ref.shape[2]
    query = got_ref[s, :part]
    key = got_ref[: s + 1, part : part + count].reshape(length, size)
    value = got_ref[: s + 1, part + count : part + 2 * count].reshape(length, size)
    return query, key, value


def visible_pairs(got_ref, half, s, part, count):
    size = got_ref.shape[2]
    per_block = count // size
    first = part + 2 * count

    def rows(block):
        return got_ref[block, first : first + 16].astype(F32)

    own = jnp.broadcast_to(rows(s)[per_block : per_block + 1], (size, size)).T
    pieces = []
    for block in range(s + 1):
        values = rows(block)
        for r in range(per_block):
            pieces.append(own == values[r : r + 1])
    pieces = [jnp.where(piece, 1.0, 0.0) for piece in pieces]
    same = jnp.concatenate(pieces, 1) > 0.5
    query = lax.broadcasted_iota(jnp.int32, same.shape, 0)
    piece = part // 4
    query_pos = s * count + query // piece * (count // 4) + half * piece + query % piece
    return same & (lax.broadcasted_iota(jnp.int32, same.shape, 1) <= query_pos)


def attend_kernel(part, count, half_ref, got_ref, mix_ref, log_ref):
    half = half_ref[0]
    size = got_ref.shape[2]
    for s in range(SPAN):
        query, key, value = head_views(got_ref, s, part, count)
        visible = visible_pairs(got_ref, half, s, part, count)
        scores = jnp.where(visible, dot(query, key, 1, 1) / math.sqrt(size), NEGATIVE)
        top = jnp.max(scores, -1, keepdims=True)
        weights = jnp.where(visible, jnp.exp(scores - top), 0.0)
        total = jnp.sum(weights, -1, keepdims=True)
        mix_ref[s] = dot((weights / total).astype(BF), value, 1, 0).astype(BF)
        log_ref[s] = jnp.broadcast_to(top + jnp.log(total), (part, size))


def attend(got, half, part, count):
    size = got.shape[2]
    return pl.pallas_call(
        functools.partial(attend_kernel, part, count),
        in_specs=[
            pl.BlockSpec(memory_space=pltpu.SMEM),
            pl.BlockSpec(memory_space=pltpu.VMEM),
        ],
        out_shape=[
            jax.ShapeDtypeStruct((SPAN, part, size), BF),
            jax.ShapeDtypeStruct((SPAN, part, size), F32),
        ],
        compiler_params=PARAMS,
        cost_estimate=cost(SPAN * SPAN * part * count * size, 4 * got.size, SPAN * SPAN * part * count),
    )(half, got)


def attend_back_kernel(part, count, half_ref, got_ref, log_ref, grad_ref, out_ref, key_sum, value_sum):
    half = half_ref[0]
    size = got_ref.shape[2]
    root = math.sqrt(size)
    for s in reversed(range(SPAN)):
        length = (s + 1) * count
        query, key, value = head_views(got_ref, s, part, count)
        visible = visible_pairs(got_ref, half, s, part, count)
        scores = dot(query, key, 1, 1) / root - log_ref[s, :, :1]
        probs = jnp.where(visible, jnp.exp(jnp.where(visible, scores, 0.0)), 0.0)
        grad = grad_ref[s]
        probs_grad = dot(grad, value, 1, 1)
        inner = jnp.sum(probs * probs_grad, -1, keepdims=True)
        low = (probs * (probs_grad - inner)).astype(BF)
        out_ref[s, :part] = (dot(low, key, 1, 0) / root).astype(BF)
        key_back = dot(low, query, 0, 0)
        value_back = dot(probs.astype(BF), grad, 0, 0)
        if s == SPAN - 1:
            key_sum[...] = key_back
            value_sum[...] = value_back
        else:
            key_sum[:length] += key_back
            value_sum[:length] += value_back
    for s in range(SPAN):
        span = slice(s * count, (s + 1) * count)
        out_ref[s, part : part + count] = (key_sum[span] / root).astype(BF)
        out_ref[s, part + count :] = value_sum[span].astype(BF)


def attend_back(got, half, log_total, mix_grad, part, count):
    size = got.shape[2]
    vmem = pl.BlockSpec(memory_space=pltpu.VMEM)
    return pl.pallas_call(
        functools.partial(attend_back_kernel, part, count),
        in_specs=[pl.BlockSpec(memory_space=pltpu.SMEM), vmem, vmem, vmem],
        out_shape=jax.ShapeDtypeStruct((SPAN, part + 2 * count, size), BF),
        scratch_shapes=[pltpu.VMEM((SPAN * count, size), F32)] * 2,
        compiler_params=PARAMS,
        cost_estimate=cost(
            3 * SPAN * SPAN * part * count * size, 6 * got.size, SPAN * SPAN * part * count
        ),
    )(half, got, log_total, mix_grad)


def middle_kernel(experts, place_ref, tokens_ref, mix_ref, *refs):
    weights, refs = refs[:4], refs[4:]
    gain_ref, router_ref, routes_ref, resid_ref, probs_ref, chosen_ref = refs[:6]
    row_refs = refs[6:]
    step = pl.program_id(0)
    parts = mix_ref.shape[0] // 4

    @pl.when(step == 0)
    def _():
        resid_ref[...] = tokens_ref[...].astype(F32)

    total = resid_ref[...]
    for r in range(4):
        rows = [mix_ref[p * 4 + (r ^ place_ref[0])] for p in range(parts)]
        total = total + dot(jnp.concatenate(rows, 0), weights[r][...], 1, 0)
    resid_ref[...] = total

    @pl.when(step == pl.num_programs(0) - 1)
    def _():
        state = total
        scale = lax.rsqrt(jnp.mean(state * state, -1, keepdims=True) + EPSILON)
        normed = (state * scale * gain_ref[...]).astype(BF)
        logits = dot(normed, router_ref[...], 1, 0)
        lane = lax.broadcasted_iota(jnp.int32, logits.shape, 1)
        real = lane < experts
        top = jnp.max(jnp.where(real, logits, NEGATIVE), -1, keepdims=True)
        powers = jnp.exp(jnp.minimum(logits - top, 0.0))
        probs = powers / jnp.sum(jnp.where(real, powers, 0.0), -1, keepdims=True)
        routes = routes_ref[...]
        chosen = jnp.zeros(logits.shape, F32)
        for k in range(routes.shape[1]):
            column = routes[:, k : k + 1]
            hit = (lane == column) | (lane == column + experts)
            chosen = jnp.where(hit, 1.0, chosen)
        probs_ref[...] = jnp.where(real, probs, 0.0)
        chosen_ref[...] = jnp.where(real, chosen, 0.0)
        gates = probs * chosen
        high = gates.astype(BF).astype(F32)
        side = jnp.where(real, high, jnp.where(lane < 2 * experts, gates - high, 0.0))
        rows = jnp.concatenate([normed, side.astype(BF)], 1)
        begin = 0
        for ref in row_refs:
            ref[...] = rows[:, begin : begin + ref.shape[1]]
            begin += ref.shape[1]


def middle(tokens, mix, weights, gain, router_wide, routes, place, experts, groups):
    local, width = weights[0].shape
    size = mix.shape[2]
    heads = local // size
    own = tokens.shape[0] // 4
    wide = router_wide.shape[1]
    shape = jax.ShapeDtypeStruct
    return pl.pallas_call(
        functools.partial(middle_kernel, experts),
        grid_spec=pltpu.PrefetchScalarGridSpec(
            num_scalar_prefetch=1,
            grid=(heads,),
            in_specs=[
                pl.BlockSpec((own, width), lambda i, place_ref: (place_ref[0], 0)),
                pl.BlockSpec((mix.shape[0] // heads,) + mix.shape[1:], lambda i, *_: (i, 0, 0)),
            ]
            + [pl.BlockSpec((size, width), lambda i, *_: (i, 0))] * 4
            + [
                resident((1, width)),
                resident(router_wide.shape),
                pl.BlockSpec((own, routes.shape[1]), lambda i, place_ref: (place_ref[0], 0)),
            ],
            out_specs=[
                resident((own, width)),
                resident((own, wide)),
                resident((own, wide)),
            ]
            + [resident((own, columns)) for columns in groups],
        ),
        out_shape=[
            shape((own, width), F32),
            shape((own, wide), F32),
            shape((own, wide), F32),
        ]
        + [shape((own, columns), BF) for columns in groups],
        compiler_params=PARAMS,
        cost_estimate=cost(4 * own * width * local, 8 * width * local),
    )(place, tokens, mix, *weights, gain[None], router_wide, routes)


def middle_back_kernel(experts, place_ref, *refs):
    homes, weights, refs = refs[:6], refs[6:10], refs[10:]
    resid_ref, probs_ref, chosen_ref, gain_ref, router_ref, cotangent_ref = refs[:6]
    grad_ref, low_ref, small_ref, mix_ref = refs[6:]
    width = resid_ref.shape[1]

    @pl.when(pl.program_id(0) == 0)
    def _():
        parts = [a[...].astype(F32) + b[...].astype(F32) for a, b in zip(homes[:3], homes[3:])]
        home = jnp.concatenate(parts, 1)
        side = home[:, width:]
        lanes = side.shape[1]
        gate_grad = (side + pltpu.roll(side, lanes - experts, 1)) * chosen_ref[...]
        probs = probs_ref[...]
        inner = jnp.sum(probs * gate_grad, -1, keepdims=True)
        logit_low = (probs * (gate_grad - inner)).astype(BF)
        state = resid_ref[...]
        scale = lax.rsqrt(jnp.mean(state * state, -1, keepdims=True) + EPSILON)
        unit = state * scale
        mid_grad = home[:, :width] + dot(logit_low, router_ref[...], 1, 1)
        scaled = mid_grad * gain_ref[...]
        grad = cotangent_ref[...].astype(F32) + scale * (
            scaled - unit * jnp.mean(scaled * unit, -1, keepdims=True)
        )
        grad_ref[...] = grad
        low_ref[...] = grad.astype(BF)
        normed = (unit * gain_ref[...]).astype(BF)
        small_ref[:experts] = dot(logit_low, normed, 0, 0)[:experts]
        d_gain = jnp.sum(mid_grad * unit, 0, keepdims=True)
        row = lax.broadcasted_iota(jnp.int32, (8, width), 0)
        small_ref[experts:] = jnp.where(row == 0, d_gain, 0.0)

    low = low_ref[...]
    parts, piece = mix_ref.shape[0] // 4, mix_ref.shape[1]
    for r in range(4):
        product = dot(low, weights[r][...], 1, 1).astype(BF)
        for p in range(parts):
            mix_ref[p * 4 + (r ^ place_ref[0])] = product[p * piece : (p + 1) * piece]


def middle_back(homes, weights, resid, probs, chosen, gain, router_wide, cotangent, place, experts, size):
    own, width = resid.shape
    heads = weights[0].shape[0] // size
    parts = SPAN // heads
    shape = jax.ShapeDtypeStruct
    arrays = [resid, probs, chosen, gain[None], router_wide]
    return pl.pallas_call(
        functools.partial(middle_back_kernel, experts),
        grid_spec=pltpu.PrefetchScalarGridSpec(
            num_scalar_prefetch=1,
            grid=(heads,),
            in_specs=[resident(a.shape) for a in homes]
            + [pl.BlockSpec((size, width), lambda i, *_: (i, 0))] * 4
            + [resident(a.shape) for a in arrays]
            + [pl.BlockSpec((own, width), lambda i, place_ref: (place_ref[0], 0))],
            out_specs=[
                resident((own, width)),
                resident((own, width)),
                resident((experts + 8, width)),
                pl.BlockSpec((parts * 4, own // parts, size), lambda i, *_: (i, 0, 0)),
            ],
        ),
        out_shape=[
            shape((own, width), F32),
            shape((own, width), BF),
            shape((experts + 8, width), F32),
            shape((heads * parts * 4, own // parts, size), BF),
        ],
        compiler_params=PARAMS,
        cost_estimate=cost(4 * own * width * heads * size, 8 * heads * size * width),
    )(place, *homes, *weights, *arrays, cotangent)


def spread(block):
    side = swap(block, "tensor", 2)
    core = swap(block, "tensor", 1)
    return block, core, side, swap(side, "tensor", 1)


def out_grad_kernel(*refs):
    blocks, mixes, out_ref = refs[:4], refs[4:8], refs[8]
    lows = jnp.concatenate([ref[...] for ref in blocks], 0)
    own = blocks[0].shape[0]
    parts = own // mixes[0].shape[1]
    pieces = []
    for h in range(mixes[0].shape[0] // parts):
        rows = [ref[h * parts + p] for ref in mixes for p in range(parts)]
        pieces.append(dot(jnp.concatenate(rows, 0), lows, 0, 0).astype(BF))
    product = jnp.concatenate(pieces, 0)
    if len(out_ref.shape) == 2:
        out_ref[...] = product
        return
    rows, wide = out_ref.shape[1:]
    block = lows.shape[1]
    for q in range(wide // block):
        out_ref[0, :, q * block : (q + 1) * block] = product[q * rows : (q + 1) * rows]


def out_weight_grad(blocks, mixes, local, owners):
    own, width = blocks[0].shape
    block = width // owners
    if block % LANES == 0:
        rows = local // owners
        out = pl.BlockSpec((1, rows, width), lambda d: (d, 0, 0))
        shape = jax.ShapeDtypeStruct((owners, rows, width), BF)
    else:
        block = 4 * LANES
        out = pl.BlockSpec((local, block), lambda d: (0, d))
        shape = jax.ShapeDtypeStruct((local, width), BF)
    return pl.pallas_call(
        out_grad_kernel,
        grid=(width // block,),
        in_specs=[pl.BlockSpec((own, block), lambda d: (0, d))] * 4
        + [resident(mix.shape) for mix in mixes],
        out_specs=out,
        out_shape=shape,
        compiler_params=PARAMS,
        cost_estimate=cost(4 * own * local * width, local * width * 3),
    )(*blocks, *mixes)


def unturn_kernel(full_width, back_ref, query_ref, key_ref, sums_ref, *refs):
    query_gain_ref, key_gain_ref, cos_ref, sin_ref = refs[:4]
    query_out_ref, key_out_ref, value_out_ref, inner_ref, gains_ref = refs[4:]
    heads, size = query_gain_ref.shape
    parts = SPAN // heads
    count = cos_ref.shape[0]
    part = count // parts
    piece = part // 4
    scales = scales_of(sums_ref[...], full_width)
    inner = [0.0, 0.0]
    for h in range(heads):
        span = slice(h * size, (h + 1) * size)
        first = h * parts
        query = jnp.concatenate(
            [
                back_ref[first + p, t * piece : (t + 1) * piece]
                for t in range(4)
                for p in range(parts)
            ],
            0,
        )
        key = sum(back_ref[first + p, part : part + count].astype(F32) for p in range(parts))
        value = sum(back_ref[first + p, part + count :].astype(F32) for p in range(parts))
        value_out_ref[:, span] = value.astype(BF)
        key = key.astype(BF)
        items = ((query, query_ref, query_gain_ref, query_out_ref), (key, key_ref, key_gain_ref, key_out_ref))
        for n, (grad, raw_ref, gain_ref, out_ref) in enumerate(items):
            grad = grad.astype(F32)
            gain_in = grad * cos_ref[...] - pltpu.roll(grad, size // 2, 1) * sin_ref[...]
            unit = raw_ref[:, span] * scales[:, n : n + 1]
            gains_ref[n * heads + h] = jnp.broadcast_to(
                jnp.sum(gain_in * unit, 0, keepdims=True), (8, size)
            )
            scaled = gain_in * gain_ref[pl.ds(h, 1), :]
            out_ref[:, span] = scaled
            inner[n] = inner[n] + scaled * unit
    inner_ref[...] = two_rows(inner[0], inner[1])


def unturn(back, query, key, sums, query_gain, key_gain, cos, sin, full_width):
    count, local = query.shape
    heads, size = query_gain.shape
    shape = jax.ShapeDtypeStruct
    return pl.pallas_call(
        functools.partial(unturn_kernel, full_width),
        out_shape=[
            shape((count, local), F32),
            shape((count, local), F32),
            shape((count, local), BF),
            shape((8, count), F32),
            shape((2 * heads, 8, size), F32),
        ],
        compiler_params=PARAMS,
        cost_estimate=cost(0, 24 * query.size),
    )(back, query, key, sums, query_gain, key_gain, cos, sin)


def columns_kernel(full_width, *refs):
    query_scaled_ref, key_scaled_ref, value_ref, query_ref, key_ref, sums_ref, inner_ref = refs[:7]
    query_low_ref, key_low_ref, out_ref = refs[7:]
    owners, rows, _ = out_ref.shape
    rows = rows // 3
    scales = scales_of(sums_ref[...], full_width)
    means = inner_ref[...].T / full_width
    items = ((query_scaled_ref, query_ref, query_low_ref), (key_scaled_ref, key_ref, key_low_ref))
    lows = []
    for n, (scaled_ref, raw_ref, low_ref) in enumerate(items):
        scale = scales[:, n : n + 1]
        unit = raw_ref[...] * scale
        low = (scale * (scaled_ref[...] - unit * means[:, n : n + 1])).astype(BF)
        low_ref[...] = low
        lows.append(low)
    for n, low in enumerate(lows + [value_ref[...]]):
        turned = low.T
        for d in range(owners):
            out_ref[d, n * rows : (n + 1) * rows] = turned[d * rows : (d + 1) * rows]


def columns_of(query_scaled, key_scaled, value, query, key, sums, inner, full_width, owners):
    count, local = query.shape
    low = jax.ShapeDtypeStruct((count, local), BF)
    return pl.pallas_call(
        functools.partial(columns_kernel, full_width),
        out_shape=[low, low, jax.ShapeDtypeStruct((owners, 3 * local // owners, count), BF)],
        compiler_params=PARAMS,
        cost_estimate=cost(0, 24 * query.size),
    )(query_scaled, key_scaled, value, query, key, sums, inner)


def input_kernel(own, place_ref, *refs):
    lows, weights, kept_ref, sent_ref = refs[:3], refs[3:6], refs[6], refs[7]
    place = place_ref[0]
    total = None
    for low_ref, weight_ref in zip(lows, weights):
        rows = [
            low_ref[pl.ds(pl.multiple_of((r ^ place) * own, own), own), :] for r in range(4)
        ]
        product = dot(jnp.concatenate(rows, 0), weight_ref[...], 1, 1)
        total = product if total is None else total + product
    total = total.astype(BF)
    for r in range(4):
        ref = sent_ref if r % 2 else kept_ref
        ref[r // 2] = total[r * own : (r + 1) * own]


def input_back(lows, weights, place, own, block=512):
    width, local = weights[0].shape
    out = pl.BlockSpec((2, own, block), lambda d, *_: (0, 0, d))
    shape = jax.ShapeDtypeStruct((2, own, width), BF)
    return pl.pallas_call(
        functools.partial(input_kernel, own),
        grid_spec=pltpu.PrefetchScalarGridSpec(
            num_scalar_prefetch=1,
            grid=(width // block,),
            in_specs=[resident(lows[0].shape)] * 3
            + [pl.BlockSpec((block, local), lambda d, *_: (d, 0))] * 3,
            out_specs=[out, out],
        ),
        out_shape=[shape, shape],
        compiler_params=PARAMS,
        cost_estimate=cost(12 * own * local * width, local * width * 7),
    )(place, *lows, *weights)


def last_kernel(place_ref, tokens_ref, *refs):
    kept_ref, core_ref, side_ref, grad_ref, gain_ref, small_ref, out_ref = refs
    own = grad_ref.shape[0]
    extra = out_ref.shape[0] - own
    used = small_ref.shape[0]
    state = tokens_ref[...].astype(F32)
    scale = lax.rsqrt(jnp.mean(state * state, -1, keepdims=True) + EPSILON)
    unit = state * scale
    grad = kept_ref[0].astype(F32) + core_ref[0].astype(F32) + side_ref[...].astype(F32)
    scaled = grad * gain_ref[...]
    out = grad_ref[...] + scale * (scaled - unit * jnp.mean(scaled * unit, -1, keepdims=True))
    out_ref[:own] = out.astype(BF)
    d_gain = jnp.sum(grad * unit, 0, keepdims=True)
    row = lax.broadcasted_iota(jnp.int32, (8, state.shape[1]), 0)
    gains = small_ref[used - 8 :] + jnp.where(row == 1, d_gain, 0.0)
    rows = [small_ref[: used - 8], gains]
    if extra > used:
        rows.append(jnp.zeros((extra - used, state.shape[1]), F32))
    out_ref[own:] = jnp.concatenate(rows, 0).astype(BF)


def last(tokens, kept, core, side, grad, gain, small, place):
    own, width = side.shape
    arrays = [kept, core, side, grad, gain[None], small]
    rows = own + -(-small.shape[0] // 16) * 16
    return pl.pallas_call(
        last_kernel,
        grid_spec=pltpu.PrefetchScalarGridSpec(
            num_scalar_prefetch=1,
            grid=(1,),
            in_specs=[pl.BlockSpec((own, width), lambda i, place_ref: (place_ref[0], 0))]
            + [resident(a.shape) for a in arrays],
            out_specs=resident((rows, width)),
        ),
        out_shape=jax.ShapeDtypeStruct((rows, width), BF),
        compiler_params=PARAMS,
        cost_estimate=cost(0, own),
    )(place, tokens, *arrays)


def tile_kernel(rows_ref, out_ref):
    rows, wide = rows_ref.shape
    block = out_ref.shape[1]
    for q in range(wide // block):
        out_ref[q * rows : (q + 1) * rows] = rows_ref[:, q * block : (q + 1) * block].astype(F32)


def tile_rows(rows, local):
    return pl.pallas_call(
        tile_kernel,
        out_shape=jax.ShapeDtypeStruct((local, rows.size // local), F32),
        compiler_params=PARAMS,
        cost_estimate=cost(0, rows.size * 6),
    )(rows)


def join_kernel(own, place_ref, *refs):
    out_ref = refs[4]
    for r in range(4):
        start = pl.multiple_of((r ^ place_ref[0]) * own, own)
        out_ref[pl.ds(start, own), :] = refs[r][:own].astype(out_ref.dtype)


def join_blocks(blocks, place, own, kind):
    width = blocks[0].shape[1]
    vmem = pl.BlockSpec(memory_space=pltpu.VMEM)
    return pl.pallas_call(
        functools.partial(join_kernel, own),
        in_specs=[pl.BlockSpec(memory_space=pltpu.SMEM)] + [vmem] * 4,
        out_shape=jax.ShapeDtypeStruct((4 * own, width), kind),
        compiler_params=PARAMS,
        cost_estimate=cost(0, own),
    )(place, *blocks)


def weights_kernel(columns_ref, rows_ref, small_ref, out_ref):
    owners, columns, count = columns_ref.shape
    total = None
    for s in range(owners):
        product = dot(columns_ref[s], rows_ref[pl.ds(s * count, count), :], 1, 0)
        total = product if total is None else total + product
    out_ref[0, :columns] = total.astype(BF)
    out_ref[0, columns:] = small_ref[0]


def weight_columns(columns, rows, small):
    owners, count3, count = columns.shape
    width = rows.shape[1]
    slab = width // owners
    extra = small.shape[1]
    return pl.pallas_call(
        weights_kernel,
        grid=(owners,),
        in_specs=[
            resident(columns.shape),
            pl.BlockSpec((rows.shape[0], slab), lambda d: (0, d)),
            pl.BlockSpec((1, extra, slab), lambda d: (d, 0, 0)),
        ],
        out_specs=pl.BlockSpec((1, count3 + extra, slab), lambda d: (d, 0, 0)),
        out_shape=jax.ShapeDtypeStruct((owners, count3 + extra, slab), BF),
        compiler_params=PARAMS,
        cost_estimate=cost(rows.shape[0] * width * count3, rows.size * 2),
    )(columns, rows, small)


def unpack_kernel(given_ref, *outs):
    owners, _, slab = given_ref.shape
    local = outs[0].shape[1]
    rows = local // owners
    group = LANES // rows
    for n, out_ref in enumerate(outs[:3]):
        for s in range(0, owners, group):
            pieces = [given_ref[s + g, n * rows : (n + 1) * rows] for g in range(group)]
            turned = jnp.concatenate(pieces, 0).astype(F32).T
            out_ref[:, s * rows : (s + group) * rows] = turned
    total = given_ref[0, 3 * rows :].astype(F32)
    for s in range(1, owners):
        total = total + given_ref[s, 3 * rows :].astype(F32)
    outs[3][...] = total


def unpack(given, local):
    owners, rows, slab = given.shape
    extra = rows - 3 * local // owners
    weight = jax.ShapeDtypeStruct((slab, local), F32)
    return pl.pallas_call(
        unpack_kernel,
        out_shape=[weight, weight, weight, jax.ShapeDtypeStruct((extra, slab), F32)],
        compiler_params=PARAMS,
        cost_estimate=cost(0, given.size * 6),
    )(given)


def per_device(
    tokens,
    segment_ids,
    routes,
    norm1_gain,
    w_query,
    w_key,
    w_value,
    query_gain,
    key_gain,
    w_out,
    norm2_gain,
    w_router,
    w_gate,
    w_up,
    w_down,
    cotangent,
):
    tok_count, model_width = tokens.shape
    heads_here, head_size = query_gain.shape
    local_width = heads_here * head_size
    tensor_count = lax.axis_size("tensor")
    full_width = local_width * tensor_count
    experts = w_router.shape[1]
    owners = lax.axis_size("dp")
    dp_place = lax.axis_index("dp")
    tensor_place = lax.axis_index("tensor")
    own = tok_count // tensor_count
    parts = SPAN // heads_here
    part = tok_count // parts
    groups = [list(range(g, g + SPAN)) for g in range(0, owners, SPAN)]
    place = tensor_place.astype(jnp.int32).reshape(1)
    index = jnp.stack([dp_place, tensor_place]).astype(jnp.int32)
    half = (dp_place % SPAN % parts).astype(jnp.int32).reshape(1)

    def mine(array):
        return lax.dynamic_slice_in_dim(array, tensor_place * own, own, 0)

    def trade(array):
        return lax.all_to_all(
            array, "dp", split_axis=0, concat_axis=0, tiled=True, axis_index_groups=groups
        )

    def trade_every(array):
        wide = None
        if owners > SPAN:
            count = SPAN * tensor_count
            wide = [list(range(g, g + count)) for g in range(0, owners * tensor_count, count)]
        return lax.all_to_all(
            array, EVERY, split_axis=0, concat_axis=0, tiled=True, axis_index_groups=wide
        )

    def sum_tensor(kept, sent):
        core = swap(sent, "tensor", 1)
        given = (kept[1].astype(F32) + core[1].astype(F32)).astype(BF)
        return kept, core, swap(given, "tensor", 2)

    out_grad_all = lax.all_gather(mine(cotangent), EVERY, axis=0, tiled=True)
    both_turned, down_turned = turn_weights(w_gate, w_up, w_down)
    side_width = -(-2 * experts // LANES) * LANES
    router_wide = jnp.pad(
        jnp.concatenate([w_router, w_router], 1), ((0, 0), (0, side_width - 2 * experts))
    )
    local_pos = jnp.arange(tok_count, dtype=jnp.int32)
    positions = (dp_place % SPAN * tok_count + local_pos).astype(F32)
    cos_table, sin_table = rope_tables(positions, head_size)
    segment_low = segment_ids.astype(BF)
    segment_parts = segment_low.reshape(tensor_count, parts, -1).transpose(1, 0, 2)
    segment_rows = jnp.concatenate(
        [
            jnp.broadcast_to(segment_low.reshape(1, -1, head_size), (parts, tok_count // head_size, head_size)),
            segment_parts.reshape(parts, 1, part),
        ],
        1,
    )
    segment_rows = jnp.pad(segment_rows, ((0, 0), (0, 16 - segment_rows.shape[1]), (0, 0)))

    normed_in, query_raw, key_raw, value_att, squares = project(
        tokens, norm1_gain, w_query, w_key, w_value
    )
    squares, w_out = lax.optimization_barrier((total_tensor(squares), w_out))
    out_weights = spread(w_out)
    packed = pack_heads(
        query_raw,
        key_raw,
        value_att,
        squares,
        query_gain,
        key_gain,
        cos_table,
        sin_table,
        segment_rows,
        full_width,
    )
    got = trade(packed)
    mix_heads, log_total = attend(got, half, part, tok_count)
    pieces_count, piece = SPAN * tensor_count, own // parts
    mix, both_turned, down_turned = lax.optimization_barrier(
        (
            trade_every(mix_heads.reshape(pieces_count, piece, head_size)),
            both_turned,
            down_turned,
        )
    )
    lanes = -(-(model_width + side_width) // (3 * LANES)) * LANES
    resid_state, router_probs, chosen, *rows_own = middle(
        tokens,
        mix,
        out_weights,
        norm2_gain,
        router_wide,
        routes,
        place,
        experts,
        [lanes, lanes, model_width + side_width - 2 * lanes],
    )
    bits = owners.bit_length() - 1
    first_three = [("tensor", 2), ("dp", 1), ("dp", 2)]
    rest = [("dp", 1 << b) for b in range(2, bits)]
    orders = [first_three[g:] + first_three[:g] + rest for g in range(3)]
    pieces, names, back_all, tokens_own = gather_every(
        rows_own,
        [order[::-1] for order in orders],
        hidden_back(out_grad_all, down_turned),
        mine(tokens),
    )
    tokens_all = lax.all_gather(tokens_own, EVERY, axis=0, tiled=True)
    (rows_all, hid, hid_turned, glow, ulow), kept_groups, sent_groups = expert_rows(
        pieces, names, back_all, w_gate, w_up, both_turned, index, experts, tok_count
    )
    out_kept, out_sent = expert_out(hid, w_down, place % 2, tok_count)
    d_w_gate = over_rows(rows_all, glow, w_gate.shape)

    def add_core(kept_rows, sent_rows):
        core_rows = swap(sent_rows, "tensor", 1)
        return ((kept_rows.astype(F32) + core_rows.astype(F32)).astype(BF),)

    homes, out_part = sum_every(kept_groups, sent_groups, orders, (out_kept, out_sent), add_core)
    core_groups = [
        [d * tensor_count + x * 2 + c for d in range(owners) for x in range(2)] for c in range(2)
    ]
    expert_full = lax.psum_scatter(
        out_part.reshape(-1, model_width),
        EVERY,
        scatter_dimension=0,
        tiled=True,
        axis_index_groups=core_groups,
    )
    d_w_down = turned_rows(hid_turned, out_grad_all).reshape(w_down.shape)
    d_w_up = over_rows(rows_all, ulow, w_up.shape)
    normed_in_all = norm_all(tokens_all, norm1_gain, tok_count)

    resid_grad, resid_low, small, mix_grad = middle_back(
        [home[0] for home in homes] + [home[1] for home in homes],
        out_weights,
        resid_state,
        router_probs,
        chosen,
        norm2_gain,
        router_wide,
        cotangent,
        place,
        experts,
        head_size,
    )
    mix_grad, d_w_up = lax.optimization_barrier((trade_every(mix_grad), d_w_up))
    mix_by_block = mix.reshape(SPAN, tensor_count, piece, head_size)
    mix_by_block, mix_grad = lax.optimization_barrier((mix_by_block, mix_grad))
    mixes = [
        lax.dynamic_index_in_dim(mix_by_block, tensor_place ^ r, 1, keepdims=False)
        for r in range(4)
    ]
    mixes = mixes[:1] + [swap(mixes[r], "tensor", r) for r in range(1, 4)]
    lows = [resid_low] + [swap(resid_low, "tensor", r) for r in range(1, 4)]
    d_out = out_weight_grad(lows, mixes, local_width, owners)
    back, d_w_down, normed_in_all, d_out = lax.optimization_barrier(
        (
            trade(
                attend_back(
                    got,
                    half,
                    log_total,
                    mix_grad.reshape(SPAN, part, head_size),
                    part,
                    tok_count,
                )
            ),
            d_w_down,
            normed_in_all,
            d_out,
        )
    )
    query_scaled, key_scaled, value_low, inner, gains = unturn(
        back, query_raw, key_raw, squares, query_gain, key_gain, cos_table, sin_table, full_width
    )
    inner = total_tensor(inner)
    query_low, key_low, columns = columns_of(
        query_scaled, key_scaled, value_low, query_raw, key_raw, squares, inner, full_width, owners
    )
    columns, expert_full, d_out = lax.optimization_barrier((columns, expert_full, d_out))
    model_slice = model_width // owners
    if model_slice % LANES == 0:
        d_out = lax.psum_scatter(d_out, "dp", scatter_dimension=0, tiled=True)[0]
        d_out = tile_rows(d_out, local_width)
    else:
        d_out = lax.psum_scatter(d_out, "dp", scatter_dimension=1, tiled=True).astype(F32)
    block_own = (resid_state + expert_full.astype(F32)).astype(BF)
    out_blocks = spread(block_own)

    columns = lax.all_to_all(columns, "dp", split_axis=0, concat_axis=0, tiled=True)
    block_output = join_blocks(out_blocks, place, own, BF)
    kept, core, side = sum_tensor(
        *input_back(
            (query_low, key_low, value_low), (w_query, w_key, w_value), place, own
        )
    )
    input_blocks = spread(
        last(tokens, kept, core, side, resid_grad, norm1_gain, small, place)
    )
    input_grad = join_blocks(input_blocks, place, own, F32)

    head_slice = head_size // owners
    slice_width = local_width // owners
    gain_count = 2 * heads_here * head_slice
    gain_rows = -(-gain_count // model_slice)
    gains = gains[:, 0].reshape(2 * heads_here, owners, head_slice).transpose(1, 0, 2)
    gains = jnp.pad(
        gains.reshape(owners, gain_count), ((0, 0), (0, gain_rows * model_slice - gain_count))
    ).reshape(owners, gain_rows, model_slice)
    shared = sum(block[own : own + experts + 2].astype(F32) for block in input_blocks)
    shared = shared.reshape(experts + 2, owners, model_slice).transpose(1, 0, 2)
    extra = jnp.concatenate([shared, gains], 1).astype(BF)
    extra = jnp.pad(extra, ((0, 0), (0, -extra.shape[1] % 16), (0, 0)))
    if model_slice % LANES == 0:
        final = weight_columns(columns, normed_in_all, extra)
    else:
        columns = columns.transpose(1, 0, 2).reshape(3 * slice_width, owners * tok_count)
        final = dot(columns, normed_in_all, 1, 0).reshape(3 * slice_width, owners, model_slice)
        final = jnp.concatenate([final.transpose(1, 0, 2).astype(BF), extra], 1)
    final, block_output, input_grad = lax.optimization_barrier(
        (
            lax.all_to_all(final, "dp", split_axis=0, concat_axis=0, tiled=True),
            block_output,
            input_grad,
        )
    )
    *weights, extra = unpack(final, local_width)
    gains = extra[experts + 2 : experts + 2 + gain_rows].reshape(-1)[:gain_count]
    gains = gains.reshape(2, heads_here, head_slice)

    return (
        block_output,
        input_grad,
        extra[experts + 1],
        weights[0],
        weights[1],
        weights[2],
        gains[0],
        gains[1],
        d_out,
        extra[experts],
        extra[:experts].T,
        d_w_gate,
        d_w_up,
        d_w_down,
    )


def solution(mesh):
    in_specs = (
        P("dp", None),
        P("dp"),
        P("dp", None),
        P(),
        P(None, "tensor"),
        P(None, "tensor"),
        P(None, "tensor"),
        P("tensor", None),
        P("tensor", None),
        P("tensor", None),
        P(),
        P(),
        P("dp", None, "tensor"),
        P("dp", None, "tensor"),
        P("dp", "tensor", None),
        P("dp", None),
    )
    out_specs = (
        P("dp", None),
        P("dp", None),
        P("dp"),
        P("dp", "tensor"),
        P("dp", "tensor"),
        P("dp", "tensor"),
        P("tensor", "dp"),
        P("tensor", "dp"),
        P("tensor", "dp"),
        P("dp"),
        P("dp", None),
        P("dp", None, "tensor"),
        P("dp", None, "tensor"),
        P("dp", "tensor", None),
    )
    return jax.shard_map(
        per_device, mesh=mesh, in_specs=in_specs, out_specs=out_specs, check_vma=False
    )
```

```python
import functools
import math

import jax
import jax.numpy as jnp
from jax import lax
from jax.experimental import pallas as pl
from jax.experimental.pallas import tpu as pltpu
from jax.sharding import PartitionSpec as P

SPAN = 8


EPSILON = 1e-05
ROPE_BASE = 10000.0
NEGATIVE = -1e30
BF = jnp.bfloat16
F32 = jnp.float32
EVERY = ("dp", "tensor")
VMEM_LIMIT = 56 * 1024 * 1024
LANES = 128


def rope_tables(positions, head_size):
    frequency = ROPE_BASE ** (-jnp.arange(0, head_size, 2, dtype=jnp.float32) / head_size)
    angles = positions[:, None] * frequency[None, :]
    cosine, sine = jnp.cos(angles), jnp.sin(angles)
    return jnp.concatenate([cosine, cosine], -1), jnp.concatenate([-sine, sine], -1)


def dot(left_side, right_side, left_dim, right_dim):
    return lax.dot_general(
        left_side,
        right_side,
        (((left_dim,), (right_dim,)), ((), ())),
        preferred_element_type=jnp.float32,
    )


def swap(array, axis, bit):
    count = lax.axis_size(axis)
    return lax.ppermute(array, axis, [(i, i ^ bit) for i in range(count)])


def total_tensor(array):
    others = [swap(array, "tensor", r) for r in range(1, 4)]
    return (array + others[0]) + (others[1] + others[2])


def resident(shape):
    return pl.BlockSpec(shape, lambda *_: (0,) * len(shape), pipeline_mode=pl.Buffered(1))


def cost(macs, size, transcendentals=0):
    return pl.CostEstimate(flops=2 * macs, bytes_accessed=size, transcendentals=transcendentals)


PARAMS = pltpu.CompilerParams(vmem_limit_bytes=VMEM_LIMIT)


def turn_kernel(gate_ref, up_ref, down_ref, both_ref, down_out_ref):
    count, _, hidden = gate_ref.shape
    for e in range(count):
        both_ref[pl.ds(e * hidden, hidden), :] = gate_ref[e].T
        both_ref[pl.ds((count + e) * hidden, hidden), :] = up_ref[e].T
        down_out_ref[:, pl.ds(e * hidden, hidden)] = down_ref[e].T


def turn_weights(w_gate, w_up, w_down, block=256):
    count, width, hidden = w_gate.shape
    mid = count * hidden
    rows = pl.BlockSpec((count, block, hidden), lambda d: (0, d, 0))
    return pl.pallas_call(
        turn_kernel,
        grid=(width // block,),
        in_specs=[rows, rows, pl.BlockSpec((count, hidden, block), lambda d: (0, 0, d))],
        out_specs=[
            pl.BlockSpec((2 * mid, block), lambda d: (0, d)),
            pl.BlockSpec((block, mid), lambda d: (d, 0)),
        ],
        out_shape=[
            jax.ShapeDtypeStruct((2 * mid, width), BF),
            jax.ShapeDtypeStruct((width, mid), BF),
        ],
        compiler_params=PARAMS,
        cost_estimate=cost(0, 12 * mid * width),
    )(w_gate, w_up, w_down)


def hidden_back_kernel(grad_ref, down_ref, out_ref):
    out_ref[...] = dot(grad_ref[...], down_ref[...], 1, 0)


def hidden_back(grad_all, down_turned, block=256):
    width, mid = down_turned.shape
    total = grad_all.shape[0]
    return pl.pallas_call(
        hidden_back_kernel,
        grid=(total // block,),
        in_specs=[pl.BlockSpec((block, width), lambda i: (i, 0)), resident(down_turned.shape)],
        out_specs=pl.BlockSpec((block, mid), lambda i: (i, 0)),
        out_shape=jax.ShapeDtypeStruct((total, mid), F32),
        compiler_params=PARAMS,
        cost_estimate=cost(total * width * mid, total * width * 3),
    )(grad_all, down_turned)


def expert_kernel(experts, axes, index_ref, *refs):
    pieces, refs = (refs[:3], refs[3:6]), refs[6:]
    back_ref, gate_ref, up_ref, both_ref, rows_ref = refs[:5]
    hid_ref, hid_turned_ref, glow_ref, ulow_ref = refs[5:9]
    kept_refs, sent_refs, low_ref, side_ref = refs[9:12], refs[12:15], refs[15], refs[16]
    count, width, hidden_size = gate_ref.shape
    mid = count * hidden_size
    own = kept_refs[0].shape[2]
    starts = [pl.multiple_of((r ^ index_ref[1]) * own, own) for r in range(4)]
    for r in range(4):
        begin = 0
        for piece, axis in zip(pieces[r % 2], axes):
            place = [0] * (len(piece.shape) - 2)
            place[axis] = r // 2
            columns = piece.shape[-1]
            end = min(begin + columns, width)
            value = piece[tuple(place)]
            rows_ref[pl.ds(starts[r], own), begin:end] = value[:, : end - begin]
            if end - begin < columns:
                side_ref[pl.ds(starts[r], own), :] = value[:, end - begin :]
            begin = end
    rows = rows_ref[...]
    side = side_ref[...].astype(F32)
    lane = lax.broadcasted_iota(jnp.int32, side.shape, 1)
    dots = jnp.zeros(side.shape, F32)
    for e in range(count):
        column = index_ref[0] * count + e
        gate = jnp.sum(
            jnp.where((lane == column) | (lane == experts + column), side, 0.0), -1, keepdims=True
        )
        span = pl.ds(e * hidden_size, hidden_size)
        gate_pre = dot(rows, gate_ref[e], 1, 0)
        up_pre = dot(rows, up_ref[e], 1, 0)
        out_back = back_ref[:, span]
        sigma = 1.0 / (1.0 + jnp.exp(-gate_pre))
        silu = gate_pre * sigma
        hidden = silu * up_pre
        inner = jnp.sum(hidden * out_back, -1, keepdims=True)
        high = inner.astype(BF).astype(F32)
        dots = jnp.where(lane == column, high, dots)
        dots = jnp.where(lane == experts + column, inner - high, dots)
        hidden_low = (gate * hidden).astype(BF)
        hidden_grad = gate * out_back
        glow = (hidden_grad * up_pre * sigma * (1.0 + gate_pre * (1.0 - sigma))).astype(BF)
        ulow = (hidden_grad * silu).astype(BF)
        hid_ref[:, span] = hidden_low
        hid_turned_ref[span, :] = hidden_low.T
        glow_ref[:, span] = glow
        ulow_ref[:, span] = ulow
        low_ref[:, span] = glow
        low_ref[:, pl.ds(mid + e * hidden_size, hidden_size)] = ulow
    low_ref[:, 2 * mid :] = dots.astype(BF)
    low = jnp.concatenate([low_ref[pl.ds(start, own), :] for start in starts], 0)
    begin = 0
    for kept_ref, sent_ref in zip(kept_refs, sent_refs):
        columns = kept_ref.shape[3]
        end = min(begin + columns, width)
        back = dot(low[:, : 2 * mid], both_ref[:, begin:end], 1, 0).astype(BF)
        if end - begin < columns:
            back = jnp.concatenate([back, low[:, 2 * mid :]], 1)
        begin = end
        for r in range(4):
            ref = sent_ref if r % 2 else kept_ref
            ref[0, r // 2] = back[r * own : (r + 1) * own]


def expert_rows(pieces, names, back_all, w_gate, w_up, both_turned, index, experts, block):
    count, width, hidden = w_gate.shape
    total, mid = back_all.shape
    owners = total // block
    groups = [piece.shape[-1] for piece in pieces[0]]
    side = sum(groups) - width

    def rows(columns):
        return pl.BlockSpec((block, columns), lambda i, index_ref: (i ^ index_ref[0], 0))

    def shape(columns):
        return jax.ShapeDtypeStruct((total, columns), BF)

    def given(columns, order):
        sizes = tuple(1 if axis == "dp" else 2 for axis, _ in order)

        def place(i, *_):
            return tuple(i // bit % 2 if axis == "dp" else 0 for axis, bit in order) + (0, 0)

        return pl.BlockSpec(sizes + (block // 4, columns), place)

    def part(columns):
        return pl.BlockSpec((1, 2, block // 4, columns), lambda i, *_: (i, 0, 0, 0))

    def part_shape(columns):
        return jax.ShapeDtypeStruct((owners, 2, block // 4, columns), BF)

    given_specs = [given(columns, order) for columns, order in zip(groups, names)]
    axes = [[axis for axis, _ in order].index("tensor") for order in names]
    outs = pl.pallas_call(
        functools.partial(expert_kernel, experts, axes),
        grid_spec=pltpu.PrefetchScalarGridSpec(
            num_scalar_prefetch=1,
            grid=(owners,),
            in_specs=given_specs * 2
            + [
                rows(mid),
                resident(w_gate.shape),
                resident(w_up.shape),
                resident(both_turned.shape),
            ],
            out_specs=[
                rows(width),
                rows(mid),
                pl.BlockSpec((mid, block), lambda i, index_ref: (0, i ^ index_ref[0])),
                rows(mid),
                rows(mid),
            ]
            + [part(columns) for columns in groups] * 2,
            scratch_shapes=[pltpu.VMEM((block, 2 * mid + side), BF), pltpu.VMEM((block, side), BF)],
        ),
        out_shape=[
            shape(width),
            shape(mid),
            jax.ShapeDtypeStruct((mid, total), BF),
            shape(mid),
            shape(mid),
        ]
        + [part_shape(columns) for columns in groups] * 2,
        compiler_params=PARAMS,
        cost_estimate=cost(4 * total * width * mid, total * width * 8, total * mid),
    )(index, *pieces[0], *pieces[1], back_all, w_gate, w_up, both_turned)
    return outs[:5], outs[5:8], outs[8:]


def gather_every(groups, orders, beside, later):
    totals, names = list(groups), [[] for _ in groups]
    for step in range(len(orders[0])):
        if step == len(orders[0]) - 1:
            totals, later = lax.optimization_barrier((totals, later))
        others = [swap(total, *order[step]) for total, order in zip(totals, orders)]
        if step == len(orders[0]) - 1:
            others, beside = lax.optimization_barrier((others, beside))
        totals = [jnp.stack([total, other]) for total, other in zip(totals, others)]
        for name, order in zip(names, orders):
            name.insert(0, order[step])
    return (totals, [swap(total, "tensor", 1) for total in totals]), names, beside, later


def sum_every(kept, sent, orders, beside, finish):
    bits = lax.axis_size("dp").bit_length() - 1
    totals, names = [], []
    for kept_group, sent_group in zip(kept, sent):
        own, columns = kept_group.shape[2:]
        total = kept_group.astype(F32) + swap(sent_group, "tensor", 1).astype(F32)
        totals.append(total.astype(BF).reshape((2,) * (bits + 1) + (own, columns)))
        names.append([("dp", 1 << (bits - 1 - i)) for i in range(bits)] + [("tensor", 2)])
    for step in range(bits + 1):
        halves, others = [], []
        for total, left, order in zip(totals, names, orders):
            axis = left.index(order[step])
            left.pop(axis)
            given = lax.index_in_dim(total, 1, axis, keepdims=False)
            halves.append(lax.index_in_dim(total, 0, axis, keepdims=False))
            others.append(swap(given, *order[step]))
        if step == 0:
            others, beside = lax.optimization_barrier((others, beside))
        if step == bits:
            others, beside = lax.optimization_barrier((others, finish(*beside)))
        totals = [(a.astype(F32) + b.astype(F32)).astype(BF) for a, b in zip(halves, others)]
    return list(zip(halves, others)), *beside


def out_kernel(core_ref, hid_ref, down_ref, kept_ref, sent_ref):
    count, hidden, _ = down_ref.shape
    own = kept_ref.shape[1]
    rows = []
    for r in range(4):
        start = pl.multiple_of((r // 2 * 2 + ((r % 2) ^ core_ref[0])) * own, own)
        rows.append(hid_ref[pl.ds(start, own), :])
    weight = down_ref[...].reshape(count * hidden, -1)
    out = dot(jnp.concatenate(rows, 0), weight, 1, 0).astype(BF)
    for r in range(4):
        ref = sent_ref if r % 2 else kept_ref
        ref[r // 2] = out[r * own : (r + 1) * own]


def expert_out(hid, w_down, core, block):
    count, hidden, width = w_down.shape
    total = hid.shape[0]
    out = pl.BlockSpec((2, block // 4, width), lambda i, *_: (i, 0, 0))
    shape = jax.ShapeDtypeStruct((total // block * 2, block // 4, width), BF)
    return pl.pallas_call(
        out_kernel,
        grid_spec=pltpu.PrefetchScalarGridSpec(
            num_scalar_prefetch=1,
            grid=(total // block,),
            in_specs=[
                pl.BlockSpec((block, count * hidden), lambda i, *_: (i, 0)),
                resident(w_down.shape),
            ],
            out_specs=[out, out],
        ),
        out_shape=[shape, shape],
        compiler_params=PARAMS,
        cost_estimate=cost(total * width * count * hidden, total * width * 3),
    )(core, hid, w_down)


def over_kernel(left_ref, right_ref, out_ref):
    count, _, hidden = out_ref.shape
    product = dot(left_ref[...], right_ref[...], 0, 0)

    @pl.when(pl.program_id(1) == 0)
    def _():
        for e in range(count):
            out_ref[e] = product[:, e * hidden : (e + 1) * hidden]

    @pl.when(pl.program_id(1) > 0)
    def _():
        for e in range(count):
            out_ref[e] += product[:, e * hidden : (e + 1) * hidden]


def over_rows(rows, low, shape, block=256, chunk=2048):
    count, width, hidden = shape
    total = rows.shape[0]
    chunk = min(chunk, total)
    return pl.pallas_call(
        over_kernel,
        grid=(width // block, total // chunk),
        in_specs=[
            pl.BlockSpec((chunk, block), lambda d, k: (k, d)),
            pl.BlockSpec((chunk, count * hidden), lambda d, k: (k, 0)),
        ],
        out_specs=pl.BlockSpec((count, block, hidden), lambda d, k: (0, d, 0)),
        out_shape=jax.ShapeDtypeStruct(shape, F32),
        compiler_params=PARAMS,
        cost_estimate=cost(total * width * count * hidden, total * width * 4),
    )(rows, low)


def turned_kernel(left_ref, right_ref, out_ref):
    product = dot(left_ref[...], right_ref[...], 1, 0)

    @pl.when(pl.program_id(1) == 0)
    def _():
        out_ref[...] = product

    @pl.when(pl.program_id(1) > 0)
    def _():
        out_ref[...] += product


def turned_rows(left, right, block=256, chunk=2048):
    mid, total = left.shape
    width = right.shape[1]
    chunk = min(chunk, total)
    return pl.pallas_call(
        turned_kernel,
        grid=(width // block, total // chunk),
        in_specs=[
            pl.BlockSpec((mid, chunk), lambda d, k: (0, k)),
            pl.BlockSpec((chunk, block), lambda d, k: (k, d)),
        ],
        out_specs=pl.BlockSpec((mid, block), lambda d, k: (0, d)),
        out_shape=jax.ShapeDtypeStruct((mid, width), F32),
        compiler_params=PARAMS,
        cost_estimate=cost(total * width * mid, total * width * 4),
    )(left, right)


def front_kernel(tokens_ref, gain_ref, query_ref, key_ref, value_ref, *outs):
    normed_ref, query_out_ref, key_out_ref, value_out_ref, squares_ref = outs

    @pl.when(pl.program_id(0) == 0)
    def _():
        state = tokens_ref[...].astype(F32)
        scale = lax.rsqrt(jnp.mean(state * state, -1, keepdims=True) + EPSILON)
        normed_ref[...] = (state * scale * gain_ref[...]).astype(BF)
        squares_ref[...] = jnp.zeros_like(squares_ref)

    normed = normed_ref[...]
    query = dot(normed, query_ref[...], 1, 0)
    key = dot(normed, key_ref[...], 1, 0)
    query_out_ref[...] = query
    key_out_ref[...] = key
    value_out_ref[...] = dot(normed, value_ref[...], 1, 0).astype(BF)
    squares_ref[...] += two_rows(query * query, key * key)


def row_sums(array):
    ones = jnp.ones((8, array.shape[1]), F32)
    return lax.dot_general(
        ones,
        array,
        (((1,), (1,)), ((), ())),
        precision=lax.Precision.HIGHEST,
        preferred_element_type=F32,
    )


def two_rows(first, second):
    row = lax.broadcasted_iota(jnp.int32, (8, first.shape[0]), 0)
    return jnp.where(row == 0, row_sums(first), jnp.where(row == 1, row_sums(second), 0.0))


def norm_kernel(tokens_ref, gain_ref, out_ref):
    state = tokens_ref[...].astype(F32)
    scale = lax.rsqrt(jnp.mean(state * state, -1, keepdims=True) + EPSILON)
    out_ref[...] = (state * scale * gain_ref[...]).astype(BF)


def norm_all(tokens, gain, block):
    total, width = tokens.shape
    return pl.pallas_call(
        norm_kernel,
        grid=(total // block,),
        in_specs=[pl.BlockSpec((block, width), lambda i: (i, 0)), resident((1, width))],
        out_specs=pl.BlockSpec((block, width), lambda i: (i, 0)),
        out_shape=jax.ShapeDtypeStruct((total, width), BF),
        compiler_params=PARAMS,
        cost_estimate=cost(0, total * width * 4),
    )(tokens, gain[None])


def project(tokens, gain, w_query, w_key, w_value, block=256):
    count, width = tokens.shape
    local = w_query.shape[1]
    weight = pl.BlockSpec((width, block), lambda i: (0, i))
    out = pl.BlockSpec((count, block), lambda i: (0, i))
    return pl.pallas_call(
        front_kernel,
        grid=(local // block,),
        in_specs=[resident(tokens.shape), resident((1, width)), weight, weight, weight],
        out_specs=[resident((count, width)), out, out, out, resident((8, count))],
        out_shape=[
            jax.ShapeDtypeStruct((count, width), BF),
            jax.ShapeDtypeStruct((count, local), F32),
            jax.ShapeDtypeStruct((count, local), F32),
            jax.ShapeDtypeStruct((count, local), BF),
            jax.ShapeDtypeStruct((8, count), F32),
        ],
        compiler_params=PARAMS,
        cost_estimate=cost(3 * count * width * local, 6 * width * local),
    )(tokens, gain[None], w_query, w_key, w_value)


def scales_of(sums, full_width):
    return lax.rsqrt(sums.T / full_width + EPSILON)


def pack_kernel(full_width, query_ref, key_ref, value_ref, sums_ref, *refs):
    query_gain_ref, key_gain_ref, cos_ref, sin_ref, segment_ref, out_ref = refs
    parts, heads = out_ref.shape[0] // query_gain_ref.shape[0], query_gain_ref.shape[0]
    size = cos_ref.shape[1]
    count = cos_ref.shape[0]
    part = count // parts
    piece = part // 4
    scales = scales_of(sums_ref[...], full_width)
    for h in range(heads):
        span = slice(h * size, (h + 1) * size)

        def turned(ref, column, gain_ref):
            unit = ref[:, span] * scales[:, column : column + 1]
            vector = unit * gain_ref[pl.ds(h, 1), :]
            rolled = pltpu.roll(vector, size // 2, 1)
            return (vector * cos_ref[...] + rolled * sin_ref[...]).astype(BF)

        query = turned(query_ref, 0, query_gain_ref)
        key = turned(key_ref, 1, key_gain_ref)
        value = value_ref[:, span]
        for p in range(parts):
            place = h * parts + p
            for t in range(4):
                start = (t * parts + p) * piece
                out_ref[place, t * piece : (t + 1) * piece] = query[start : start + piece]
            out_ref[place, part : part + count] = key
            out_ref[place, part + count : part + 2 * count] = value
            out_ref[place, part + 2 * count :] = segment_ref[p]


def pack_heads(query, key, value, sums, query_gain, key_gain, cos, sin, segments, full_width):
    count = query.shape[0]
    size = cos.shape[1]
    parts = SPAN // query_gain.shape[0]
    return pl.pallas_call(
        functools.partial(pack_kernel, full_width),
        out_shape=jax.ShapeDtypeStruct(
            (SPAN, count // parts + 2 * count + segments.shape[1], size), BF
        ),
        compiler_params=PARAMS,
        cost_estimate=cost(0, 12 * query.size),
    )(query, key, value, sums, query_gain, key_gain, cos, sin, segments)


def head_views(got_ref, s, part, count):
    length = (s + 1) * count
    size = got_ref.shape[2]
    query = got_ref[s, :part]
    key = got_ref[: s + 1, part : part + count].reshape(length, size)
    value = got_ref[: s + 1, part + count : part + 2 * count].reshape(length, size)
    return query, key, value


def visible_pairs(got_ref, half, s, part, count):
    size = got_ref.shape[2]
    per_block = count // size
    first = part + 2 * count

    def rows(block):
        return got_ref[block, first : first + 16].astype(F32)

    own = jnp.broadcast_to(rows(s)[per_block : per_block + 1], (size, size)).T
    pieces = []
    for block in range(s + 1):
        values = rows(block)
        for r in range(per_block):
            pieces.append(own == values[r : r + 1])
    pieces = [jnp.where(piece, 1.0, 0.0) for piece in pieces]
    same = jnp.concatenate(pieces, 1) > 0.5
    query = lax.broadcasted_iota(jnp.int32, same.shape, 0)
    piece = part // 4
    query_pos = s * count + query // piece * (count // 4) + half * piece + query % piece
    return same & (lax.broadcasted_iota(jnp.int32, same.shape, 1) <= query_pos)


def attend_kernel(part, count, half_ref, got_ref, mix_ref, log_ref):
    half = half_ref[0]
    size = got_ref.shape[2]
    for s in range(SPAN):
        query, key, value = head_views(got_ref, s, part, count)
        visible = visible_pairs(got_ref, half, s, part, count)
        scores = jnp.where(visible, dot(query, key, 1, 1) / math.sqrt(size), NEGATIVE)
        top = jnp.max(scores, -1, keepdims=True)
        weights = jnp.where(visible, jnp.exp(scores - top), 0.0)
        total = jnp.sum(weights, -1, keepdims=True)
        mix_ref[s] = dot((weights / total).astype(BF), value, 1, 0).astype(BF)
        log_ref[s] = jnp.broadcast_to(top + jnp.log(total), (part, size))


def attend(got, half, part, count):
    size = got.shape[2]
    return pl.pallas_call(
        functools.partial(attend_kernel, part, count),
        in_specs=[
            pl.BlockSpec(memory_space=pltpu.SMEM),
            pl.BlockSpec(memory_space=pltpu.VMEM),
        ],
        out_shape=[
            jax.ShapeDtypeStruct((SPAN, part, size), BF),
            jax.ShapeDtypeStruct((SPAN, part, size), F32),
        ],
        compiler_params=PARAMS,
        cost_estimate=cost(SPAN * SPAN * part * count * size, 4 * got.size, SPAN * SPAN * part * count),
    )(half, got)


def attend_back_kernel(part, count, half_ref, got_ref, log_ref, grad_ref, out_ref, key_sum, value_sum):
    half = half_ref[0]
    size = got_ref.shape[2]
    root = math.sqrt(size)
    for s in reversed(range(SPAN)):
        length = (s + 1) * count
        query, key, value = head_views(got_ref, s, part, count)
        visible = visible_pairs(got_ref, half, s, part, count)
        scores = dot(query, key, 1, 1) / root - log_ref[s, :, :1]
        probs = jnp.where(visible, jnp.exp(jnp.where(visible, scores, 0.0)), 0.0)
        grad = grad_ref[s]
        probs_grad = dot(grad, value, 1, 1)
        inner = jnp.sum(probs * probs_grad, -1, keepdims=True)
        low = (probs * (probs_grad - inner)).astype(BF)
        out_ref[s, :part] = (dot(low, key, 1, 0) / root).astype(BF)
        key_back = dot(low, query, 0, 0)
        value_back = dot(probs.astype(BF), grad, 0, 0)
        if s == SPAN - 1:
            key_sum[...] = key_back
            value_sum[...] = value_back
        else:
            key_sum[:length] += key_back
            value_sum[:length] += value_back
    for s in range(SPAN):
        span = slice(s * count, (s + 1) * count)
        out_ref[s, part : part + count] = (key_sum[span] / root).astype(BF)
        out_ref[s, part + count :] = value_sum[span].astype(BF)


def attend_back(got, half, log_total, mix_grad, part, count):
    size = got.shape[2]
    vmem = pl.BlockSpec(memory_space=pltpu.VMEM)
    return pl.pallas_call(
        functools.partial(attend_back_kernel, part, count),
        in_specs=[pl.BlockSpec(memory_space=pltpu.SMEM), vmem, vmem, vmem],
        out_shape=jax.ShapeDtypeStruct((SPAN, part + 2 * count, size), BF),
        scratch_shapes=[pltpu.VMEM((SPAN * count, size), F32)] * 2,
        compiler_params=PARAMS,
        cost_estimate=cost(
            3 * SPAN * SPAN * part * count * size, 6 * got.size, SPAN * SPAN * part * count
        ),
    )(half, got, log_total, mix_grad)


def middle_kernel(experts, place_ref, tokens_ref, mix_ref, *refs):
    weights, refs = refs[:4], refs[4:]
    gain_ref, router_ref, routes_ref, resid_ref, probs_ref, chosen_ref = refs[:6]
    row_refs = refs[6:]
    step = pl.program_id(0)
    parts = mix_ref.shape[0] // 4

    @pl.when(step == 0)
    def _():
        resid_ref[...] = tokens_ref[...].astype(F32)

    total = resid_ref[...]
    for r in range(4):
        rows = [mix_ref[p * 4 + (r ^ place_ref[0])] for p in range(parts)]
        total = total + dot(jnp.concatenate(rows, 0), weights[r][...], 1, 0)
    resid_ref[...] = total

    @pl.when(step == pl.num_programs(0) - 1)
    def _():
        state = total
        scale = lax.rsqrt(jnp.mean(state * state, -1, keepdims=True) + EPSILON)
        normed = (state * scale * gain_ref[...]).astype(BF)
        logits = dot(normed, router_ref[...], 1, 0)
        lane = lax.broadcasted_iota(jnp.int32, logits.shape, 1)
        real = lane < experts
        top = jnp.max(jnp.where(real, logits, NEGATIVE), -1, keepdims=True)
        powers = jnp.exp(jnp.minimum(logits - top, 0.0))
        probs = powers / jnp.sum(jnp.where(real, powers, 0.0), -1, keepdims=True)
        routes = routes_ref[...]
        chosen = jnp.zeros(logits.shape, F32)
        for k in range(routes.shape[1]):
            column = routes[:, k : k + 1]
            hit = (lane == column) | (lane == column + experts)
            chosen = jnp.where(hit, 1.0, chosen)
        probs_ref[...] = jnp.where(real, probs, 0.0)
        chosen_ref[...] = jnp.where(real, chosen, 0.0)
        gates = probs * chosen
        high = gates.astype(BF).astype(F32)
        side = jnp.where(real, high, jnp.where(lane < 2 * experts, gates - high, 0.0))
        rows = jnp.concatenate([normed, side.astype(BF)], 1)
        begin = 0
        for ref in row_refs:
            ref[...] = rows[:, begin : begin + ref.shape[1]]
            begin += ref.shape[1]


def middle(tokens, mix, weights, gain, router_wide, routes, place, experts, groups):
    local, width = weights[0].shape
    size = mix.shape[2]
    heads = local // size
    own = tokens.shape[0] // 4
    wide = router_wide.shape[1]
    shape = jax.ShapeDtypeStruct
    return pl.pallas_call(
        functools.partial(middle_kernel, experts),
        grid_spec=pltpu.PrefetchScalarGridSpec(
            num_scalar_prefetch=1,
            grid=(heads,),
            in_specs=[
                pl.BlockSpec((own, width), lambda i, place_ref: (place_ref[0], 0)),
                pl.BlockSpec((mix.shape[0] // heads,) + mix.shape[1:], lambda i, *_: (i, 0, 0)),
            ]
            + [pl.BlockSpec((size, width), lambda i, *_: (i, 0))] * 4
            + [
                resident((1, width)),
                resident(router_wide.shape),
                pl.BlockSpec((own, routes.shape[1]), lambda i, place_ref: (place_ref[0], 0)),
            ],
            out_specs=[
                resident((own, width)),
                resident((own, wide)),
                resident((own, wide)),
            ]
            + [resident((own, columns)) for columns in groups],
        ),
        out_shape=[
            shape((own, width), F32),
            shape((own, wide), F32),
            shape((own, wide), F32),
        ]
        + [shape((own, columns), BF) for columns in groups],
        compiler_params=PARAMS,
        cost_estimate=cost(4 * own * width * local, 8 * width * local),
    )(place, tokens, mix, *weights, gain[None], router_wide, routes)


def middle_back_kernel(experts, place_ref, *refs):
    homes, weights, refs = refs[:6], refs[6:10], refs[10:]
    resid_ref, probs_ref, chosen_ref, gain_ref, router_ref, cotangent_ref = refs[:6]
    grad_ref, low_ref, small_ref, mix_ref = refs[6:]
    width = resid_ref.shape[1]

    @pl.when(pl.program_id(0) == 0)
    def _():
        parts = [a[...].astype(F32) + b[...].astype(F32) for a, b in zip(homes[:3], homes[3:])]
        home = jnp.concatenate(parts, 1)
        side = home[:, width:]
        lanes = side.shape[1]
        gate_grad = (side + pltpu.roll(side, lanes - experts, 1)) * chosen_ref[...]
        probs = probs_ref[...]
        inner = jnp.sum(probs * gate_grad, -1, keepdims=True)
        logit_low = (probs * (gate_grad - inner)).astype(BF)
        state = resid_ref[...]
        scale = lax.rsqrt(jnp.mean(state * state, -1, keepdims=True) + EPSILON)
        unit = state * scale
        mid_grad = home[:, :width] + dot(logit_low, router_ref[...], 1, 1)
        scaled = mid_grad * gain_ref[...]
        grad = cotangent_ref[...].astype(F32) + scale * (
            scaled - unit * jnp.mean(scaled * unit, -1, keepdims=True)
        )
        grad_ref[...] = grad
        low_ref[...] = grad.astype(BF)
        normed = (unit * gain_ref[...]).astype(BF)
        small_ref[:experts] = dot(logit_low, normed, 0, 0)[:experts]
        d_gain = jnp.sum(mid_grad * unit, 0, keepdims=True)
        row = lax.broadcasted_iota(jnp.int32, (8, width), 0)
        small_ref[experts:] = jnp.where(row == 0, d_gain, 0.0)

    low = low_ref[...]
    parts, piece = mix_ref.shape[0] // 4, mix_ref.shape[1]
    for r in range(4):
        product = dot(low, weights[r][...], 1, 1).astype(BF)
        for p in range(parts):
            mix_ref[p * 4 + (r ^ place_ref[0])] = product[p * piece : (p + 1) * piece]


def middle_back(homes, weights, resid, probs, chosen, gain, router_wide, cotangent, place, experts, size):
    own, width = resid.shape
    heads = weights[0].shape[0] // size
    parts = SPAN // heads
    shape = jax.ShapeDtypeStruct
    arrays = [resid, probs, chosen, gain[None], router_wide]
    return pl.pallas_call(
        functools.partial(middle_back_kernel, experts),
        grid_spec=pltpu.PrefetchScalarGridSpec(
            num_scalar_prefetch=1,
            grid=(heads,),
            in_specs=[resident(a.shape) for a in homes]
            + [pl.BlockSpec((size, width), lambda i, *_: (i, 0))] * 4
            + [resident(a.shape) for a in arrays]
            + [pl.BlockSpec((own, width), lambda i, place_ref: (place_ref[0], 0))],
            out_specs=[
                resident((own, width)),
                resident((own, width)),
                resident((experts + 8, width)),
                pl.BlockSpec((parts * 4, own // parts, size), lambda i, *_: (i, 0, 0)),
            ],
        ),
        out_shape=[
            shape((own, width), F32),
            shape((own, width), BF),
            shape((experts + 8, width), F32),
            shape((heads * parts * 4, own // parts, size), BF),
        ],
        compiler_params=PARAMS,
        cost_estimate=cost(4 * own * width * heads * size, 8 * heads * size * width),
    )(place, *homes, *weights, *arrays, cotangent)


def spread(block):
    side = swap(block, "tensor", 2)
    core = swap(block, "tensor", 1)
    return block, core, side, swap(side, "tensor", 1)


def out_grad_kernel(*refs):
    blocks, mixes, out_ref = refs[:4], refs[4:8], refs[8]
    lows = jnp.concatenate([ref[...] for ref in blocks], 0)
    own = blocks[0].shape[0]
    parts = own // mixes[0].shape[1]
    pieces = []
    for h in range(mixes[0].shape[0] // parts):
        rows = [ref[h * parts + p] for ref in mixes for p in range(parts)]
        pieces.append(dot(jnp.concatenate(rows, 0), lows, 0, 0).astype(BF))
    product = jnp.concatenate(pieces, 0)
    if len(out_ref.shape) == 2:
        out_ref[...] = product
        return
    rows, wide = out_ref.shape[1:]
    block = lows.shape[1]
    for q in range(wide // block):
        out_ref[0, :, q * block : (q + 1) * block] = product[q * rows : (q + 1) * rows]


def out_weight_grad(blocks, mixes, local, owners):
    own, width = blocks[0].shape
    block = width // owners
    if block % LANES == 0:
        rows = local // owners
        out = pl.BlockSpec((1, rows, width), lambda d: (d, 0, 0))
        shape = jax.ShapeDtypeStruct((owners, rows, width), BF)
    else:
        block = 4 * LANES
        out = pl.BlockSpec((local, block), lambda d: (0, d))
        shape = jax.ShapeDtypeStruct((local, width), BF)
    return pl.pallas_call(
        out_grad_kernel,
        grid=(width // block,),
        in_specs=[pl.BlockSpec((own, block), lambda d: (0, d))] * 4
        + [resident(mix.shape) for mix in mixes],
        out_specs=out,
        out_shape=shape,
        compiler_params=PARAMS,
        cost_estimate=cost(4 * own * local * width, local * width * 3),
    )(*blocks, *mixes)


def unturn_kernel(full_width, back_ref, query_ref, key_ref, sums_ref, *refs):
    query_gain_ref, key_gain_ref, cos_ref, sin_ref = refs[:4]
    query_out_ref, key_out_ref, value_out_ref, inner_ref, gains_ref = refs[4:]
    heads, size = query_gain_ref.shape
    parts = SPAN // heads
    count = cos_ref.shape[0]
    part = count // parts
    piece = part // 4
    scales = scales_of(sums_ref[...], full_width)
    inner = [0.0, 0.0]
    for h in range(heads):
        span = slice(h * size, (h + 1) * size)
        first = h * parts
        query = jnp.concatenate(
            [
                back_ref[first + p, t * piece : (t + 1) * piece]
                for t in range(4)
                for p in range(parts)
            ],
            0,
        )
        key = sum(back_ref[first + p, part : part + count].astype(F32) for p in range(parts))
        value = sum(back_ref[first + p, part + count :].astype(F32) for p in range(parts))
        value_out_ref[:, span] = value.astype(BF)
        key = key.astype(BF)
        items = ((query, query_ref, query_gain_ref, query_out_ref), (key, key_ref, key_gain_ref, key_out_ref))
        for n, (grad, raw_ref, gain_ref, out_ref) in enumerate(items):
            grad = grad.astype(F32)
            gain_in = grad * cos_ref[...] - pltpu.roll(grad, size // 2, 1) * sin_ref[...]
            unit = raw_ref[:, span] * scales[:, n : n + 1]
            gains_ref[n * heads + h] = jnp.broadcast_to(
                jnp.sum(gain_in * unit, 0, keepdims=True), (8, size)
            )
            scaled = gain_in * gain_ref[pl.ds(h, 1), :]
            out_ref[:, span] = scaled
            inner[n] = inner[n] + scaled * unit
    inner_ref[...] = two_rows(inner[0], inner[1])


def unturn(back, query, key, sums, query_gain, key_gain, cos, sin, full_width):
    count, local = query.shape
    heads, size = query_gain.shape
    shape = jax.ShapeDtypeStruct
    return pl.pallas_call(
        functools.partial(unturn_kernel, full_width),
        out_shape=[
            shape((count, local), F32),
            shape((count, local), F32),
            shape((count, local), BF),
            shape((8, count), F32),
            shape((2 * heads, 8, size), F32),
        ],
        compiler_params=PARAMS,
        cost_estimate=cost(0, 24 * query.size),
    )(back, query, key, sums, query_gain, key_gain, cos, sin)


def columns_kernel(full_width, *refs):
    query_scaled_ref, key_scaled_ref, value_ref, query_ref, key_ref, sums_ref, inner_ref = refs[:7]
    query_low_ref, key_low_ref, out_ref = refs[7:]
    owners, rows, _ = out_ref.shape
    rows = rows // 3
    scales = scales_of(sums_ref[...], full_width)
    means = inner_ref[...].T / full_width
    items = ((query_scaled_ref, query_ref, query_low_ref), (key_scaled_ref, key_ref, key_low_ref))
    lows = []
    for n, (scaled_ref, raw_ref, low_ref) in enumerate(items):
        scale = scales[:, n : n + 1]
        unit = raw_ref[...] * scale
        low = (scale * (scaled_ref[...] - unit * means[:, n : n + 1])).astype(BF)
        low_ref[...] = low
        lows.append(low)
    for n, low in enumerate(lows + [value_ref[...]]):
        turned = low.T
        for d in range(owners):
            out_ref[d, n * rows : (n + 1) * rows] = turned[d * rows : (d + 1) * rows]


def columns_of(query_scaled, key_scaled, value, query, key, sums, inner, full_width, owners):
    count, local = query.shape
    low = jax.ShapeDtypeStruct((count, local), BF)
    return pl.pallas_call(
        functools.partial(columns_kernel, full_width),
        out_shape=[low, low, jax.ShapeDtypeStruct((owners, 3 * local // owners, count), BF)],
        compiler_params=PARAMS,
        cost_estimate=cost(0, 24 * query.size),
    )(query_scaled, key_scaled, value, query, key, sums, inner)


def input_kernel(own, place_ref, *refs):
    lows, weights, kept_ref, sent_ref = refs[:3], refs[3:6], refs[6], refs[7]
    place = place_ref[0]
    total = None
    for low_ref, weight_ref in zip(lows, weights):
        rows = [
            low_ref[pl.ds(pl.multiple_of((r ^ place) * own, own), own), :] for r in range(4)
        ]
        product = dot(jnp.concatenate(rows, 0), weight_ref[...], 1, 1)
        total = product if total is None else total + product
    total = total.astype(BF)
    for r in range(4):
        ref = sent_ref if r % 2 else kept_ref
        ref[r // 2] = total[r * own : (r + 1) * own]


def input_back(lows, weights, place, own, block=512):
    width, local = weights[0].shape
    out = pl.BlockSpec((2, own, block), lambda d, *_: (0, 0, d))
    shape = jax.ShapeDtypeStruct((2, own, width), BF)
    return pl.pallas_call(
        functools.partial(input_kernel, own),
        grid_spec=pltpu.PrefetchScalarGridSpec(
            num_scalar_prefetch=1,
            grid=(width // block,),
            in_specs=[resident(lows[0].shape)] * 3
            + [pl.BlockSpec((block, local), lambda d, *_: (d, 0))] * 3,
            out_specs=[out, out],
        ),
        out_shape=[shape, shape],
        compiler_params=PARAMS,
        cost_estimate=cost(12 * own * local * width, local * width * 7),
    )(place, *lows, *weights)


def last_kernel(place_ref, tokens_ref, *refs):
    kept_ref, core_ref, side_ref, grad_ref, gain_ref, small_ref, out_ref = refs
    own = grad_ref.shape[0]
    extra = out_ref.shape[0] - own
    used = small_ref.shape[0]
    state = tokens_ref[...].astype(F32)
    scale = lax.rsqrt(jnp.mean(state * state, -1, keepdims=True) + EPSILON)
    unit = state * scale
    grad = kept_ref[0].astype(F32) + core_ref[0].astype(F32) + side_ref[...].astype(F32)
    scaled = grad * gain_ref[...]
    out = grad_ref[...] + scale * (scaled - unit * jnp.mean(scaled * unit, -1, keepdims=True))
    out_ref[:own] = out.astype(BF)
    d_gain = jnp.sum(grad * unit, 0, keepdims=True)
    row = lax.broadcasted_iota(jnp.int32, (8, state.shape[1]), 0)
    gains = small_ref[used - 8 :] + jnp.where(row == 1, d_gain, 0.0)
    rows = [small_ref[: used - 8], gains]
    if extra > used:
        rows.append(jnp.zeros((extra - used, state.shape[1]), F32))
    out_ref[own:] = jnp.concatenate(rows, 0).astype(BF)


def last(tokens, kept, core, side, grad, gain, small, place):
    own, width = side.shape
    arrays = [kept, core, side, grad, gain[None], small]
    rows = own + -(-small.shape[0] // 16) * 16
    return pl.pallas_call(
        last_kernel,
        grid_spec=pltpu.PrefetchScalarGridSpec(
            num_scalar_prefetch=1,
            grid=(1,),
            in_specs=[pl.BlockSpec((own, width), lambda i, place_ref: (place_ref[0], 0))]
            + [resident(a.shape) for a in arrays],
            out_specs=resident((rows, width)),
        ),
        out_shape=jax.ShapeDtypeStruct((rows, width), BF),
        compiler_params=PARAMS,
        cost_estimate=cost(0, own),
    )(place, tokens, *arrays)


def tile_kernel(rows_ref, out_ref):
    rows, wide = rows_ref.shape
    block = out_ref.shape[1]
    for q in range(wide // block):
        out_ref[q * rows : (q + 1) * rows] = rows_ref[:, q * block : (q + 1) * block].astype(F32)


def tile_rows(rows, local):
    return pl.pallas_call(
        tile_kernel,
        out_shape=jax.ShapeDtypeStruct((local, rows.size // local), F32),
        compiler_params=PARAMS,
        cost_estimate=cost(0, rows.size * 6),
    )(rows)


def join_kernel(own, place_ref, *refs):
    out_ref = refs[4]
    for r in range(4):
        start = pl.multiple_of((r ^ place_ref[0]) * own, own)
        out_ref[pl.ds(start, own), :] = refs[r][:own].astype(out_ref.dtype)


def join_blocks(blocks, place, own, kind):
    width = blocks[0].shape[1]
    vmem = pl.BlockSpec(memory_space=pltpu.VMEM)
    return pl.pallas_call(
        functools.partial(join_kernel, own),
        in_specs=[pl.BlockSpec(memory_space=pltpu.SMEM)] + [vmem] * 4,
        out_shape=jax.ShapeDtypeStruct((4 * own, width), kind),
        compiler_params=PARAMS,
        cost_estimate=cost(0, own),
    )(place, *blocks)


def weights_kernel(columns_ref, rows_ref, small_ref, out_ref):
    owners, columns, count = columns_ref.shape
    total = None
    for s in range(owners):
        product = dot(columns_ref[s], rows_ref[pl.ds(s * count, count), :], 1, 0)
        total = product if total is None else total + product
    out_ref[0, :columns] = total.astype(BF)
    out_ref[0, columns:] = small_ref[0]


def weight_columns(columns, rows, small):
    owners, count3, count = columns.shape
    width = rows.shape[1]
    slab = width // owners
    extra = small.shape[1]
    return pl.pallas_call(
        weights_kernel,
        grid=(owners,),
        in_specs=[
            resident(columns.shape),
            pl.BlockSpec((rows.shape[0], slab), lambda d: (0, d)),
            pl.BlockSpec((1, extra, slab), lambda d: (d, 0, 0)),
        ],
        out_specs=pl.BlockSpec((1, count3 + extra, slab), lambda d: (d, 0, 0)),
        out_shape=jax.ShapeDtypeStruct((owners, count3 + extra, slab), BF),
        compiler_params=PARAMS,
        cost_estimate=cost(rows.shape[0] * width * count3, rows.size * 2),
    )(columns, rows, small)


def unpack_kernel(given_ref, *outs):
    owners, _, slab = given_ref.shape
    local = outs[0].shape[1]
    rows = local // owners
    group = LANES // rows
    for n, out_ref in enumerate(outs[:3]):
        for s in range(0, owners, group):
            pieces = [given_ref[s + g, n * rows : (n + 1) * rows] for g in range(group)]
            turned = jnp.concatenate(pieces, 0).astype(F32).T
            out_ref[:, s * rows : (s + group) * rows] = turned
    total = given_ref[0, 3 * rows :].astype(F32)
    for s in range(1, owners):
        total = total + given_ref[s, 3 * rows :].astype(F32)
    outs[3][...] = total


def unpack(given, local):
    owners, rows, slab = given.shape
    extra = rows - 3 * local // owners
    weight = jax.ShapeDtypeStruct((slab, local), F32)
    return pl.pallas_call(
        unpack_kernel,
        out_shape=[weight, weight, weight, jax.ShapeDtypeStruct((extra, slab), F32)],
        compiler_params=PARAMS,
        cost_estimate=cost(0, given.size * 6),
    )(given)


def per_device(
    tokens,
    segment_ids,
    routes,
    norm1_gain,
    w_query,
    w_key,
    w_value,
    query_gain,
    key_gain,
    w_out,
    norm2_gain,
    w_router,
    w_gate,
    w_up,
    w_down,
    cotangent,
):
    tok_count, model_width = tokens.shape
    heads_here, head_size = query_gain.shape
    local_width = heads_here * head_size
    tensor_count = lax.axis_size("tensor")
    full_width = local_width * tensor_count
    experts = w_router.shape[1]
    owners = lax.axis_size("dp")
    dp_place = lax.axis_index("dp")
    tensor_place = lax.axis_index("tensor")
    own = tok_count // tensor_count
    parts = SPAN // heads_here
    part = tok_count // parts
    groups = [list(range(g, g + SPAN)) for g in range(0, owners, SPAN)]
    place = tensor_place.astype(jnp.int32).reshape(1)
    index = jnp.stack([dp_place, tensor_place]).astype(jnp.int32)
    half = (dp_place % SPAN % parts).astype(jnp.int32).reshape(1)

    def mine(array):
        return lax.dynamic_slice_in_dim(array, tensor_place * own, own, 0)

    def trade(array):
        return lax.all_to_all(
            array, "dp", split_axis=0, concat_axis=0, tiled=True, axis_index_groups=groups
        )

    def trade_every(array):
        wide = None
        if owners > SPAN:
            count = SPAN * tensor_count
            wide = [list(range(g, g + count)) for g in range(0, owners * tensor_count, count)]
        return lax.all_to_all(
            array, EVERY, split_axis=0, concat_axis=0, tiled=True, axis_index_groups=wide
        )

    def sum_tensor(kept, sent):
        core = swap(sent, "tensor", 1)
        given = (kept[1].astype(F32) + core[1].astype(F32)).astype(BF)
        return kept, core, swap(given, "tensor", 2)

    out_grad_all = lax.all_gather(mine(cotangent), EVERY, axis=0, tiled=True)
    both_turned, down_turned = turn_weights(w_gate, w_up, w_down)
    side_width = -(-2 * experts // LANES) * LANES
    router_wide = jnp.pad(
        jnp.concatenate([w_router, w_router], 1), ((0, 0), (0, side_width - 2 * experts))
    )
    local_pos = jnp.arange(tok_count, dtype=jnp.int32)
    positions = (dp_place % SPAN * tok_count + local_pos).astype(F32)
    cos_table, sin_table = rope_tables(positions, head_size)
    segment_low = segment_ids.astype(BF)
    segment_parts = segment_low.reshape(tensor_count, parts, -1).transpose(1, 0, 2)
    segment_rows = jnp.concatenate(
        [
            jnp.broadcast_to(segment_low.reshape(1, -1, head_size), (parts, tok_count // head_size, head_size)),
            segment_parts.reshape(parts, 1, part),
        ],
        1,
    )
    segment_rows = jnp.pad(segment_rows, ((0, 0), (0, 16 - segment_rows.shape[1]), (0, 0)))

    normed_in, query_raw, key_raw, value_att, squares = project(
        tokens, norm1_gain, w_query, w_key, w_value
    )
    squares, w_out = lax.optimization_barrier((total_tensor(squares), w_out))
    out_weights = spread(w_out)
    packed = pack_heads(
        query_raw,
        key_raw,
        value_att,
        squares,
        query_gain,
        key_gain,
        cos_table,
        sin_table,
        segment_rows,
        full_width,
    )
    got = trade(packed)
    mix_heads, log_total = attend(got, half, part, tok_count)
    pieces_count, piece = SPAN * tensor_count, own // parts
    mix, both_turned, down_turned = lax.optimization_barrier(
        (
            trade_every(mix_heads.reshape(pieces_count, piece, head_size)),
            both_turned,
            down_turned,
        )
    )
    lanes = -(-(model_width + side_width) // (3 * LANES)) * LANES
    resid_state, router_probs, chosen, *rows_own = middle(
        tokens,
        mix,
        out_weights,
        norm2_gain,
        router_wide,
        routes,
        place,
        experts,
        [lanes, lanes, model_width + side_width - 2 * lanes],
    )
    bits = owners.bit_length() - 1
    first_three = [("tensor", 2), ("dp", 1), ("dp", 2)]
    rest = [("dp", 1 << b) for b in range(2, bits)]
    orders = [first_three[g:] + first_three[:g] + rest for g in range(3)]
    pieces, names, back_all, tokens_own = gather_every(
        rows_own,
        [order[::-1] for order in orders],
        hidden_back(out_grad_all, down_turned),
        mine(tokens),
    )
    tokens_all = lax.all_gather(tokens_own, EVERY, axis=0, tiled=True)
    (rows_all, hid, hid_turned, glow, ulow), kept_groups, sent_groups = expert_rows(
        pieces, names, back_all, w_gate, w_up, both_turned, index, experts, tok_count
    )
    out_kept, out_sent = expert_out(hid, w_down, place % 2, tok_count)
    d_w_gate = over_rows(rows_all, glow, w_gate.shape)

    def add_core(kept_rows, sent_rows):
        core_rows = swap(sent_rows, "tensor", 1)
        return ((kept_rows.astype(F32) + core_rows.astype(F32)).astype(BF),)

    homes, out_part = sum_every(kept_groups, sent_groups, orders, (out_kept, out_sent), add_core)
    core_groups = [
        [d * tensor_count + x * 2 + c for d in range(owners) for x in range(2)] for c in range(2)
    ]
    expert_full = lax.psum_scatter(
        out_part.reshape(-1, model_width),
        EVERY,
        scatter_dimension=0,
        tiled=True,
        axis_index_groups=core_groups,
    )
    d_w_down = turned_rows(hid_turned, out_grad_all).reshape(w_down.shape)
    d_w_up = over_rows(rows_all, ulow, w_up.shape)
    normed_in_all = norm_all(tokens_all, norm1_gain, tok_count)

    resid_grad, resid_low, small, mix_grad = middle_back(
        [home[0] for home in homes] + [home[1] for home in homes],
        out_weights,
        resid_state,
        router_probs,
        chosen,
        norm2_gain,
        router_wide,
        cotangent,
        place,
        experts,
        head_size,
    )
    mix_grad, d_w_up = lax.optimization_barrier((trade_every(mix_grad), d_w_up))
    mix_by_block = mix.reshape(SPAN, tensor_count, piece, head_size)
    mix_by_block, mix_grad = lax.optimization_barrier((mix_by_block, mix_grad))
    mixes = [
        lax.dynamic_index_in_dim(mix_by_block, tensor_place ^ r, 1, keepdims=False)
        for r in range(4)
    ]
    mixes = mixes[:1] + [swap(mixes[r], "tensor", r) for r in range(1, 4)]
    lows = [resid_low] + [swap(resid_low, "tensor", r) for r in range(1, 4)]
    d_out = out_weight_grad(lows, mixes, local_width, owners)
    back, d_w_down, normed_in_all, d_out = lax.optimization_barrier(
        (
            trade(
                attend_back(
                    got,
                    half,
                    log_total,
                    mix_grad.reshape(SPAN, part, head_size),
                    part,
                    tok_count,
                )
            ),
            d_w_down,
            normed_in_all,
            d_out,
        )
    )
    query_scaled, key_scaled, value_low, inner, gains = unturn(
        back, query_raw, key_raw, squares, query_gain, key_gain, cos_table, sin_table, full_width
    )
    inner = total_tensor(inner)
    query_low, key_low, columns = columns_of(
        query_scaled, key_scaled, value_low, query_raw, key_raw, squares, inner, full_width, owners
    )
    query_low, expert_full, d_out = lax.optimization_barrier((query_low, expert_full, d_out))
    model_slice = model_width // owners
    if model_slice % LANES == 0:
        d_out = lax.psum_scatter(d_out, "dp", scatter_dimension=0, tiled=True)[0]
        d_out = tile_rows(d_out, local_width)
    else:
        d_out = lax.psum_scatter(d_out, "dp", scatter_dimension=1, tiled=True).astype(F32)
    block_own = (resid_state + expert_full.astype(F32)).astype(BF)
    out_blocks = spread(block_own)

    columns = lax.all_to_all(columns, "dp", split_axis=0, concat_axis=0, tiled=True)
    block_output = join_blocks(out_blocks, place, own, BF)
    kept, core, side = sum_tensor(
        *input_back(
            (query_low, key_low, value_low), (w_query, w_key, w_value), place, own
        )
    )
    input_blocks = spread(
        last(tokens, kept, core, side, resid_grad, norm1_gain, small, place)
    )
    input_grad = join_blocks(input_blocks, place, own, F32)

    head_slice = head_size // owners
    slice_width = local_width // owners
    gain_count = 2 * heads_here * head_slice
    gain_rows = -(-gain_count // model_slice)
    gains = gains[:, 0].reshape(2 * heads_here, owners, head_slice).transpose(1, 0, 2)
    gains = jnp.pad(
        gains.reshape(owners, gain_count), ((0, 0), (0, gain_rows * model_slice - gain_count))
    ).reshape(owners, gain_rows, model_slice)
    shared = sum(block[own : own + experts + 2].astype(F32) for block in input_blocks)
    shared = shared.reshape(experts + 2, owners, model_slice).transpose(1, 0, 2)
    extra = jnp.concatenate([shared, gains], 1).astype(BF)
    extra = jnp.pad(extra, ((0, 0), (0, -extra.shape[1] % 16), (0, 0)))
    if model_slice % LANES == 0:
        final = weight_columns(columns, normed_in_all, extra)
    else:
        columns = columns.transpose(1, 0, 2).reshape(3 * slice_width, owners * tok_count)
        final = dot(columns, normed_in_all, 1, 0).reshape(3 * slice_width, owners, model_slice)
        final = jnp.concatenate([final.transpose(1, 0, 2).astype(BF), extra], 1)
    final, block_output, input_grad = lax.optimization_barrier(
        (
            lax.all_to_all(final, "dp", split_axis=0, concat_axis=0, tiled=True),
            block_output,
            input_grad,
        )
    )
    *weights, extra = unpack(final, local_width)
    gains = extra[experts + 2 : experts + 2 + gain_rows].reshape(-1)[:gain_count]
    gains = gains.reshape(2, heads_here, head_slice)

    return (
        block_output,
        input_grad,
        extra[experts + 1],
        weights[0],
        weights[1],
        weights[2],
        gains[0],
        gains[1],
        d_out,
        extra[experts],
        extra[:experts].T,
        d_w_gate,
        d_w_up,
        d_w_down,
    )


def solution(mesh):
    in_specs = (
        P("dp", None),
        P("dp"),
        P("dp", None),
        P(),
        P(None, "tensor"),
        P(None, "tensor"),
        P(None, "tensor"),
        P("tensor", None),
        P("tensor", None),
        P("tensor", None),
        P(),
        P(),
        P("dp", None, "tensor"),
        P("dp", None, "tensor"),
        P("dp", "tensor", None),
        P("dp", None),
    )
    out_specs = (
        P("dp", None),
        P("dp", None),
        P("dp"),
        P("dp", "tensor"),
        P("dp", "tensor"),
        P("dp", "tensor"),
        P("tensor", "dp"),
        P("tensor", "dp"),
        P("tensor", "dp"),
        P("dp"),
        P("dp", None),
        P("dp", None, "tensor"),
        P("dp", None, "tensor"),
        P("dp", "tensor", None),
    )
    return jax.shard_map(
        per_device, mesh=mesh, in_specs=in_specs, out_specs=out_specs, check_vma=False
    )
```
